32 devices in a mesh: dp: 8 (over z, y), cls: 4 (over x, core).
Axes of the slice: x: 2, y: 2, z: 4, core: 2. Of those that a mesh axis runs over, the one named last changes fastest.
Arguments:
- patches: bfloat16 [16384, 768], P(('dp', 'cls')), may hold values from -6 to 6
- image_ids: int32 [32, 512], P('dp'), may hold values from 0 to 16, as said below
- patch_place: int32 [32, 2, 512], P(('dp', 'cls')), may hold values from 0 to 33, as said below
- labels: int32 [32, 16], P('dp'), may hold values from 0 to 21842
- attn_w: float32 [3072, 768], P(('dp', 'cls')), may hold values from -0.21875 to 0.21875
- mlp_w: float32 [3072, 1536], P(('dp', 'cls')), may hold values from -0.21875 to 0.21875
- embed_w: float32 [1024, 768], P(('dp', 'cls'))
- vec_w: float32 [15, 768], replicated
- head_w: float32 [768, 21848], P('dp', 'cls')
- attn_mom: float32 [3072, 768], P(('dp', 'cls')), may hold values from -0.00015258789 to 0.00015258789
- mlp_mom: float32 [3072, 1536], P(('dp', 'cls')), may hold values from -0.00015258789 to 0.00015258789
- embed_m: float32 [1024, 768], P(('dp', 'cls')), may hold values from -0.00015258789 to 0.00015258789
- embed_v: float32 [1024, 768], P(('dp', 'cls')), may hold values from 5.069944e-14 to 8.1119107e-13
- vec_m: float32 [15, 768], replicated, may hold values from -0.00061035156 to 0.00061035156
- vec_v: float32 [15, 768], replicated, may hold values from 8.1119107e-13 to 1.2979057e-11
- head_m: float32 [768, 21848], P('dp', 'cls'), may hold values from -0.00015258789 to 0.00015258789
- head_v: float32 [768, 21848], P('dp', 'cls'), may hold values from 5.069944e-14 to 8.1119107e-13
Outputs:
- loss_sum: float32 [], replicated
- image_total: float32 [], replicated
- grad_norm: float32 [], replicated
- attn_out: float32 [3072, 768], P(('dp', 'cls'))
- attn_mom_out: float32 [3072, 768], P(('dp', 'cls'))
- attn_copy: bfloat16 [3072, 768], P(('dp', 'cls'))
- mlp_out: float32 [3072, 1536], P(('dp', 'cls'))
- mlp_mom_out: float32 [3072, 1536], P(('dp', 'cls'))
- mlp_copy: bfloat16 [3072, 1536], P(('dp', 'cls'))
- embed_out: float32 [1024, 768], P(('dp', 'cls'))
- embed_m_out: float32 [1024, 768], P(('dp', 'cls'))
- embed_v_out: float32 [1024, 768], P(('dp', 'cls'))
- embed_copy: bfloat16 [1024, 768], P(('dp', 'cls'))
- vec_out: float32 [15, 768], replicated
- vec_m_out: float32 [15, 768], replicated
- vec_v_out: float32 [15, 768], replicated
- vec_copy: bfloat16 [15, 768], replicated
- head_out: float32 [768, 21848], P('dp', 'cls')
- head_m_out: float32 [768, 21848], P('dp', 'cls')
- head_v_out: float32 [768, 21848], P('dp', 'cls')
- head_copy: bfloat16 [768, 21848], P('dp', 'cls')
The draws below stay inside these ranges and needn't reach their ends.
Inputs may be any that keep to these rules, and one draw needn't show every extreme that they name: `image_ids`: in each pack the patches of an image stand together, images in slot order from slot 0, padding patches (slot 16) at the end; the last pack fills all 16 slots. `patch_place`: row and column of a patch within its image grid, 0 for padding patches.
All inputs are finite; a program needn't handle non-finite values.
Results may differ from the reference program's by a relative error of at most 0.015.
Values may be sent and summed in bfloat16 or wider, within the bound.
No kernel may reach another device: no remote copies, remote signals or barrier semaphores. Data moves between devices by JAX's collectives and lax.ppermute only.
A program may use at most 192 MiB of HBM per device.

```python
import math
import jax
import jax.numpy as jnp
from jax import lax

D = 768
H = 12
FF = 3072
PD = 768
CLASSES = 21843
GRID = 128
IMG_DEV = 16
STEP = 10
TOK_DEV = 512
PACKS = 32
TOKENS = 16384
CLS_PAD = 21848
VEC = 15
NPARAM = 24655104


def pack_layout(key):
    key_count, key_height = jax.random.split(jax.random.fold_in(key, 17))
    pack_index = jnp.arange(PACKS)
    least_count = max(1, IMG_DEV // 3)
    rising = least_count + pack_index * (IMG_DEV - least_count) // max(PACKS - 1, 1)
    image_count = jnp.clip(rising - jax.random.randint(key_count, (PACKS,), 0, 2), least_count, IMG_DEV)
    image_count = jnp.where(pack_index == 0, least_count, image_count)
    image_count = jnp.where(pack_index == PACKS - 1, IMG_DEV, image_count)
    budget = TOK_DEV // image_count
    heights = jax.random.randint(key_height, (PACKS, IMG_DEV), 3, 13)
    first_slot = (pack_index[:, None] == 0) & (jnp.arange(IMG_DEV)[None, :] == 0)
    heights = jnp.where(first_slot, 3, heights)
    widths = budget[:, None] // heights
    slot_index = jnp.arange(IMG_DEV)
    image_sizes = jnp.where(slot_index[None] < image_count[:, None], heights * widths, 0)
    image_ends = jnp.cumsum(image_sizes, axis=1)
    starts = image_ends - image_sizes
    position = jnp.arange(TOK_DEV)
    image_index = jnp.sum((position[None, :, None] >= image_ends[:, None, :]).astype(jnp.int32), axis=2)
    clamped = jnp.minimum(image_index, IMG_DEV - 1)
    offset = position[None] - jnp.take_along_axis(starts, clamped, axis=1)
    row_width = jnp.take_along_axis(widths, clamped, axis=1)
    inside = image_index < IMG_DEV
    grid_rows = jnp.where(inside, offset // row_width, 0)
    grid_cols = jnp.where(inside, offset % row_width, 0)
    return (image_index.astype(jnp.int32), grid_rows.astype(jnp.int32), grid_cols.astype(jnp.int32))


def draw_image_ids(key, part):
    image_index, grid_rows, grid_cols = pack_layout(key)
    return image_index


def draw_patch_place(key, part):
    image_index, grid_rows, grid_cols = pack_layout(key)
    return jnp.stack([grid_rows, grid_cols], axis=1)


def draw_embed_w(key, part):
    key = jax.random.fold_in(key, 3)
    normal_part = jax.random.normal(key, (PD + 2 * GRID, D), jnp.float32)
    row_scale = jnp.where(jnp.arange(PD + 2 * GRID) < PD, PD ** (-0.5), 0.05)
    return normal_part * row_scale[:, None]


def draw_vec_w(key, part):
    key = jax.random.fold_in(key, 5)
    key_gain, key_bias = jax.random.split(key)
    rising = 0.6 + 0.8 * jnp.arange(D, dtype=jnp.float32) / D
    noise = jax.random.uniform(key_gain, (VEC, D), jnp.float32, 0.8, 1.2)
    biases = 0.3 * jax.random.normal(key_bias, (VEC, D), jnp.float32)
    row_index = jnp.arange(VEC)
    gain_rows = (row_index == 4) | (row_index == 6) | (row_index == 8)
    return jnp.where(gain_rows[:, None], rising[None] * noise, biases)


def draw_head_w(key, part):
    key = jax.random.fold_in(key, 7)
    normal_part = jax.random.normal(key, (D, CLS_PAD), jnp.float32)
    rising = 1.0 + 2.0 * jnp.arange(CLS_PAD, dtype=jnp.float32) / CLS_PAD
    return normal_part * rising[None] * D ** (-0.5)


def set_ends(values, key, least, top_value):
    longest = values.shape.index(max(values.shape))
    spots = []
    for shift in (0, 1):
        where = [jax.random.randint(jax.random.fold_in(key, axis), (), 0, length) for axis, length in enumerate(values.shape)]
        where[longest] = (where[longest] + shift) % values.shape[longest]
        spots.append(tuple(where))
    return values.at[spots[0]].set(least).at[spots[1]].set(top_value)


def block_levels(rng, dims, shards, low, top_value):
    def one(dim, blocks):
        draws = jax.random.uniform(jax.random.fold_in(jax.random.fold_in(rng, 6), dim), (blocks,), jnp.float32, low / len(shards), top_value / len(shards))
        return jnp.repeat(jnp.exp(draws), dims[dim] // blocks).reshape((-1,) + (1,) * (len(dims) - dim - 1))

    level = one(*shards[0])
    for cut in shards[1:]:
        level = level * one(*cut)
    return level


def scatter_about(key, shape, width, limit, cuts=(), kind=jnp.bfloat16):
    values = width * jax.random.normal(key, shape, jnp.float32)
    if cuts:
        values = values * block_levels(key, shape, cuts, -0.22, 0.18)
    return jnp.clip(values, -limit, limit).astype(kind)


def setup_inputs(seed: int = 0) -> dict:
    streams_of = jax.random.split(jax.random.key(seed), 18)
    patches = scatter_about(streams_of[0], (TOKENS, PD), 1.0, 6.0, ((0, 32),))
    image_ids = draw_image_ids(jax.random.fold_in(streams_of[17], 71), 0)
    patch_place = draw_patch_place(jax.random.fold_in(streams_of[17], 71), 0)
    labels = set_ends(jax.random.randint(streams_of[3], (PACKS, IMG_DEV), 0, CLASSES), jax.random.fold_in(streams_of[3], 1), 0, CLASSES - 1).astype(jnp.int32)
    attn_w = scatter_about(streams_of[4], (4 * D, D), D ** -0.5, 0.21875, ((0, 32),), jnp.float32)
    mlp_w = scatter_about(streams_of[5], (FF, 2 * D), D ** -0.5, 0.21875, ((0, 32),), jnp.float32)
    embed_w = draw_embed_w(jax.random.fold_in(streams_of[17], 71), 0)
    vec_w = draw_vec_w(jax.random.fold_in(streams_of[17], 71), 0)
    head_w = draw_head_w(jax.random.fold_in(streams_of[17], 71), 0)
    attn_mom = scatter_about(streams_of[9], (4 * D, D), (0.05 / NPARAM ** 0.5), 0.00015258789, ((0, 32),), jnp.float32)
    mlp_mom = scatter_about(streams_of[10], (FF, 2 * D), (0.05 / NPARAM ** 0.5), 0.00015258789, ((0, 32),), jnp.float32)
    embed_m = scatter_about(streams_of[11], (PD + 2 * GRID, D), (0.05 / NPARAM ** 0.5), 0.00015258789, ((0, 32),), jnp.float32)
    embed_v = jnp.clip(jnp.exp(math.log(8.111910665756228e-13) - 2.7725887 * jax.random.uniform(streams_of[12], (PD + 2 * GRID, D), jnp.float32) ** block_levels(streams_of[12], (PD + 2 * GRID, D), ((0, 32),), -0.2, 0.2)), 5.0699441660976424e-14, 8.111910665756228e-13)
    vec_m = scatter_about(streams_of[13], (VEC, D), (0.2 / NPARAM ** 0.5), 0.00061035156, (), jnp.float32)
    vec_v = jnp.clip(jnp.exp(jax.random.uniform(streams_of[14], (VEC, D), jnp.float32, math.log(8.111910665756228e-13), math.log(1.2979057065209965e-11))), 8.111910665756228e-13, 1.2979057065209965e-11)
    head_m = scatter_about(streams_of[15], (D, CLS_PAD), (0.05 / NPARAM ** 0.5), 0.00015258789, ((0, 8), (1, 4)), jnp.float32)
    head_v = jnp.clip(jnp.exp(math.log(8.111910665756228e-13) - 2.7725887 * jax.random.uniform(streams_of[16], (D, CLS_PAD), jnp.float32) ** block_levels(streams_of[16], (D, CLS_PAD), ((0, 8), (1, 4)), -0.2, 0.2)), 5.0699441660976424e-14, 8.111910665756228e-13)
    return dict(patches=patches, image_ids=image_ids, patch_place=patch_place, labels=labels, attn_w=attn_w, mlp_w=mlp_w, embed_w=embed_w, vec_w=vec_w, head_w=head_w, attn_mom=attn_mom, mlp_mom=mlp_mom, embed_m=embed_m, embed_v=embed_v, vec_m=vec_m, vec_v=vec_v, head_m=head_m, head_v=head_v)


highest = lax.Precision.HIGHEST
newton_one = 3.4445
newton_two = -4.775
newton_three = 2.0315
clip_limit = 0.05
muon_rate = 0.3
decay_rate = 0.05
adam_rate = 0.01
vector_rate = 0.05
momentum_keep = 0.5
adam_first = 0.5
adam_second = 0.999

@jax.custom_vjp
def low(v):
    return lax.optimization_barrier(v.astype(jnp.bfloat16)).astype(jnp.float32)

@jax.custom_vjp
def low_back(v):
    return v

def low_keep(v):
    return (low(v), None)

def low_pass(kept, grad):
    return (grad,)

def back_keep(v):
    return (v, None)

def back_low(kept, grad):
    return (low(grad),)
low.defvjp(low_keep, low_pass)
low_back.defvjp(back_keep, back_low)

def product(left_side, right_side):
    return jnp.dot(left_side, right_side, precision=highest)

def layer_norm(inputs, gain_row, shift_row):
    mean_row = lax.optimization_barrier(jnp.mean(inputs, axis=-1, keepdims=True))
    centred = inputs - mean_row
    variance = lax.optimization_barrier(jnp.mean(centred * centred, axis=-1, keepdims=True))
    return centred * lax.rsqrt(variance + 1e-06) * gain_row + shift_row

def encode_pack(weights, patch_rows, image_index, position):
    attn_w, mlp_w, embed_w, vec_w = weights
    model_width = attn_w.shape[1]
    token_count = patch_rows.shape[0]
    head_shape = (token_count, H, model_width // H)
    embed_low = low(embed_w)
    attn_low = low(attn_w)
    mlp_low = low(mlp_w)
    embedded = product(patch_rows, embed_low[:PD]) + vec_w[10] + jnp.take(embed_low[PD:PD + GRID], position[0], axis=0) + jnp.take(embed_low[PD + GRID:], position[1], axis=0)
    embedded = low_back(embedded)
    normed = low(layer_norm(embedded, vec_w[4], vec_w[5]))
    queries = low_back(low(product(normed, attn_low[:model_width]) + vec_w[0]))
    key_rows = low_back(low(product(normed, attn_low[model_width:2 * model_width])))
    values = low_back(low(product(normed, attn_low[2 * model_width:3 * model_width]) + vec_w[1]))
    scores = jnp.einsum('qhd,khd->hqk', queries.reshape(head_shape), key_rows.reshape(head_shape), precision=highest)
    scores = low_back(scores * (model_width // H) ** (-0.5))
    same_image = image_index[:, None] == image_index[None, :]
    scores = jnp.where(same_image[None], scores, -1e+30)
    row_max = lax.optimization_barrier(jnp.max(scores, axis=-1, keepdims=True))
    exponents = jnp.exp(scores - row_max)
    probs_low = low(exponents / lax.optimization_barrier(jnp.sum(exponents, axis=-1, keepdims=True)))
    mixed_out = jnp.einsum('hqk,khd->qhd', probs_low, values.reshape(head_shape), precision=highest)
    mixed_out = low_back(low(mixed_out.reshape(token_count, model_width)))
    middle = embedded + low_back(product(mixed_out, attn_low[3 * model_width:]) + vec_w[2])
    normed_two = low(layer_norm(middle, vec_w[6], vec_w[7]))
    hidden = lax.dot_general(normed_two, mlp_low[:, :model_width], (((1,), (1,)), ((), ())), precision=highest)
    hidden = low_back(hidden + vec_w[11:].reshape(-1))
    active = low(jax.nn.gelu(hidden, approximate=False))
    final_rows = middle + low_back(product(active, mlp_low[:, model_width:]) + vec_w[3])
    closing = layer_norm(final_rows, vec_w[8], vec_w[9])
    member = (image_index[None, :] == jnp.arange(IMG_DEV)[:, None]).astype(jnp.float32)
    counts = lax.optimization_barrier(jnp.sum(member, axis=1))
    pooled = product(member, closing) / jnp.maximum(counts, 1.0)[:, None]
    return (pooled, counts)

def forward(params, patch_packs, image_ids, patch_place, labels):
    attn_w, mlp_w, embed_w, vec_w, head_w = params

    def one_pack(items):
        return jax.checkpoint(encode_pack)((attn_w, mlp_w, embed_w, vec_w), *items)
    pooled, counts = lax.map(one_pack, (patch_packs, image_ids, patch_place))
    pooled = low(pooled.reshape(-1, attn_w.shape[1]))
    valid = counts.reshape(-1) > 0.5
    logits = low_back(product(pooled, low(head_w)))
    usable = jnp.arange(head_w.shape[1]) < CLASSES
    logits = jnp.where(usable[None], logits, -1e+30)
    row_max = lax.optimization_barrier(jnp.max(logits, axis=1, keepdims=True))
    normaliser = row_max[:, 0] + jnp.log(lax.optimization_barrier(jnp.sum(jnp.exp(logits - row_max), axis=1)))
    target = jnp.take_along_axis(logits, labels.reshape(-1, 1).astype(jnp.int32), axis=1)[:, 0]
    image_total = jnp.sum(valid.astype(jnp.float32))
    loss_sum = jnp.sum(jnp.where(valid, normaliser - target, 0.0))
    return (loss_sum / image_total, (loss_sum, image_total))

def orthogonal(matrix):
    scaled = matrix / (jnp.sqrt(jnp.sum(matrix * matrix)) + 1e-07)
    for sweep_index in range(5):
        gram_matrix = jnp.dot(scaled.T, scaled, precision=highest)
        polynomial = newton_two * gram_matrix + newton_three * jnp.dot(gram_matrix, gram_matrix, precision=highest)
        scaled = newton_one * scaled + jnp.dot(scaled, polynomial, precision=highest)
    return scaled

def adam_step(weight, first_moment, second_moment, gradient, step_rate):
    first_moment = adam_first * first_moment + (1.0 - adam_first) * gradient
    second_moment = adam_second * second_moment + (1.0 - adam_second) * gradient * gradient
    first_hat = first_moment / (1.0 - adam_first ** STEP)
    second_hat = second_moment / (1.0 - adam_second ** STEP)
    weight = weight * (1.0 - step_rate * decay_rate) - step_rate * first_hat / (jnp.sqrt(second_hat) + 1e-08)
    return (weight, first_moment, second_moment)

def reference(patches, image_ids, patch_place, labels, attn_w, mlp_w, embed_w, vec_w, head_w, attn_mom, mlp_mom, embed_m, embed_v, vec_m, vec_v, head_m, head_v):
    pack_total, token_count = image_ids.shape
    patch_packs = patches.astype(jnp.float32).reshape(pack_total, token_count, -1)

    def loss_fn(*params):
        return forward(params, patch_packs, image_ids, patch_place, labels)
    mean_loss, pullback, totals = jax.vjp(loss_fn, attn_w, mlp_w, embed_w, vec_w, head_w, has_aux=True)
    loss_sum, image_total = totals
    grads = pullback(jnp.ones_like(mean_loss))
    grad_norm = jnp.sqrt(sum((jnp.sum(gradient * gradient) for gradient in grads)))
    factor = jnp.minimum(1.0, clip_limit / (grad_norm + 1e-06))
    g_attn, g_mlp, g_embed, g_vec, g_head = [factor * gradient for gradient in grads]
    model_width = attn_w.shape[1]
    attn_mom_out = momentum_keep * attn_mom + g_attn
    attn_dir = jnp.concatenate([orthogonal(attn_mom_out[index * model_width:(index + 1) * model_width]) for index in range(4)], axis=0)
    attn_out = attn_w * (1.0 - muon_rate * decay_rate) - muon_rate * attn_dir
    mlp_mom_out = momentum_keep * mlp_mom + g_mlp
    mlp_dir = jnp.concatenate([orthogonal(mlp_mom_out[:, :model_width]), orthogonal(mlp_mom_out[:, model_width:])], axis=1)
    mlp_out = mlp_w * (1.0 - muon_rate * decay_rate) - muon_rate * math.sqrt(FF / D) * mlp_dir
    embed_out, embed_m_out, embed_v_out = adam_step(embed_w, embed_m, embed_v, g_embed, adam_rate)
    vec_out, vec_m_out, vec_v_out = adam_step(vec_w, vec_m, vec_v, g_vec, vector_rate)
    head_out, head_m_out, head_v_out = adam_step(head_w, head_m, head_v, g_head, adam_rate)
    return (loss_sum, image_total, grad_norm, attn_out, attn_mom_out, attn_out.astype(jnp.bfloat16), mlp_out, mlp_mom_out, mlp_out.astype(jnp.bfloat16), embed_out, embed_m_out, embed_v_out, embed_out.astype(jnp.bfloat16), vec_out, vec_m_out, vec_v_out, vec_out.astype(jnp.bfloat16), head_out, head_m_out, head_v_out, head_out.astype(jnp.bfloat16))
```

```python
import math

import jax
import jax.numpy as jnp
from jax import lax
from jax.sharding import PartitionSpec as P

H = 12
CLASSES = 21843
STEP = 10


highest = lax.Precision.HIGHEST
newton_one = 3.4445
newton_two = -4.775
newton_three = 2.0315
clip_limit = 0.05
muon_rate = 0.3
decay_rate = 0.05
adam_rate = 0.01
vector_rate = 0.05
momentum_keep = 0.5
adam_first = 0.5
adam_second = 0.999


AXES = ("dp", "cls")


def swap(value, count, masks):
    return lax.ppermute(value, AXES, [(i, i ^ masks[i & 1]) for i in range(count)])


def pick(value, index, axis):
    return lax.dynamic_index_in_dim(value, index, axis, keepdims=False)


def codes(masks):
    found = [0]
    for mask in masks:
        found = found + [code ^ mask for code in found]
    return found


def ordered_pair(bit, mine, other, axis):
    return jnp.where(
        bit == 0, jnp.stack([mine, other], axis=axis), jnp.stack([other, mine], axis=axis)
    )


def product(left_side, right_side):
    return jnp.dot(left_side, right_side, precision=highest)


def low_dot(left_side, right_side):
    return jnp.dot(left_side, right_side, preferred_element_type=jnp.float32)


def contract_rows(left_side, right_side):
    return lax.dot_general(
        left_side, right_side, (((0,), (0,)), ((), ())), preferred_element_type=jnp.float32
    )


def contract_cols(left_side, right_side):
    return lax.dot_general(
        left_side, right_side, (((1,), (1,)), ((), ())), preferred_element_type=jnp.float32
    )


def layer_norm(inputs, gain_row, shift_row):
    mean_row = jnp.mean(inputs, axis=-1, keepdims=True)
    centred = inputs - mean_row
    variance = jnp.mean(centred * centred, axis=-1, keepdims=True)
    return centred * lax.rsqrt(variance + 1e-06) * gain_row + shift_row


def exact_gelu(value):
    return jax.nn.gelu(value, approximate=False)


def attend(queries, key_rows, same_image):
    token_count, model_width = queries.shape
    head_shape = (token_count, H, model_width // H)
    scores = jnp.einsum(
        "qhd,khd->hqk",
        queries.reshape(head_shape),
        key_rows.reshape(head_shape),
        preferred_element_type=jnp.float32,
    ) * (model_width // H) ** (-0.5)
    return jnp.where(same_image[None], scores, -1e30)


def layer_forward(weights, vec_w, first_bias, patches, image_index, position):
    attn_b, embed_b, mlp_parts = weights
    token_count = patches.shape[0]
    model_width = attn_b.shape[1]
    patch_dim = patches.shape[1]
    grid_size = (embed_b.shape[0] - patch_dim) // 2
    head_shape = (token_count, H, model_width // H)
    embedded = (
        low_dot(patches, embed_b[:patch_dim])
        + vec_w[10]
        + jnp.take(embed_b[patch_dim : patch_dim + grid_size], position[0], axis=0).astype(
            jnp.float32
        )
        + jnp.take(embed_b[patch_dim + grid_size :], position[1], axis=0).astype(jnp.float32)
    )
    normed = layer_norm(embedded, vec_w[4], vec_w[5]).astype(jnp.bfloat16)
    queries = (low_dot(normed, attn_b[:model_width]) + vec_w[0]).astype(jnp.bfloat16)
    key_rows = low_dot(normed, attn_b[model_width : 2 * model_width]).astype(jnp.bfloat16)
    values = (low_dot(normed, attn_b[2 * model_width : 3 * model_width]) + vec_w[1]).astype(
        jnp.bfloat16
    )
    same_image = image_index[:, None] == image_index[None, :]
    scores = attend(queries, key_rows, same_image)
    row_max = jnp.max(scores, axis=-1, keepdims=True)
    exponents = jnp.exp(scores - row_max)
    row_total = jnp.sum(exponents, axis=-1, keepdims=True)
    probs_low = (exponents / row_total).astype(jnp.bfloat16)
    summary = row_max + jnp.log(row_total)
    mixed_out = (
        jnp.einsum(
            "hqk,khd->qhd",
            probs_low,
            values.reshape(head_shape),
            preferred_element_type=jnp.float32,
        )
        .reshape(token_count, model_width)
        .astype(jnp.bfloat16)
    )
    middle = embedded + low_dot(mixed_out, attn_b[3 * model_width :]) + vec_w[2]
    normed_two = layer_norm(middle, vec_w[6], vec_w[7]).astype(jnp.bfloat16)
    final_rows = middle + vec_w[3]
    hidden, active = [], []
    for part, bias in zip(mlp_parts, first_bias):
        hidden.append(contract_cols(normed_two, part[:, :model_width]) + bias)
        active.append(exact_gelu(hidden[-1]).astype(jnp.bfloat16))
        final_rows = final_rows + low_dot(active[-1], part[:, model_width:])
    kept_rows = (
        embedded,
        normed,
        queries,
        key_rows,
        values,
        summary,
        mixed_out,
        middle,
        normed_two,
        hidden,
        active,
    )
    return (final_rows, kept_rows)


def mlp_backward(mlp_parts, normed_two, hidden, active, d_out, send):
    model_width = d_out.shape[1]
    d_normed_two = 0.0
    bias_grads, grads = [None] * 4, [None] * 4
    for index in (2, 3, 1, 0):
        part = mlp_parts[index]
        d_active = contract_cols(d_out, part[:, model_width:])
        d_hidden = jax.vjp(exact_gelu, hidden[index])[1](d_active)[0].astype(jnp.bfloat16)
        bias_grads[index] = jnp.sum(d_hidden.astype(jnp.float32), axis=0)
        both = (contract_rows(d_hidden, normed_two), contract_rows(active[index], d_out))
        grads[index] = send(index, both, grads)
        d_normed_two = d_normed_two + low_dot(d_hidden, part[:, :model_width])
    return d_normed_two, jnp.stack(bias_grads), grads[0]


def attention_backward(weights, vec_w, patches, image_index, position, kept_rows, d_middle):
    attn_b, embed_b = weights
    embedded, normed, queries, key_rows, values, summary, mixed_out = kept_rows
    token_count, model_width = embedded.shape
    patch_dim = patches.shape[1]
    grid_size = (embed_b.shape[0] - patch_dim) // 2
    head_shape = (token_count, H, model_width // H)
    d_proj = d_middle.astype(jnp.bfloat16)
    g_out_bias = jnp.sum(d_proj.astype(jnp.float32), axis=0)
    g_out = contract_rows(mixed_out, d_proj)
    d_mixed = (
        contract_cols(d_proj, attn_b[3 * model_width :]).astype(jnp.bfloat16).reshape(head_shape)
    )
    same_image = image_index[:, None] == image_index[None, :]
    scores = attend(queries, key_rows, same_image)
    probs_full = jnp.exp(scores - summary)
    probs_low = probs_full.astype(jnp.bfloat16)
    d_values = jnp.einsum("hqk,qhd->khd", probs_low, d_mixed, preferred_element_type=jnp.float32)
    d_values = d_values.reshape(token_count, model_width).astype(jnp.bfloat16)
    d_probs = jnp.einsum(
        "qhd,khd->hqk", d_mixed, values.reshape(head_shape), preferred_element_type=jnp.float32
    )
    d_scores = probs_full * (d_probs - jnp.sum(probs_full * d_probs, axis=-1, keepdims=True))
    d_scores = d_scores.astype(jnp.bfloat16)
    scale = (model_width // H) ** (-0.5)
    d_queries = jnp.einsum(
        "hqk,khd->qhd", d_scores, key_rows.reshape(head_shape), preferred_element_type=jnp.float32
    )
    d_queries = (d_queries * scale).reshape(token_count, model_width).astype(jnp.bfloat16)
    d_keys = jnp.einsum(
        "hqk,qhd->khd", d_scores, queries.reshape(head_shape), preferred_element_type=jnp.float32
    )
    d_keys = (d_keys * scale).reshape(token_count, model_width).astype(jnp.bfloat16)
    g_query = contract_rows(normed, d_queries)
    g_key = contract_rows(normed, d_keys)
    g_value = contract_rows(normed, d_values)
    g_query_bias = jnp.sum(d_queries.astype(jnp.float32), axis=0)
    g_value_bias = jnp.sum(d_values.astype(jnp.float32), axis=0)
    d_normed = (
        contract_cols(d_queries, attn_b[:model_width])
        + contract_cols(d_keys, attn_b[model_width : 2 * model_width])
        + contract_cols(d_values, attn_b[2 * model_width : 3 * model_width])
    )
    d_emb_norm, g_gain_one, g_shift_one = jax.vjp(layer_norm, embedded, vec_w[4], vec_w[5])[1](
        d_normed
    )
    d_embed_low = (d_middle + d_emb_norm).astype(jnp.bfloat16)
    g_patch_bias = jnp.sum(d_embed_low.astype(jnp.float32), axis=0)
    grid_index = jnp.arange(grid_size)
    row_hot = (position[0][:, None] == grid_index[None]).astype(jnp.bfloat16)
    col_hot = (position[1][:, None] == grid_index[None]).astype(jnp.bfloat16)
    embed_grad = jnp.concatenate(
        [
            contract_rows(patches, d_embed_low),
            contract_rows(row_hot, d_embed_low),
            contract_rows(col_hot, d_embed_low),
        ],
        axis=0,
    )
    attn_grad = jnp.concatenate([g_query, g_key, g_value, g_out], axis=0)
    small = (g_query_bias, g_value_bias, g_out_bias, g_gain_one, g_shift_one, g_patch_bias)
    return (attn_grad, embed_grad, small)


def gram_of(parts):
    total = contract_rows(parts[0], parts[0])
    for part in parts[1:]:
        total = total + contract_rows(part, part)
    return total


def update_of(gram_matrix):
    low_gram = gram_matrix.astype(jnp.bfloat16)
    return (newton_two * gram_matrix + newton_three * low_dot(low_gram, low_gram)).astype(
        jnp.bfloat16
    )


def orthogonal_rows(parts, row_count, full_steps):
    gram_matrix = gram_of(parts)
    width = gram_matrix.shape[0]
    trace = jnp.sum(jnp.where(jnp.eye(width, dtype=bool), gram_matrix, 0.0))
    inverse = 1.0 / (jnp.sqrt(trace) + 1e-07)
    gram_matrix = gram_matrix * (inverse * inverse)
    rows = parts[0][:row_count].astype(jnp.float32)
    for step in range(5):
        change = update_of(gram_matrix)
        if step < full_steps:
            scale = inverse if step == 0 else 1.0
            wide = [
                scale * (newton_one * part.astype(jnp.float32) + low_dot(part, change))
                for part in parts
            ]
            rows = wide[0][:row_count]
            parts = [part.astype(jnp.bfloat16) for part in wide]
            if step < 4:
                gram_matrix = gram_of(parts)
        else:
            rows = newton_one * rows + low_dot(rows.astype(jnp.bfloat16), change)
            if step < 4:
                once = newton_one * gram_matrix + low_dot(gram_matrix.astype(jnp.bfloat16), change)
                gram_matrix = newton_one * once + low_dot(once.astype(jnp.bfloat16), change)
    return rows


def adam_step(weight, first_moment, second_moment, gradient, step_rate):
    first_moment = adam_first * first_moment + (1.0 - adam_first) * gradient
    second_moment = adam_second * second_moment + (1.0 - adam_second) * gradient * gradient
    first_hat = first_moment / (1.0 - adam_first**STEP)
    second_hat = second_moment / (1.0 - adam_second**STEP)
    weight = weight * (1.0 - step_rate * decay_rate) - step_rate * first_hat / (
        jnp.sqrt(second_hat) + 1e-08
    )
    return (weight, first_moment, second_moment)


def on_device(
    patches,
    image_ids,
    patch_place,
    labels,
    attn_w,
    mlp_w,
    embed_w,
    vec_w,
    head_w,
    attn_mom,
    mlp_mom,
    embed_m,
    embed_v,
    vec_m,
    vec_v,
    head_m,
    head_v,
):
    groups = lax.axis_size("cls")
    owners = lax.axis_size("dp")
    count = groups * owners
    top = count.bit_length() - 1
    low_bits = groups.bit_length() - 1
    member_index = lax.axis_index("cls")
    owner_index = lax.axis_index("dp")
    me = owner_index * groups + member_index
    core = me & 1
    model_width = vec_w.shape[1]
    slot_count = labels.shape[1]
    high_bits = list(range(top - 1, 2, -1))
    third, fourth, pair = (2, 4), (4, 2), (1, 1)
    third_mine = jnp.where(core == 0, third[0], third[1])
    fourth_mine = jnp.where(core == 0, fourth[0], fourth[1])

    def exchange(value, masks):
        return swap(value, count, masks)

    def bit_of(bit):
        return (me >> bit) & 1

    attn_rows, embed_rows, mlp_rows = attn_w.shape[0], embed_w.shape[0], mlp_w.shape[0]
    block = jnp.concatenate([attn_w, embed_w], axis=0).astype(jnp.bfloat16)
    for axis, bit in enumerate(high_bits):
        block = ordered_pair(bit_of(bit), block, exchange(block, (1 << bit,) * 2), axis)
    block = block.reshape(-1, attn_rows + embed_rows, model_width)
    pieces = [block, exchange(block, third)]
    pieces = jnp.stack(pieces)
    pieces = jnp.concatenate([pieces, exchange(pieces, fourth)], axis=0)
    others = exchange(pieces, pair)
    sibling = me ^ 1
    places = [
        me,
        me ^ third_mine,
        me ^ fourth_mine,
        me ^ 6,
        sibling,
        sibling ^ fourth_mine,
        sibling ^ third_mine,
        sibling ^ 6,
    ]
    attn_b = jnp.zeros((count // 8, 8, attn_rows, model_width), jnp.bfloat16)
    embed_b = jnp.zeros((count // 8, 8, embed_rows, model_width), jnp.bfloat16)
    for index, place in enumerate(places):
        piece = (pieces if index < 4 else others)[index % 4]
        attn_b = lax.dynamic_update_slice_in_dim(attn_b, piece[:, None, :attn_rows], place & 7, 1)
        embed_b = lax.dynamic_update_slice_in_dim(embed_b, piece[:, None, attn_rows:], place & 7, 1)
    attn_b = attn_b.reshape(count * attn_rows, model_width)
    embed_b = embed_b.reshape(count * embed_rows, model_width)

    block = mlp_w.astype(jnp.bfloat16)[None]
    for bit in high_bits:
        block = jnp.concatenate([block, exchange(block, (1 << bit,) * 2)], axis=0)
    part_a = jnp.concatenate([block, exchange(block, third)], axis=0)
    part_b = exchange(part_a, fourth)
    part_c = exchange(part_a, pair)
    part_d = exchange(part_b, pair)
    mlp_parts = [
        part.reshape(-1, 2 * model_width) for part in (part_a, part_b, part_c, part_d)
    ]
    masks = [1 << bit for bit in high_bits]
    own_codes = [jnp.array(codes(masks + [third[c], fourth[c]]), jnp.int32) for c in (0, 1)]
    arrival = me ^ jnp.where(
        core == 0,
        jnp.concatenate([own_codes[0], own_codes[1] ^ 1]),
        jnp.concatenate([own_codes[1], own_codes[0] ^ 1]),
    )
    first_bias = jnp.take(vec_w[11:].reshape(count, mlp_rows), arrival, axis=0)
    first_bias = first_bias.reshape(4, -1)

    shard_rows, shard_width = head_w.shape
    chunk = -(-shard_width // (owners * 128)) * 128
    padding = owners * chunk - shard_width
    owner_bits = list(range(low_bits, top))

    def transposed(value):
        value = value.reshape((2,) * len(owner_bits) + value.shape[1:])
        for bit in owner_bits:
            axis = top - 1 - bit
            mine = bit_of(bit)
            stay, leave = pick(value, mine, axis), pick(value, 1 - mine, axis)
            value = ordered_pair(mine, stay, exchange(leave, (1 << bit,) * 2), axis)
        return value.reshape((owners,) + value.shape[len(owner_bits) :])

    head_low = jnp.pad(head_w.astype(jnp.bfloat16), ((0, 0), (0, padding)))
    head_low = head_low.reshape(shard_rows, owners, chunk).transpose(1, 0, 2)
    head_b = transposed(head_low).reshape(owners * shard_rows, chunk)

    image_index = lax.dynamic_index_in_dim(image_ids, member_index, 0, keepdims=False)
    my_labels = lax.dynamic_index_in_dim(labels, member_index, 0, keepdims=False)
    position = patch_place[0]
    final_rows, kept_rows = layer_forward(
        (attn_b, embed_b, mlp_parts), vec_w, first_bias, patches, image_index, position
    )
    closing, close_pull = jax.vjp(layer_norm, final_rows, vec_w[8], vec_w[9])
    member = (image_index[None, :] == jnp.arange(slot_count)[:, None]).astype(jnp.float32)
    slot_sizes = jnp.sum(member, axis=1)
    divisor = jnp.maximum(slot_sizes, 1.0)[:, None]
    pooled = product(member, closing) / divisor
    facts = jnp.stack(
        [(slot_sizes > 0.5).astype(jnp.int32), my_labels // 256, my_labels % 256], axis=1
    )
    facts = jnp.pad(facts, ((0, 0), (0, 125))).astype(jnp.bfloat16)
    block = jnp.concatenate([pooled.astype(jnp.bfloat16), facts], axis=1)
    for axis, bit in enumerate(range(top - 1, -1, -1)):
        block = ordered_pair(bit_of(bit), block, exchange(block, (1 << bit,) * 2), axis)
    block = block.reshape(count * slot_count, -1)
    all_pooled = block[:, :model_width]
    facts = block[:, model_width : model_width + 3].astype(jnp.int32)
    valid = facts[:, 0] > 0
    all_labels = facts[:, 1] * 256 + facts[:, 2]
    image_total = jnp.sum(valid.astype(jnp.float32))

    logits = low_dot(all_pooled, head_b)
    within = owner_index * chunk + jnp.arange(chunk)
    columns = member_index * shard_width + within
    usable = (within < shard_width) & (columns < CLASSES)
    logits = jnp.where(usable[None], logits, -1e30)
    onehot = (usable[None] & (columns[None, :] == all_labels[:, None])).astype(jnp.float32)
    row_max = jnp.max(logits, axis=1)
    exp_sums = jnp.sum(jnp.exp(logits - row_max[:, None]), axis=1)
    stats = jnp.stack([row_max, exp_sums, jnp.sum(onehot * logits, axis=1)])
    for bit in range(top):
        other = exchange(stats, (1 << bit,) * 2)
        lower = jnp.where(bit_of(bit) == 0, stats, other)
        upper = jnp.where(bit_of(bit) == 0, other, stats)
        row_max = jnp.maximum(lower[0], upper[0])
        exp_sums = lower[1] * jnp.exp(lower[0] - row_max) + upper[1] * jnp.exp(upper[0] - row_max)
        stats = jnp.stack([row_max, exp_sums, lower[2] + upper[2]])
    normaliser = stats[0] + jnp.log(stats[1])
    loss_sum = jnp.sum(jnp.where(valid, normaliser - stats[2], 0.0))
    probs_class = jnp.exp(logits - normaliser[:, None])
    d_logits = (jnp.where(valid[:, None], probs_class - onehot, 0.0) / image_total).astype(
        jnp.bfloat16
    )
    d_pooled = contract_cols(d_logits, head_b)
    d_pooled = d_pooled.reshape((2,) * top + (slot_count, model_width))
    for bit in range(top):
        axis = top - 1 - bit
        mine = bit_of(bit)
        leave = pick(d_pooled, 1 - mine, axis).astype(jnp.bfloat16)
        d_pooled = pick(d_pooled, mine, axis) + exchange(leave, (1 << bit,) * 2).astype(
            jnp.float32
        )
    head_grad = contract_rows(all_pooled, d_logits).astype(jnp.bfloat16)
    head_grad = transposed(head_grad.reshape(owners, shard_rows, chunk)).transpose(1, 0, 2)
    head_grad = head_grad.reshape(shard_rows, owners * chunk)[:, :shard_width].astype(jnp.float32)

    d_closing = product(member.T, d_pooled / divisor)
    d_final, g_gain_final, g_shift_final = close_pull(d_closing)
    d_out = d_final.astype(jnp.bfloat16)
    g_second_bias = jnp.sum(d_out.astype(jnp.float32), axis=0)

    def send(index, both, grads):
        if index in (2, 3):
            low = jnp.concatenate([grad.astype(jnp.bfloat16) for grad in both], axis=1)
            return exchange(low, pair)
        arrived = grads[3 if index == 1 else 2].astype(jnp.float32)
        summed = jnp.concatenate(both, axis=1) + arrived
        if index == 1:
            return exchange(summed.astype(jnp.bfloat16), fourth)
        return summed + grads[1].astype(jnp.float32)

    (embedded, normed, queries, key_rows, values, summary, mixed_out, middle, normed_two, hidden, active) = (
        kept_rows
    )
    d_normed_two, bias_grads, mlp_grad = mlp_backward(
        mlp_parts, normed_two, hidden, active, d_out, send
    )
    mlp_grad = mlp_grad.reshape(-1, mlp_rows, 2 * model_width)
    for stage in [third] + [(1 << bit,) * 2 for bit in reversed(high_bits)]:
        half = mlp_grad.shape[0] // 2
        mlp_grad = mlp_grad[:half] + exchange(
            mlp_grad[half:].astype(jnp.bfloat16), stage
        ).astype(jnp.float32)
    mlp_sum = mlp_grad[0]

    def by_core(value):
        low = value.astype(jnp.bfloat16)
        left, right = low[:, :model_width], low[:, model_width:]
        mine = jnp.where(core == 0, left, right)
        rows = jnp.stack([mine, exchange(jnp.where(core == 0, right, left), pair)])
        for stage in [(1 << bit,) * 2 for bit in high_bits] + [third]:
            rows = jnp.concatenate([rows, exchange(rows, stage)], axis=0)
        return [part.reshape(-1, model_width) for part in (rows, exchange(rows, fourth))]

    def by_block(value):
        rows = value.astype(jnp.bfloat16)[None]
        for stage in [(1 << bit,) * 2 for bit in high_bits[2:]] + [third, fourth, pair]:
            rows = jnp.concatenate([rows, exchange(rows, stage)], axis=0)
        return rows.reshape(-1, model_width)

    mlp_mom_late, attn_mom_late, _ = lax.optimization_barrier((mlp_mom, attn_mom, part_d))
    mlp_moms = by_core(mlp_mom_late)
    attn_moms = by_block(attn_mom_late)
    mlp_grads = by_core(mlp_sum)

    d_mid_norm, g_gain_two, g_shift_two = jax.vjp(layer_norm, middle, vec_w[6], vec_w[7])[1](
        d_normed_two
    )
    d_middle = d_final + d_mid_norm
    attn_grad, embed_grad, small = attention_backward(
        (attn_b, embed_b),
        vec_w,
        patches,
        image_index,
        position,
        (embedded, normed, queries, key_rows, values, summary, mixed_out),
        d_middle,
    )
    g_query_bias, g_value_bias, g_out_bias, g_gain_one, g_shift_one, g_patch_bias = small
    g_first_bias = jnp.take(
        bias_grads.reshape(count, mlp_rows), jnp.argsort(arrival), axis=0
    )

    def scattered(grad, rows):
        grad = grad.reshape(count // 8, 4, 2, rows, model_width)
        leave = pick(grad, 1 - core, 2).astype(jnp.bfloat16)
        grad = pick(grad, core, 2) + exchange(leave, pair).astype(jnp.float32)
        quarter = (me >> 1) & 3
        to_third, to_fourth = third_mine >> 1, fourth_mine >> 1
        leave = [pick(grad, quarter ^ to_fourth, 1), pick(grad, quarter ^ 3, 1)]
        leave = exchange(jnp.stack(leave).astype(jnp.bfloat16), fourth).astype(jnp.float32)
        leaving = (pick(grad, quarter ^ to_third, 1) + leave[1]).astype(jnp.bfloat16)
        grad = pick(grad, quarter, 1) + leave[0]
        grad = grad + exchange(leaving, third).astype(jnp.float32)
        grad = grad.reshape((2,) * len(high_bits) + (rows, model_width))
        for bit in reversed(high_bits):
            axis = top - 1 - bit
            mine = bit_of(bit)
            leave = pick(grad, 1 - mine, axis).astype(jnp.bfloat16)
            grad = pick(grad, mine, axis) + exchange(leave, (1 << bit,) * 2).astype(jnp.float32)
        return grad

    attn_sum = scattered(attn_grad, attn_rows)
    embed_sum = scattered(embed_grad, embed_rows)
    attn_grads = by_block(attn_sum)
    vec_grad = jnp.concatenate(
        [
            jnp.stack(
                [
                    g_query_bias,
                    g_value_bias,
                    g_out_bias,
                    g_second_bias,
                    g_gain_one,
                    g_shift_one,
                    g_gain_two,
                    g_shift_two,
                    g_gain_final,
                    g_shift_final,
                    g_patch_bias,
                ]
            ),
            g_first_bias.reshape(-1, model_width),
        ],
        axis=0,
    )
    local_squares = sum(
        jnp.sum(grad * grad, axis=0) for grad in (attn_sum, embed_sum, mlp_sum[:, :model_width], mlp_sum[:, model_width:])
    )
    head_squares = jnp.sum(head_grad * head_grad) / model_width
    small_sums = jnp.concatenate([vec_grad, (local_squares + head_squares)[None]], axis=0)
    for bit in range(top):
        small_sums = small_sums + exchange(small_sums, (1 << bit,) * 2)
    vec_sum = small_sums[:-1]
    grad_norm = jnp.sqrt(jnp.sum(small_sums[-1]) + jnp.sum(vec_sum * vec_sum))
    factor = jnp.minimum(1.0, clip_limit / (grad_norm + 1e-06))
    attn_mom_out = momentum_keep * attn_mom + factor * attn_sum
    mlp_mom_out = momentum_keep * mlp_mom + factor * mlp_sum

    def momentum_of(moment, grad):
        return (
            momentum_keep * moment.astype(jnp.float32) + factor * grad.astype(jnp.float32)
        ).astype(jnp.bfloat16)

    mlp_result = orthogonal_rows(
        [momentum_of(moment, grad) for moment, grad in zip(mlp_moms, mlp_grads)], 2 * mlp_rows, 2
    )
    mlp_other = exchange(mlp_result[mlp_rows:], pair)
    mlp_result = mlp_result[:mlp_rows]
    mlp_dir = jnp.concatenate(
        [
            jnp.where(core == 0, mlp_result, mlp_other),
            jnp.where(core == 0, mlp_other, mlp_result),
        ],
        axis=1,
    )
    attn_dir = orthogonal_rows([momentum_of(attn_moms, attn_grads)], attn_rows, 4)
    mlp_scale = math.sqrt(mlp_rows * count / model_width)
    attn_out = attn_w * (1.0 - muon_rate * decay_rate) - muon_rate * attn_dir
    mlp_out = mlp_w * (1.0 - muon_rate * decay_rate) - muon_rate * mlp_scale * mlp_dir
    embed_out, embed_m_out, embed_v_out = adam_step(
        embed_w, embed_m, embed_v, factor * embed_sum, adam_rate
    )
    vec_out, vec_m_out, vec_v_out = adam_step(vec_w, vec_m, vec_v, factor * vec_sum, vector_rate)
    head_out, head_m_out, head_v_out = adam_step(
        head_w, head_m, head_v, factor * head_grad, adam_rate
    )
    return (
        loss_sum,
        image_total,
        grad_norm,
        attn_out,
        attn_mom_out,
        attn_out.astype(jnp.bfloat16),
        mlp_out,
        mlp_mom_out,
        mlp_out.astype(jnp.bfloat16),
        embed_out,
        embed_m_out,
        embed_v_out,
        embed_out.astype(jnp.bfloat16),
        vec_out,
        vec_m_out,
        vec_v_out,
        vec_out.astype(jnp.bfloat16),
        head_out,
        head_m_out,
        head_v_out,
        head_out.astype(jnp.bfloat16),
    )


def solution(mesh):
    return jax.shard_map(
        on_device,
        mesh=mesh,
        in_specs=(
            P(("dp", "cls"), None),
            P("dp", None),
            P(("dp", "cls"), None, None),
            P("dp", None),
            P(("dp", "cls"), None),
            P(("dp", "cls"), None),
            P(("dp", "cls"), None),
            P(),
            P("dp", "cls"),
            P(("dp", "cls"), None),
            P(("dp", "cls"), None),
            P(("dp", "cls"), None),
            P(("dp", "cls"), None),
            P(),
            P(),
            P("dp", "cls"),
            P("dp", "cls"),
        ),
        out_specs=(
            P(),
            P(),
            P(),
            P(("dp", "cls"), None),
            P(("dp", "cls"), None),
            P(("dp", "cls"), None),
            P(("dp", "cls"), None),
            P(("dp", "cls"), None),
            P(("dp", "cls"), None),
            P(("dp", "cls"), None),
            P(("dp", "cls"), None),
            P(("dp", "cls"), None),
            P(("dp", "cls"), None),
            P(),
            P(),
            P(),
            P(),
            P("dp", "cls"),
            P("dp", "cls"),
            P("dp", "cls"),
            P("dp", "cls"),
        ),
        check_vma=False,
    )
```

```python
import functools
import math

import jax
import jax.numpy as jnp
from jax import lax
from jax.experimental import pallas as pl
from jax.experimental.pallas import tpu as pltpu
from jax.sharding import PartitionSpec as P

H = 12
CLASSES = 21843
STEP = 10


highest = lax.Precision.HIGHEST
newton_one = 3.4445
newton_two = -4.775
newton_three = 2.0315
clip_limit = 0.05
muon_rate = 0.3
decay_rate = 0.05
adam_rate = 0.01
vector_rate = 0.05
momentum_keep = 0.5
adam_first = 0.5
adam_second = 0.999


AXES = ("dp", "cls")


def swap(value, count, masks):
    return lax.ppermute(value, AXES, [(i, i ^ masks[i & 1]) for i in range(count)])


def pick(value, index, axis):
    return lax.dynamic_index_in_dim(value, index, axis, keepdims=False)


def codes(masks):
    found = [0]
    for mask in masks:
        found = found + [code ^ mask for code in found]
    return found


def ordered_pair(bit, mine, other, axis):
    return jnp.where(
        bit == 0, jnp.stack([mine, other], axis=axis), jnp.stack([other, mine], axis=axis)
    )


def product(left_side, right_side):
    return jnp.dot(left_side, right_side, precision=highest)


def low_dot(left_side, right_side):
    return jnp.dot(left_side, right_side, preferred_element_type=jnp.float32)


def contract_rows(left_side, right_side):
    return lax.dot_general(
        left_side, right_side, (((0,), (0,)), ((), ())), preferred_element_type=jnp.float32
    )


def contract_cols(left_side, right_side):
    return lax.dot_general(
        left_side, right_side, (((1,), (1,)), ((), ())), preferred_element_type=jnp.float32
    )


def layer_norm(inputs, gain_row, shift_row):
    mean_row = jnp.mean(inputs, axis=-1, keepdims=True)
    centred = inputs - mean_row
    variance = jnp.mean(centred * centred, axis=-1, keepdims=True)
    return centred * lax.rsqrt(variance + 1e-06) * gain_row + shift_row


def tie(*values):
    return lax.optimization_barrier(values)


class Lane:
    def __init__(self, steps, exchange, what):
        self.steps, self.exchange, self.what = steps, exchange, what
        self.moving, self.result = False, None
        self.value, self.masks = next(steps)

    def advance(self, value):
        masks = self.masks
        if self.moving:
            try:
                value, masks = self.steps.send(value)
            except StopIteration as end:
                self.value, self.result, self.moving = None, end.value, False
                return
        self.moving = True
        self.value, self.masks = self.exchange(value, masks, self.what), masks


def sync(values, *lanes):
    lanes = [lane for lane in lanes if lane.result is None]
    tied = tie(*values, *[lane.value for lane in lanes])
    for lane, value in zip(lanes, tied[len(values) :]):
        lane.advance(value)
    return tied[: len(values)]


def finish(*lanes):
    while any(lane.result is None for lane in lanes):
        sync((), *lanes)
    return [lane.result for lane in lanes]


def collecting(value, stages):
    for stage in stages[:-1]:
        value = jnp.concatenate([value, (yield value, stage)], axis=0)
    return [value, (yield value, stages[-1])]


def gelu_with_slope(value):
    size = jnp.abs(value)
    bell = jnp.exp(-0.5 * value * value)
    t = 1.0 / (1.0 + (0.3275911 * 0.7071067811865476) * size)
    poly = 1.061405429
    for term in (-1.453152027, 1.421413741, -0.284496736, 0.254829592):
        poly = poly * t + term
    tail = 0.5 * poly * t * bell
    share = jnp.where(value < 0, tail, 1.0 - tail)
    return value * share, share + value * (0.3989422804014327 * bell)


def projections(attn_b, vec_w, embedded):
    model_width = attn_b.shape[1]
    normed = layer_norm(embedded, vec_w[4], vec_w[5]).astype(jnp.bfloat16)
    queries = (low_dot(normed, attn_b[:model_width]) + vec_w[0]).astype(jnp.bfloat16)
    key_rows = low_dot(normed, attn_b[model_width : 2 * model_width]).astype(jnp.bfloat16)
    values = (low_dot(normed, attn_b[2 * model_width : 3 * model_width]) + vec_w[1]).astype(
        jnp.bfloat16
    )
    return (normed, queries, key_rows, values)


def half_of(value, half, width):
    lane = lax.broadcasted_iota(jnp.int32, value.shape, 1)
    keep = (lane >= half * width) & (lane < (half + 1) * width)
    return jnp.where(keep, value, jnp.zeros_like(value))


def mixing_kernel(width, rows, ids_down_ref, ids_ref, q_ref, k_ref, v_ref, out_ref, summary_ref, seen_ref):
    step = pl.program_id(0)
    pack = q_ref.shape[1] // width
    keys = [half_of(k_ref[...], half, width) for half in range(pack)]
    values = [half_of(v_ref[...], half, width) for half in range(pack)]
    scale = width ** (-0.5)
    lane = lax.broadcasted_iota(jnp.int32, (rows, seen_ref.shape[1]), 1)
    for start in range(0, q_ref.shape[0], rows):
        here = pl.ds(start, rows)
        same = ids_down_ref[here] == ids_ref[...]
        queries = q_ref[here]
        seen = seen_ref[here]
        total = None
        for half in range(pack):
            scores = jnp.where(same, contract_cols(queries, keys[half]) * scale, -1e30)
            top = jnp.max(scores, axis=1, keepdims=True)
            exponents = jnp.exp(scores - top)
            sums = jnp.sum(exponents, axis=1, keepdims=True)
            probs = (exponents * (1.0 / sums)).astype(jnp.bfloat16)
            mixed = low_dot(probs, values[half])
            total = mixed if total is None else total + mixed
            seen = jnp.where(lane == step * pack + half, top + jnp.log(sums), seen)
        out_ref[here] = total.astype(out_ref.dtype)
        seen_ref[here] = seen

    @pl.when(step == pl.num_programs(0) - 1)
    def _():
        summary_ref[...] = seen_ref[...].T[: summary_ref.shape[0]]


def mixing(queries, key_rows, values, image_index, heads, rows=256):
    token_count, model_width = queries.shape
    width = model_width // heads
    pack = 128 // width
    tile = pl.BlockSpec((token_count, 128), lambda step: (0, step))

    def whole(shape):
        return pl.BlockSpec(shape, lambda step: (0, 0))

    kept = -(-heads // 8) * 8
    return pl.pallas_call(
        functools.partial(mixing_kernel, width, rows),
        grid=(heads // pack,),
        out_shape=(
            jax.ShapeDtypeStruct((token_count, model_width), jnp.bfloat16),
            jax.ShapeDtypeStruct((kept, token_count), jnp.float32),
        ),
        in_specs=[whole((token_count, 1)), whole((1, token_count)), tile, tile, tile],
        out_specs=(tile, whole((kept, token_count))),
        scratch_shapes=[pltpu.VMEM((token_count, 128), jnp.float32)],
        compiler_params=pltpu.CompilerParams(vmem_limit_bytes=32 * 1024 * 1024),
        cost_estimate=pl.CostEstimate(
            flops=4 * token_count * token_count * model_width,
            bytes_accessed=8 * token_count * model_width,
            transcendentals=heads * token_count * token_count,
        ),
        name="mixing",
    )(image_index[:, None], image_index[None, :], queries, key_rows, values)


def mixing_grads_kernel(width, rows, ids_down_ref, ids_ref, summary_ref, q_ref, k_ref, v_ref, d_ref, dq_ref, dk_ref, dv_ref):
    step = pl.program_id(0)
    pack = q_ref.shape[1] // width
    scale = width ** (-0.5)
    keys = [half_of(k_ref[...], half, width) for half in range(pack)]
    values = [half_of(v_ref[...], half, width) for half in range(pack)]
    key_sums, value_sums = 0.0, 0.0
    for start in range(0, q_ref.shape[0], rows):
        here = pl.ds(start, rows)
        same = ids_down_ref[...] == ids_ref[:, here]
        query_sum = 0.0
        for half in range(pack):
            queries, d_mixed = half_of(q_ref[here], half, width), half_of(d_ref[here], half, width)
            scores = contract_cols(keys[half], queries) * scale
            summary = summary_ref[pl.ds(step * pack + half, 1), here]
            probs = jnp.where(same, jnp.exp(jnp.where(same, scores - summary, -1e30)), 0.0)
            d_probs = contract_cols(values[half], d_mixed)
            product = probs * d_probs
            d_scores = product - probs * jnp.sum(product, axis=0, keepdims=True)
            d_scores = d_scores.astype(jnp.bfloat16)
            value_sums = value_sums + low_dot(probs.astype(jnp.bfloat16), d_mixed)
            key_sums = key_sums + low_dot(d_scores, queries)
            query_sum = query_sum + contract_rows(d_scores, keys[half])
        dq_ref[here] = (query_sum * scale).astype(dq_ref.dtype)
    dk_ref[...] = (key_sums * scale).astype(dk_ref.dtype)
    dv_ref[...] = value_sums.astype(dv_ref.dtype)


def mixing_grads(queries, key_rows, values, d_mixed, summary, image_index, heads, rows=256):
    token_count, model_width = queries.shape
    width = model_width // heads
    pack = 128 // width
    tile = pl.BlockSpec((token_count, 128), lambda step: (0, step))

    def whole(shape):
        return pl.BlockSpec(shape, lambda step: (0, 0))

    return pl.pallas_call(
        functools.partial(mixing_grads_kernel, width, rows),
        grid=(heads // pack,),
        out_shape=(jax.ShapeDtypeStruct((token_count, model_width), jnp.bfloat16),) * 3,
        in_specs=[whole((token_count, 1)), whole((1, token_count)), whole(summary.shape)] + [tile] * 4,
        out_specs=(tile,) * 3,
        compiler_params=pltpu.CompilerParams(vmem_limit_bytes=32 * 1024 * 1024),
        cost_estimate=pl.CostEstimate(
            flops=10 * token_count * token_count * model_width,
            bytes_accessed=14 * token_count * model_width,
            transcendentals=heads * token_count * token_count,
        ),
        name="mixing_grads",
    )(image_index[:, None], image_index[None, :], summary, queries, key_rows, values, d_mixed)


IN_VMEM = pl.BlockSpec(memory_space=pltpu.VMEM)
IN_SMEM = pl.BlockSpec(memory_space=pltpu.SMEM)


def hidden_forward_kernel(rows, normed_ref, middle_ref, bias_ref, out_bias_ref, *refs):
    part_refs = refs[:4]
    final_ref, active_ref, slope_ref = refs[4:]
    width = normed_ref.shape[1]

    def block(step, carry):
        here = pl.ds(pl.multiple_of(step * rows, rows), rows)
        normed = normed_ref[here]
        total = middle_ref[here] + out_bias_ref[...]
        for index, part_ref in enumerate(part_refs):
            hidden = contract_cols(normed, part_ref[:, :width]) + bias_ref[pl.ds(index, 1)]
            active, slope = gelu_with_slope(hidden)
            active = active.astype(jnp.bfloat16)
            active_ref[index, here] = active
            slope_ref[index, here] = slope
            total = total + low_dot(active, part_ref[:, width:])
        final_ref[here] = total
        return carry

    lax.fori_loop(0, normed_ref.shape[0] // rows, block, 0)


def hidden_forward(normed, middle, bias, out_bias, parts, rows=256):
    token_count, width = normed.shape
    return pl.pallas_call(
        functools.partial(hidden_forward_kernel, rows),
        out_shape=(
            jax.ShapeDtypeStruct((token_count, width), jnp.float32),
            jax.ShapeDtypeStruct((4, token_count, width), jnp.bfloat16),
            jax.ShapeDtypeStruct((4, token_count, width), jnp.float32),
        ),
        in_specs=[IN_VMEM] * 8,
        out_specs=(IN_VMEM,) * 3,
        compiler_params=pltpu.CompilerParams(vmem_limit_bytes=48 * 1024 * 1024),
        cost_estimate=pl.CostEstimate(
            flops=16 * token_count * width * width,
            bytes_accessed=16 * width * width + 32 * token_count * width,
            transcendentals=8 * token_count * width,
        ),
        name="hidden_forward",
    )(normed, middle, bias, out_bias, *parts)


def hidden_back_kernel(core_ref, d_out_ref, normed_ref, active_ref, slope_ref, *refs):
    part_refs = refs[:4]
    d_hidden_ref, bias_ref, away_ref = refs[4:]
    width = d_out_ref.shape[1]
    first = core_ref[0, 0] == 0
    right = jnp.where(first, d_out_ref[...], normed_ref[...])
    for index, part_ref in enumerate(part_refs):
        d_active = contract_cols(d_out_ref[...], part_ref[:, width:])
        d_hidden = (slope_ref[index] * d_active).astype(jnp.bfloat16)
        d_hidden_ref[index] = d_hidden
        bias_ref[pl.ds(index, 1)] = jnp.sum(d_hidden.astype(jnp.float32), axis=0, keepdims=True)
        left = jnp.where(first, active_ref[index], d_hidden)
        away_ref[index] = contract_rows(left, right).astype(jnp.bfloat16)


def hidden_back(core, d_out, normed, active, slope, parts):
    token_count, width = d_out.shape
    return pl.pallas_call(
        hidden_back_kernel,
        out_shape=(
            jax.ShapeDtypeStruct((4, token_count, width), jnp.bfloat16),
            jax.ShapeDtypeStruct((4, width), jnp.float32),
            jax.ShapeDtypeStruct((4, width, width), jnp.bfloat16),
        ),
        in_specs=[IN_SMEM] + [IN_VMEM] * 8,
        out_specs=(IN_VMEM,) * 3,
        compiler_params=pltpu.CompilerParams(vmem_limit_bytes=48 * 1024 * 1024),
        cost_estimate=pl.CostEstimate(
            flops=16 * token_count * width * width,
            bytes_accessed=16 * width * width + 32 * token_count * width,
            transcendentals=0,
        ),
        name="hidden_back",
    )(core.reshape(1, 1), d_out, normed, active, slope, *parts)


def kept_grads_kernel(core_ref, d_out_ref, normed_ref, active_ref, d_hidden_ref, *refs):
    part_refs = refs[:4]
    d_normed_ref, kept_ref = refs[4:]
    width = d_out_ref.shape[1]
    first = core_ref[0, 0] == 0
    right = jnp.where(first, normed_ref[...], d_out_ref[...])
    total = None
    for index, part_ref in enumerate(part_refs):
        d_hidden = d_hidden_ref[index]
        term = low_dot(d_hidden, part_ref[:, :width])
        total = term if total is None else total + term
        left = jnp.where(first, d_hidden, active_ref[index])
        kept_ref[index] = contract_rows(left, right)
    d_normed_ref[...] = total


def kept_grads(core, d_out, normed, active, d_hidden, parts):
    token_count, width = d_out.shape
    return pl.pallas_call(
        kept_grads_kernel,
        out_shape=(
            jax.ShapeDtypeStruct((token_count, width), jnp.float32),
            jax.ShapeDtypeStruct((4, width, width), jnp.float32),
        ),
        in_specs=[IN_SMEM] + [IN_VMEM] * 8,
        out_specs=(IN_VMEM,) * 2,
        compiler_params=pltpu.CompilerParams(vmem_limit_bytes=48 * 1024 * 1024),
        cost_estimate=pl.CostEstimate(
            flops=16 * token_count * width * width,
            bytes_accessed=32 * width * width + 20 * token_count * width,
            transcendentals=0,
        ),
        name="kept_grads",
    )(core.reshape(1, 1), d_out, normed, active, d_hidden, *parts)


def orthogonal_kernel(part_count, chunk, full_steps, row_count, factor_ref, *refs):
    moment_refs, grad_refs = refs[:part_count], refs[part_count : 2 * part_count]
    out_ref, rows_ref, gram_ref, low_ref, change_ref = refs[2 * part_count :]
    part_rows, width = moment_refs[0].shape
    factor = factor_ref[0, 0]
    chunks = part_rows // chunk
    bf = jnp.bfloat16

    gram_ref[...] = jnp.zeros_like(gram_ref)
    for index in range(part_count):

        def start(step, carry, index=index):
            here = pl.ds(pl.multiple_of(step * chunk, chunk), chunk)
            rows = (
                momentum_keep * moment_refs[index][here].astype(jnp.float32)
                + factor * grad_refs[index][here].astype(jnp.float32)
            ).astype(bf)
            rows_ref[pl.ds(pl.multiple_of(index * part_rows + step * chunk, chunk), chunk)] = rows
            gram_ref[...] += contract_rows(rows, rows)
            return carry

        lax.fori_loop(0, chunks, start, 0)
    gram = gram_ref[...]
    diagonal = lax.broadcasted_iota(jnp.int32, gram.shape, 0) == lax.broadcasted_iota(
        jnp.int32, gram.shape, 1
    )
    trace = jnp.sum(jnp.where(diagonal, gram, 0.0))
    inverse = 1.0 / (jnp.sqrt(jnp.full((1, 1), trace)) + 1e-07)
    gram_ref[...] = gram * (inverse * inverse)
    for step in range(5):
        low_ref[...] = gram_ref[...].astype(bf)
        change_ref[...] = (
            newton_two * gram_ref[...] + newton_three * low_dot(low_ref[...], low_ref[...])
        ).astype(bf)
        if step < full_steps:
            scale = inverse if step == 0 else jnp.ones((1, 1), jnp.float32)
            last = step == full_steps - 1
            if step < 4:
                gram_ref[...] = jnp.zeros_like(gram_ref)

            def advance(index, carry, step=step, scale=scale, last=last):
                here = pl.ds(pl.multiple_of(index * chunk, chunk), chunk)
                old = rows_ref[here]
                new = scale * (newton_one * old.astype(jnp.float32) + low_dot(old, change_ref[...]))
                if last:
                    @pl.when(index == 0)
                    def _():
                        out_ref[...] = new[:row_count]
                new = new.astype(bf)
                if not last:
                    rows_ref[here] = new
                gram_ref[...] += contract_rows(new, new)
                return carry

            lax.fori_loop(0, part_count * chunks, advance, 0)
        else:
            rows = out_ref[...]
            out_ref[...] = newton_one * rows + low_dot(rows.astype(bf), change_ref[...])
            if step < 4:
                gram_ref[...] = newton_one * gram_ref[...] + low_dot(low_ref[...], change_ref[...])
                low_ref[...] = gram_ref[...].astype(bf)
                gram_ref[...] = newton_one * gram_ref[...] + low_dot(low_ref[...], change_ref[...])

def orthogonal_rows(moments, grads, factor, row_count, chunk, full_steps):
    count, (part_rows, width) = len(moments), moments[0].shape
    body = functools.partial(orthogonal_kernel, count, chunk, full_steps, row_count)
    flops = 2 * width * width * (count * part_rows * (2 * full_steps + 1) + 9 * width)
    return pl.pallas_call(
        body,
        out_shape=jax.ShapeDtypeStruct((row_count, width), jnp.float32),
        in_specs=[pl.BlockSpec(memory_space=pltpu.SMEM)]
        + [pl.BlockSpec(memory_space=pltpu.VMEM)] * (2 * count),
        out_specs=pl.BlockSpec(memory_space=pltpu.VMEM),
        scratch_shapes=[
            pltpu.VMEM((count * part_rows, width), jnp.bfloat16),
            pltpu.VMEM((width, width), jnp.float32),
            pltpu.VMEM((width, width), jnp.bfloat16),
            pltpu.VMEM((width, width), jnp.bfloat16),
        ],
        compiler_params=pltpu.CompilerParams(vmem_limit_bytes=48 * 1024 * 1024),
        cost_estimate=pl.CostEstimate(flops=flops, bytes_accessed=4 * count * part_rows * width, transcendentals=0),
        name="orthogonal_rows",
    )(factor.reshape(1, 1), *moments, *grads)


def adam_step(weight, first_moment, second_moment, gradient, step_rate):
    first_moment = adam_first * first_moment + (1.0 - adam_first) * gradient
    second_moment = adam_second * second_moment + (1.0 - adam_second) * gradient * gradient
    first_hat = first_moment / (1.0 - adam_first**STEP)
    second_hat = second_moment / (1.0 - adam_second**STEP)
    weight = weight * (1.0 - step_rate * decay_rate) - step_rate * first_hat / (
        jnp.sqrt(second_hat) + 1e-08
    )
    return (weight, first_moment, second_moment)


def on_device(
    patches,
    image_ids,
    patch_place,
    labels,
    attn_w,
    mlp_w,
    embed_w,
    vec_w,
    head_w,
    attn_mom,
    mlp_mom,
    embed_m,
    embed_v,
    vec_m,
    vec_v,
    head_m,
    head_v,
):
    groups = lax.axis_size("cls")
    owners = lax.axis_size("dp")
    count = groups * owners
    top = count.bit_length() - 1
    low_bits = groups.bit_length() - 1
    member_index = lax.axis_index("cls")
    owner_index = lax.axis_index("dp")
    me = owner_index * groups + member_index
    core = me & 1
    model_width = vec_w.shape[1]
    slot_count = labels.shape[1]
    high_bits = list(range(top - 1, 2, -1))
    third, fourth, pair = (2, 4), (4, 2), (1, 1)
    third_mine = jnp.where(core == 0, third[0], third[1])
    fourth_mine = jnp.where(core == 0, fourth[0], fourth[1])

    def exchange(value, masks, what="small"):
        with jax.named_scope(what):
            return swap(value, count, masks)

    def plain(bit):
        return (1 << bit,) * 2

    def bit_of(bit):
        return (me >> bit) & 1

    def lane(steps, what):
        return Lane(steps, exchange, what)

    def of_core(value):
        left, right = value[:, :model_width], value[:, model_width:]
        return jnp.where(core == 0, left, right), jnp.where(core == 0, right, left)

    attn_rows, embed_rows, mlp_rows = attn_w.shape[0], embed_w.shape[0], mlp_w.shape[0]
    up_stages = [plain(bit) for bit in high_bits]
    down_stages = up_stages[::-1]

    def ordered_weights(block):
        for axis, bit in enumerate(high_bits):
            block = ordered_pair(bit_of(bit), block, (yield block, plain(bit)), axis)
        block = block.reshape(-1, attn_rows + embed_rows, model_width)
        block = jnp.stack([block, (yield block, third)])
        block = jnp.concatenate([block, (yield block, fourth)], axis=0)
        return block, (yield block, pair)

    sibling = me ^ 1
    places = [
        me,
        me ^ third_mine,
        me ^ fourth_mine,
        me ^ 6,
        sibling,
        sibling ^ fourth_mine,
        sibling ^ third_mine,
        sibling ^ 6,
    ]
    attn_lane = lane(
        ordered_weights(jnp.concatenate([attn_w, embed_w], axis=0).astype(jnp.bfloat16)),
        "attn_weights",
    )
    mlp_lane = lane(
        collecting(mlp_w.astype(jnp.bfloat16)[None], up_stages + [third]), "mlp_weights"
    )
    for _ in high_bits:
        sync((), attn_lane)
    sync((), attn_lane, mlp_lane)
    sync((), attn_lane, mlp_lane)

    shard_rows, shard_width = head_w.shape
    chunk = -(-shard_width // (owners * 128)) * 128
    padding = owners * chunk - shard_width
    owner_bits = list(range(low_bits, top))

    def transposed(value, order):
        value = value.reshape((2,) * len(owner_bits) + value.shape[1:])
        for bit in order:
            axis = top - 1 - bit
            mine = bit_of(bit)
            stay, leave = pick(value, mine, axis), pick(value, 1 - mine, axis)
            value = ordered_pair(mine, stay, (yield leave, plain(bit)), axis)
        return value.reshape((owners,) + value.shape[len(owner_bits) :])

    head_low = jnp.pad(head_w.astype(jnp.bfloat16), ((0, 0), (0, padding)))
    head_low = head_low.reshape(shard_rows, owners, chunk).transpose(1, 0, 2)
    head_lane = lane(transposed(head_low, owner_bits[1:] + owner_bits[:1]), "head")

    def of_chip():
        value = mlp_mom.astype(jnp.bfloat16)
        mine, leave = of_core(value)
        rows = jnp.stack([mine, (yield leave, pair)])
        return (yield from collecting(rows, up_stages + [third, fourth]))

    mom_lane = lane(of_chip(), "mlp_moments")
    attn_mom_lane = lane(
        collecting(attn_mom.astype(jnp.bfloat16)[None], up_stages[2:] + [third, fourth, pair]),
        "attn_moments",
    )
    sync((), attn_lane, mlp_lane, head_lane)
    pieces, others = finish(attn_lane)[0]
    attn_b = jnp.zeros((count // 8, 8, attn_rows, model_width), jnp.bfloat16)
    embed_b = jnp.zeros((count // 8, 8, embed_rows, model_width), jnp.bfloat16)
    for index, place in enumerate(places):
        piece = (pieces if index < 4 else others)[index % 4]
        attn_b = lax.dynamic_update_slice_in_dim(attn_b, piece[:, None, :attn_rows], place & 7, 1)
        embed_b = lax.dynamic_update_slice_in_dim(embed_b, piece[:, None, attn_rows:], place & 7, 1)
    attn_b = attn_b.reshape(count * attn_rows, model_width)
    embed_b = embed_b.reshape(count * embed_rows, model_width)

    attn_b, embed_b = sync((attn_b, embed_b), mlp_lane, head_lane)
    part_a = jnp.concatenate(finish(mlp_lane)[0], axis=0)

    def once(value, stage):
        return (yield value, stage)

    b_lane = lane(once(part_a, fourth), "mlp_weights")
    c_lane = lane(once(part_a, pair), "mlp_weights")
    sync((), b_lane)
    sync((), c_lane)
    image_index = lax.dynamic_index_in_dim(image_ids, member_index, 0, keepdims=False)
    my_labels = lax.dynamic_index_in_dim(labels, member_index, 0, keepdims=False)
    position = patch_place[0]
    patch_dim = patches.shape[1]
    grid_size = (embed_b.shape[0] - patch_dim) // 2
    grid_index = jnp.arange(grid_size)
    places_hot = [(position[axis][:, None] == grid_index[None]).astype(jnp.bfloat16) for axis in (0, 1)]
    patch_wide = jnp.concatenate([patches] + places_hot, axis=1)
    embedded = low_dot(patch_wide, embed_b) + vec_w[10]
    normed, queries, key_rows, values = projections(attn_b, vec_w, embedded)
    queries, key_rows, values = sync((queries, key_rows, values), mom_lane)
    mixed_out, summary = mixing(queries, key_rows, values, image_index, H)
    (mixed_out,) = sync((mixed_out,), b_lane, c_lane, mom_lane, head_lane)
    part_b, part_c = b_lane.result, c_lane.result
    d_lane = lane(once(part_b, pair), "mlp_weights")
    sync((), d_lane)

    masks = [1 << bit for bit in high_bits]
    own_codes = [jnp.array(codes(masks + [third[c], fourth[c]]), jnp.int32) for c in (0, 1)]
    arrival = me ^ jnp.where(
        core == 0,
        jnp.concatenate([own_codes[0], own_codes[1] ^ 1]),
        jnp.concatenate([own_codes[1], own_codes[0] ^ 1]),
    )
    first_bias = jnp.take(vec_w[11:].reshape(count, mlp_rows), arrival, axis=0)
    first_bias = first_bias.reshape(4, -1)

    middle = embedded + low_dot(mixed_out, attn_b[3 * model_width :]) + vec_w[2]
    normed_two = layer_norm(middle, vec_w[6], vec_w[7]).astype(jnp.bfloat16)
    (normed_two,) = sync((normed_two,), d_lane)
    mlp_parts = [
        part.reshape(-1, 2 * model_width) for part in (part_a, part_b, part_c, d_lane.result)
    ]
    final_rows, active, slope = hidden_forward(
        normed_two, middle, first_bias, vec_w[3:4], mlp_parts
    )
    (final_rows,) = sync((final_rows,), head_lane, mom_lane, attn_mom_lane)
    closing, close_pull = jax.vjp(layer_norm, final_rows, vec_w[8], vec_w[9])
    member = (image_index[None, :] == jnp.arange(slot_count)[:, None]).astype(jnp.float32)
    slot_sizes = jnp.sum(member, axis=1)
    divisor = jnp.maximum(slot_sizes, 1.0)[:, None]
    pooled = product(member, closing) / divisor
    facts = jnp.stack(
        [(slot_sizes > 0.5).astype(jnp.int32), my_labels // 256, my_labels % 256], axis=1
    )
    facts = jnp.pad(facts, ((0, 0), (0, 125))).astype(jnp.bfloat16)
    block = jnp.concatenate([pooled.astype(jnp.bfloat16), facts], axis=1)
    head_b = finish(head_lane)[0].reshape(owners * shard_rows, chunk)
    for axis, bit in enumerate(range(top - 1, -1, -1)):
        block = ordered_pair(bit_of(bit), block, exchange(block, plain(bit), "pooled"), axis)
    block = block.reshape(count * slot_count, -1)
    all_pooled = block[:, :model_width]
    facts = block[:, model_width : model_width + 3].astype(jnp.int32)
    valid = facts[:, 0] > 0
    all_labels = facts[:, 1] * 256 + facts[:, 2]
    image_total = jnp.sum(valid.astype(jnp.float32))

    (all_pooled,) = sync((all_pooled,), mom_lane, attn_mom_lane)
    logits = low_dot(all_pooled, head_b)
    within = owner_index * chunk + jnp.arange(chunk)
    columns = member_index * shard_width + within
    usable = (within < shard_width) & (columns < CLASSES)
    logits = jnp.where(usable[None], logits, -1e30)
    onehot = (usable[None] & (columns[None, :] == all_labels[:, None])).astype(jnp.float32)
    row_max = jnp.max(logits, axis=1)
    exp_sums = jnp.sum(jnp.exp(logits - row_max[:, None]), axis=1)
    stats = jnp.stack([row_max, exp_sums, jnp.sum(onehot * logits, axis=1)])
    for bit in range(top):
        other = exchange(stats, plain(bit), "stats")
        lower = jnp.where(bit_of(bit) == 0, stats, other)
        upper = jnp.where(bit_of(bit) == 0, other, stats)
        row_max = jnp.maximum(lower[0], upper[0])
        exp_sums = lower[1] * jnp.exp(lower[0] - row_max) + upper[1] * jnp.exp(upper[0] - row_max)
        stats = jnp.stack([row_max, exp_sums, lower[2] + upper[2]])
    (stats,) = sync((stats,), mom_lane, attn_mom_lane)
    normaliser = stats[0] + jnp.log(stats[1])
    loss_sum = jnp.sum(jnp.where(valid, normaliser - stats[2], 0.0))
    probs_class = jnp.exp(logits - normaliser[:, None])
    d_logits = (jnp.where(valid[:, None], probs_class - onehot, 0.0) / image_total).astype(
        jnp.bfloat16
    )
    d_pooled = contract_cols(d_logits, head_b)
    d_pooled = d_pooled.reshape((2,) * top + (slot_count, model_width))
    for bit in range(top):
        axis = top - 1 - bit
        mine = bit_of(bit)
        leave = pick(d_pooled, 1 - mine, axis).astype(jnp.bfloat16)
        d_pooled = pick(d_pooled, mine, axis) + exchange(leave, plain(bit), "d_pooled").astype(
            jnp.float32
        )
    d_closing = product(member.T, d_pooled / divisor)
    d_final, g_gain_final, g_shift_final = close_pull(d_closing)
    d_out = d_final.astype(jnp.bfloat16)
    g_second_bias = jnp.sum(d_out.astype(jnp.float32), axis=0)
    d_out, all_pooled = tie(d_out, all_pooled)
    head_grad = contract_rows(all_pooled, d_logits).astype(jnp.bfloat16)
    head_lane = lane(
        transposed(
            head_grad.reshape(owners, shard_rows, chunk),
            owner_bits[1:-1] + owner_bits[:1] + owner_bits[-1:],
        ),
        "head_grads",
    )
    (d_out,) = sync((d_out,), head_lane, mom_lane, attn_mom_lane)
    mlp_moms, attn_moms = finish(mom_lane, attn_mom_lane)
    mlp_moms = [part.reshape(-1, model_width) for part in mlp_moms]
    attn_moms = jnp.concatenate(attn_moms, axis=0).reshape(-1, model_width)

    d_hidden, bias_grads, away = hidden_back(core, d_out, normed_two, active, slope, mlp_parts)
    (away, d_hidden) = sync((away, d_hidden), head_lane)
    arrived = exchange(away, pair, "mlp_grads")
    d_normed_two, kept = kept_grads(core, d_out, normed_two, active, d_hidden, mlp_parts)
    d_normed_two, kept, arrived = sync((d_normed_two, kept, arrived), head_lane)
    kept = [
        (kept[index] + arrived[(index + 2) % 4].astype(jnp.float32)).reshape(
            -1, mlp_rows, model_width
        )
        for index in range(4)
    ]

    def summing(kept):
        half = kept[0].shape[0] // 2
        leave = [kept[1], kept[2][half:], kept[3][half:]]
        leave = jnp.concatenate([grad.astype(jnp.bfloat16) for grad in leave])
        arrived = (yield leave, fourth).astype(jnp.float32)
        leave = [kept[0][half:] + arrived[half : 2 * half], kept[3][:half] + arrived[3 * half :]]
        kept = [kept[0][:half] + arrived[:half], kept[2][:half] + arrived[2 * half : 3 * half]]
        arrived = yield jnp.stack(leave).astype(jnp.bfloat16), third
        kept = jnp.stack(kept) + arrived.astype(jnp.float32)
        for stage in down_stages:
            half = kept.shape[1] // 2
            arrived = yield kept[:, half:].astype(jnp.bfloat16), stage
            kept = kept[:, :half] + arrived.astype(jnp.float32)
        return kept[:, 0]

    mlp_lane = lane(summing(kept), "mlp_grads")
    (d_normed_two,) = sync((d_normed_two,), mlp_lane)

    d_mid_norm, g_gain_two, g_shift_two = jax.vjp(layer_norm, middle, vec_w[6], vec_w[7])[1](
        d_normed_two
    )
    d_middle = d_final + d_mid_norm
    d_proj = d_middle.astype(jnp.bfloat16)
    g_out_bias = jnp.sum(d_proj.astype(jnp.float32), axis=0)
    d_mixed = contract_cols(d_proj, attn_b[3 * model_width :]).astype(jnp.bfloat16)
    d_queries, d_keys, d_values = mixing_grads(
        queries, key_rows, values, d_mixed, summary, image_index, H
    )
    d_queries, d_keys, d_values = sync((d_queries, d_keys, d_values), mlp_lane, head_lane)
    attn_grad = jnp.concatenate(
        [
            contract_rows(normed, d_queries),
            contract_rows(normed, d_keys),
            contract_rows(normed, d_values),
            contract_rows(mixed_out, d_proj),
        ],
        axis=0,
    )

    quarter = (me >> 1) & 3
    to_third, to_fourth = third_mine >> 1, fourth_mine >> 1

    def quartered(grad, rows):
        grad = grad.reshape(count // 8, 4, 2, rows, model_width)
        leave = pick(grad, 1 - core, 2).astype(jnp.bfloat16)
        grad = pick(grad, core, 2) + (yield leave, pair).astype(jnp.float32)
        leave = [pick(grad, quarter ^ to_fourth, 1), pick(grad, quarter ^ 3, 1)]
        leave = (yield jnp.stack(leave).astype(jnp.bfloat16), fourth).astype(jnp.float32)
        leaving = pick(grad, quarter ^ to_third, 1) + leave[1]
        return pick(grad, quarter, 1) + leave[0], leaving

    def last_sums(grads):
        grad = jnp.concatenate([one[0] for one in grads], axis=1)
        leave = jnp.concatenate([one[1].astype(jnp.bfloat16) for one in grads], axis=1)
        grad = grad + (yield leave, third).astype(jnp.float32)
        grad = grad.reshape((2,) * len(high_bits) + grad.shape[1:])
        for bit in reversed(high_bits):
            axis = top - 1 - bit
            mine = bit_of(bit)
            leave = pick(grad, 1 - mine, axis).astype(jnp.bfloat16)
            grad = pick(grad, mine, axis) + (yield leave, plain(bit)).astype(jnp.float32)
        return grad

    attn_lane = lane(quartered(attn_grad, attn_rows), "attn_grads")
    d_normed = (
        contract_cols(d_queries, attn_b[:model_width])
        + contract_cols(d_keys, attn_b[model_width : 2 * model_width])
        + contract_cols(d_values, attn_b[2 * model_width : 3 * model_width])
    )
    (d_normed,) = sync((d_normed,), mlp_lane, attn_lane)
    d_emb_norm, g_gain_one, g_shift_one = jax.vjp(layer_norm, embedded, vec_w[4], vec_w[5])[1](
        d_normed
    )
    d_embed_low = (d_middle + d_emb_norm).astype(jnp.bfloat16)
    (d_embed_low,) = sync((d_embed_low,), attn_lane)
    embed_grad = contract_rows(patch_wide, d_embed_low)
    embed_lane = lane(quartered(embed_grad, embed_rows), "embed_grads")
    sync((), embed_lane)
    sync((), mlp_lane)
    mlp_grad = finish(mlp_lane)[0]
    all_lane = lane(
        collecting(mlp_grad.astype(jnp.bfloat16), up_stages + [third, fourth]), "mlp_grads_all"
    )
    sync((), all_lane)
    sync((), embed_lane)
    finish(attn_lane, embed_lane)
    sum_lane = lane(last_sums([attn_lane.result, embed_lane.result]), "last_grads")
    sync((), sum_lane)
    while sum_lane.result is None:
        sync((), sum_lane, all_lane)
    attn_sum, embed_sum = sum_lane.result[:attn_rows], sum_lane.result[attn_rows:]
    g_query_bias = jnp.sum(d_queries.astype(jnp.float32), axis=0)
    g_value_bias = jnp.sum(d_values.astype(jnp.float32), axis=0)
    g_patch_bias = jnp.sum(d_embed_low.astype(jnp.float32), axis=0)
    g_first_bias = jnp.take(bias_grads.reshape(count, mlp_rows), jnp.argsort(arrival), axis=0)
    head_grad = finish(head_lane)[0].transpose(1, 0, 2)
    head_grad = head_grad.reshape(shard_rows, owners * chunk)[:, :shard_width].astype(jnp.float32)
    vec_grad = jnp.concatenate(
        [
            jnp.stack(
                [
                    g_query_bias,
                    g_value_bias,
                    g_out_bias,
                    g_second_bias,
                    g_gain_one,
                    g_shift_one,
                    g_gain_two,
                    g_shift_two,
                    g_gain_final,
                    g_shift_final,
                    g_patch_bias,
                ]
            ),
            g_first_bias.reshape(-1, model_width),
        ],
        axis=0,
    )
    local_squares = sum(
        jnp.sum(grad * grad, axis=0) for grad in (attn_sum, embed_sum, mlp_grad[0], mlp_grad[1])
    )
    head_squares = jnp.sum(head_grad * head_grad) / model_width
    small_sums = jnp.concatenate([vec_grad, (local_squares + head_squares)[None]], axis=0)

    def total(value):
        for bit in range(top):
            value = value + (yield value, plain(bit))
        return value

    small_lane = lane(total(small_sums), "small_sums")
    block_lane = lane(
        collecting(attn_sum.astype(jnp.bfloat16)[None], up_stages[2:] + [third, fourth, pair]),
        "attn_grads_all",
    )
    small_sums, attn_grads, mlp_grads = finish(small_lane, block_lane, all_lane)
    attn_grads = jnp.concatenate(attn_grads, axis=0).reshape(-1, model_width)
    mlp_grads = [part.reshape(-1, model_width) for part in mlp_grads]
    vec_sum = small_sums[:-1]
    grad_norm = jnp.sqrt(jnp.sum(small_sums[-1]) + jnp.sum(vec_sum * vec_sum))
    factor = jnp.minimum(1.0, clip_limit / (grad_norm + 1e-06))
    attn_mom_out = momentum_keep * attn_mom + factor * attn_sum
    mine, away = mlp_grad[0], exchange(mlp_grad[1], pair)
    mlp_sum = jnp.concatenate(
        [jnp.where(core == 0, mine, away), jnp.where(core == 0, away, mine)], axis=1
    )
    mlp_mom_out = momentum_keep * mlp_mom + factor * mlp_sum

    mlp_result = orthogonal_rows(mlp_moms, mlp_grads, factor, 2 * mlp_rows, 768, 2)
    mlp_other = exchange(mlp_result[mlp_rows:], pair)
    mlp_result = mlp_result[:mlp_rows]
    mlp_dir = jnp.concatenate(
        [
            jnp.where(core == 0, mlp_result, mlp_other),
            jnp.where(core == 0, mlp_other, mlp_result),
        ],
        axis=1,
    )
    attn_dir = orthogonal_rows([attn_moms], [attn_grads], factor, attn_rows, 768, 4)
    mlp_scale = math.sqrt(mlp_rows * count / model_width)
    attn_out = attn_w * (1.0 - muon_rate * decay_rate) - muon_rate * attn_dir
    mlp_out = mlp_w * (1.0 - muon_rate * decay_rate) - muon_rate * mlp_scale * mlp_dir
    embed_out, embed_m_out, embed_v_out = adam_step(
        embed_w, embed_m, embed_v, factor * embed_sum, adam_rate
    )
    vec_out, vec_m_out, vec_v_out = adam_step(vec_w, vec_m, vec_v, factor * vec_sum, vector_rate)
    head_out, head_m_out, head_v_out = adam_step(
        head_w, head_m, head_v, factor * head_grad, adam_rate
    )
    return (
        loss_sum,
        image_total,
        grad_norm,
        attn_out,
        attn_mom_out,
        attn_out.astype(jnp.bfloat16),
        mlp_out,
        mlp_mom_out,
        mlp_out.astype(jnp.bfloat16),
        embed_out,
        embed_m_out,
        embed_v_out,
        embed_out.astype(jnp.bfloat16),
        vec_out,
        vec_m_out,
        vec_v_out,
        vec_out.astype(jnp.bfloat16),
        head_out,
        head_m_out,
        head_v_out,
        head_out.astype(jnp.bfloat16),
    )


def solution(mesh):
    return jax.shard_map(
        on_device,
        mesh=mesh,
        in_specs=(
            P(("dp", "cls"), None),
            P("dp", None),
            P(("dp", "cls"), None, None),
            P("dp", None),
            P(("dp", "cls"), None),
            P(("dp", "cls"), None),
            P(("dp", "cls"), None),
            P(),
            P("dp", "cls"),
            P(("dp", "cls"), None),
            P(("dp", "cls"), None),
            P(("dp", "cls"), None),
            P(("dp", "cls"), None),
            P(),
            P(),
            P("dp", "cls"),
            P("dp", "cls"),
        ),
        out_specs=(
            P(),
            P(),
            P(),
            P(("dp", "cls"), None),
            P(("dp", "cls"), None),
            P(("dp", "cls"), None),
            P(("dp", "cls"), None),
            P(("dp", "cls"), None),
            P(("dp", "cls"), None),
            P(("dp", "cls"), None),
            P(("dp", "cls"), None),
            P(("dp", "cls"), None),
            P(("dp", "cls"), None),
            P(),
            P(),
            P(),
            P(),
            P("dp", "cls"),
            P("dp", "cls"),
            P("dp", "cls"),
            P("dp", "cls"),
        ),
        check_vma=False,
    )
```

```python
import functools
import math

import jax
import jax.numpy as jnp
from jax import lax
from jax.experimental import pallas as pl
from jax.experimental.pallas import tpu as pltpu
from jax.sharding import PartitionSpec as P

H = 12
CLASSES = 21843
STEP = 10


highest = lax.Precision.HIGHEST
newton_one = 3.4445
newton_two = -4.775
newton_three = 2.0315
clip_limit = 0.05
muon_rate = 0.3
decay_rate = 0.05
adam_rate = 0.01
vector_rate = 0.05
momentum_keep = 0.5
adam_first = 0.5
adam_second = 0.999


AXES = ("dp", "cls")


def swap(value, count, masks):
    return lax.ppermute(value, AXES, [(i, i ^ masks[i & 1]) for i in range(count)])


def pick(value, index, axis):
    return lax.dynamic_index_in_dim(value, index, axis, keepdims=False)


def codes(masks):
    found = [0]
    for mask in masks:
        found = found + [code ^ mask for code in found]
    return found


def ordered_pair(bit, mine, other, axis):
    return jnp.where(
        bit == 0, jnp.stack([mine, other], axis=axis), jnp.stack([other, mine], axis=axis)
    )


def product(left_side, right_side):
    return jnp.dot(left_side, right_side, precision=highest)


def low_dot(left_side, right_side):
    return jnp.dot(left_side, right_side, preferred_element_type=jnp.float32)


def contract_rows(left_side, right_side):
    return lax.dot_general(
        left_side, right_side, (((0,), (0,)), ((), ())), preferred_element_type=jnp.float32
    )


def contract_cols(left_side, right_side):
    return lax.dot_general(
        left_side, right_side, (((1,), (1,)), ((), ())), preferred_element_type=jnp.float32
    )


def layer_norm(inputs, gain_row, shift_row):
    mean_row = jnp.mean(inputs, axis=-1, keepdims=True)
    centred = inputs - mean_row
    variance = jnp.mean(centred * centred, axis=-1, keepdims=True)
    return centred * lax.rsqrt(variance + 1e-06) * gain_row + shift_row


def tie(*values):
    return lax.optimization_barrier(values)


class Lane:
    def __init__(self, steps, exchange, what):
        self.steps, self.exchange, self.what = steps, exchange, what
        self.moving, self.result = False, None
        self.value, self.masks = next(steps)

    def advance(self, value, start):
        masks = self.masks
        if self.moving:
            try:
                value, masks = self.steps.send(value)
            except StopIteration as end:
                self.value, self.result, self.moving = None, end.value, False
                return
            if not start:
                self.value, self.masks, self.moving = value, masks, False
                return
        self.moving = True
        self.value, self.masks = self.exchange(value, masks, self.what), masks


def sync(values, *lanes, hold=()):
    lanes = [lane for lane in lanes if lane.result is None]
    tied = tie(*values, *[lane.value for lane in lanes])
    for lane, value in zip(lanes, tied[len(values) :]):
        lane.advance(value, lane not in hold)
    return tied[: len(values)]


def finish(*lanes):
    while any(lane.result is None for lane in lanes):
        sync((), *lanes)
    return [lane.result for lane in lanes]


def collecting(value, stages):
    for stage in stages[:-1]:
        value = jnp.concatenate([value, (yield value, stage)], axis=0)
    return [value, (yield value, stages[-1])]


def gelu_with_slope(value):
    size = jnp.abs(value)
    bell = jnp.exp(-0.5 * value * value)
    t = 1.0 / (1.0 + (0.3275911 * 0.7071067811865476) * size)
    poly = 1.061405429
    for term in (-1.453152027, 1.421413741, -0.284496736, 0.254829592):
        poly = poly * t + term
    tail = 0.5 * poly * t * bell
    share = jnp.where(value < 0, tail, 1.0 - tail)
    return value * share, share + value * (0.3989422804014327 * bell)


def projections(attn_b, vec_w, embedded):
    model_width = attn_b.shape[1]
    normed = layer_norm(embedded, vec_w[4], vec_w[5]).astype(jnp.bfloat16)
    queries = (low_dot(normed, attn_b[:model_width]) + vec_w[0]).astype(jnp.bfloat16)
    key_rows = low_dot(normed, attn_b[model_width : 2 * model_width]).astype(jnp.bfloat16)
    values = (low_dot(normed, attn_b[2 * model_width : 3 * model_width]) + vec_w[1]).astype(
        jnp.bfloat16
    )
    return (normed, queries, key_rows, values)


def half_of(value, half, width):
    lane = lax.broadcasted_iota(jnp.int32, value.shape, 1)
    keep = (lane >= half * width) & (lane < (half + 1) * width)
    return jnp.where(keep, value, jnp.zeros_like(value))


def mixing_kernel(width, rows, ids_down_ref, ids_ref, q_ref, k_ref, v_ref, out_ref, summary_ref, seen_ref):
    step = pl.program_id(0)
    pack = q_ref.shape[1] // width
    keys = [half_of(k_ref[...], half, width) for half in range(pack)]
    values = [half_of(v_ref[...], half, width) for half in range(pack)]
    scale = width ** (-0.5)
    lane = lax.broadcasted_iota(jnp.int32, (rows, seen_ref.shape[1]), 1)
    for start in range(0, q_ref.shape[0], rows):
        here = pl.ds(start, rows)
        same = ids_down_ref[here] == ids_ref[...]
        queries = q_ref[here]
        seen = seen_ref[here]
        total = None
        for half in range(pack):
            scores = jnp.where(same, contract_cols(queries, keys[half]) * scale, -1e30)
            top = jnp.max(scores, axis=1, keepdims=True)
            exponents = jnp.exp(scores - top)
            sums = jnp.sum(exponents, axis=1, keepdims=True)
            probs = (exponents * (1.0 / sums)).astype(jnp.bfloat16)
            mixed = low_dot(probs, values[half])
            total = mixed if total is None else total + mixed
            seen = jnp.where(lane == step * pack + half, top + jnp.log(sums), seen)
        out_ref[here] = total.astype(out_ref.dtype)
        seen_ref[here] = seen

    @pl.when(step == pl.num_programs(0) - 1)
    def _():
        summary_ref[...] = seen_ref[...].T[: summary_ref.shape[0]]


def mixing(queries, key_rows, values, image_index, heads, rows=256):
    token_count, model_width = queries.shape
    width = model_width // heads
    pack = 128 // width
    tile = pl.BlockSpec((token_count, 128), lambda step: (0, step))

    def whole(shape):
        return pl.BlockSpec(shape, lambda step: (0, 0))

    kept = -(-heads // 8) * 8
    return pl.pallas_call(
        functools.partial(mixing_kernel, width, rows),
        grid=(heads // pack,),
        out_shape=(
            jax.ShapeDtypeStruct((token_count, model_width), jnp.bfloat16),
            jax.ShapeDtypeStruct((kept, token_count), jnp.float32),
        ),
        in_specs=[whole((token_count, 1)), whole((1, token_count)), tile, tile, tile],
        out_specs=(tile, whole((kept, token_count))),
        scratch_shapes=[pltpu.VMEM((token_count, 128), jnp.float32)],
        compiler_params=pltpu.CompilerParams(vmem_limit_bytes=32 * 1024 * 1024),
        cost_estimate=pl.CostEstimate(
            flops=4 * token_count * token_count * model_width,
            bytes_accessed=8 * token_count * model_width,
            transcendentals=heads * token_count * token_count,
        ),
        name="mixing",
    )(image_index[:, None], image_index[None, :], queries, key_rows, values)


def mixing_grads_kernel(width, rows, ids_down_ref, ids_ref, summary_ref, q_ref, k_ref, v_ref, d_ref, dq_ref, dk_ref, dv_ref):
    step = pl.program_id(0)
    pack = q_ref.shape[1] // width
    scale = width ** (-0.5)
    keys = [half_of(k_ref[...], half, width) for half in range(pack)]
    values = [half_of(v_ref[...], half, width) for half in range(pack)]
    key_sums, value_sums = 0.0, 0.0
    for start in range(0, q_ref.shape[0], rows):
        here = pl.ds(start, rows)
        same = ids_down_ref[...] == ids_ref[:, here]
        query_sum = 0.0
        for half in range(pack):
            queries, d_mixed = half_of(q_ref[here], half, width), half_of(d_ref[here], half, width)
            scores = contract_cols(keys[half], queries) * scale
            summary = summary_ref[pl.ds(step * pack + half, 1), here]
            probs = jnp.where(same, jnp.exp(jnp.where(same, scores - summary, -1e30)), 0.0)
            d_probs = contract_cols(values[half], d_mixed)
            product = probs * d_probs
            d_scores = product - probs * jnp.sum(product, axis=0, keepdims=True)
            d_scores = d_scores.astype(jnp.bfloat16)
            value_sums = value_sums + low_dot(probs.astype(jnp.bfloat16), d_mixed)
            key_sums = key_sums + low_dot(d_scores, queries)
            query_sum = query_sum + contract_rows(d_scores, keys[half])
        dq_ref[here] = (query_sum * scale).astype(dq_ref.dtype)
    dk_ref[...] = (key_sums * scale).astype(dk_ref.dtype)
    dv_ref[...] = value_sums.astype(dv_ref.dtype)


def mixing_grads(queries, key_rows, values, d_mixed, summary, image_index, heads, rows=256):
    token_count, model_width = queries.shape
    width = model_width // heads
    pack = 128 // width
    tile = pl.BlockSpec((token_count, 128), lambda step: (0, step))

    def whole(shape):
        return pl.BlockSpec(shape, lambda step: (0, 0))

    return pl.pallas_call(
        functools.partial(mixing_grads_kernel, width, rows),
        grid=(heads // pack,),
        out_shape=(jax.ShapeDtypeStruct((token_count, model_width), jnp.bfloat16),) * 3,
        in_specs=[whole((token_count, 1)), whole((1, token_count)), whole(summary.shape)] + [tile] * 4,
        out_specs=(tile,) * 3,
        compiler_params=pltpu.CompilerParams(vmem_limit_bytes=32 * 1024 * 1024),
        cost_estimate=pl.CostEstimate(
            flops=10 * token_count * token_count * model_width,
            bytes_accessed=14 * token_count * model_width,
            transcendentals=heads * token_count * token_count,
        ),
        name="mixing_grads",
    )(image_index[:, None], image_index[None, :], summary, queries, key_rows, values, d_mixed)


IN_VMEM = pl.BlockSpec(memory_space=pltpu.VMEM)
IN_SMEM = pl.BlockSpec(memory_space=pltpu.SMEM)


def hidden_forward_kernel(rows, normed_ref, middle_ref, bias_ref, *refs):
    part_refs = refs[:-3]
    final_ref, active_ref, slope_ref = refs[-3:]
    width = normed_ref.shape[1]

    def block(step, carry):
        here = pl.ds(pl.multiple_of(step * rows, rows), rows)
        normed = normed_ref[here]
        total = middle_ref[here]
        for index, part_ref in enumerate(part_refs):
            hidden = contract_cols(normed, part_ref[:, :width]) + bias_ref[pl.ds(index, 1)]
            active, slope = gelu_with_slope(hidden)
            active = active.astype(jnp.bfloat16)
            active_ref[index, here] = active
            slope_ref[index, here] = slope
            total = total + low_dot(active, part_ref[:, width:])
        final_ref[here] = total
        return carry

    lax.fori_loop(0, normed_ref.shape[0] // rows, block, 0)


def hidden_forward(normed, middle, bias, parts, rows=256):
    token_count, width = normed.shape
    count = len(parts)
    return pl.pallas_call(
        functools.partial(hidden_forward_kernel, rows),
        out_shape=(
            jax.ShapeDtypeStruct((token_count, width), jnp.float32),
            jax.ShapeDtypeStruct((count, token_count, width), jnp.bfloat16),
            jax.ShapeDtypeStruct((count, token_count, width), jnp.float32),
        ),
        in_specs=[IN_VMEM] * (3 + count),
        out_specs=(IN_VMEM,) * 3,
        compiler_params=pltpu.CompilerParams(vmem_limit_bytes=48 * 1024 * 1024),
        cost_estimate=pl.CostEstimate(
            flops=4 * count * token_count * width * width,
            bytes_accessed=4 * count * width * width + 8 * count * token_count * width,
            transcendentals=2 * count * token_count * width,
        ),
        name="hidden_forward",
    )(normed, middle, bias, *parts)


def hidden_back_kernel(core_ref, d_out_ref, normed_ref, *refs):
    active_refs, slope_refs, part_refs = refs[:2], refs[2:4], refs[4:8]
    d_hidden_ref, bias_ref, away_ref = refs[8:]
    width = d_out_ref.shape[1]
    half = width // 2
    first = core_ref[0, 0] == 0
    right = jnp.where(first, d_out_ref[...], normed_ref[...])
    slots = ((7, 3), (5, 1), (6, 4), (2, 0))
    for index, part_ref in enumerate(part_refs):
        d_active = contract_cols(d_out_ref[...], part_ref[:, width:])
        slope = slope_refs[index % 2][index // 2]
        d_hidden = (slope * d_active).astype(jnp.bfloat16)
        d_hidden_ref[index] = d_hidden
        bias_ref[pl.ds(index, 1)] = jnp.sum(d_hidden.astype(jnp.float32), axis=0, keepdims=True)
        left = jnp.where(first, active_refs[index % 2][index // 2], d_hidden)
        grad = contract_rows(left, right).astype(jnp.bfloat16)
        for side, slot in enumerate(slots[index]):
            away_ref[pl.ds(slot * half, half)] = grad[side * half : (side + 1) * half]


def hidden_back(core, d_out, normed, active, slope, parts):
    token_count, width = d_out.shape
    return pl.pallas_call(
        hidden_back_kernel,
        out_shape=(
            jax.ShapeDtypeStruct((4, token_count, width), jnp.bfloat16),
            jax.ShapeDtypeStruct((4, width), jnp.float32),
            jax.ShapeDtypeStruct((4 * width, width), jnp.bfloat16),
        ),
        in_specs=[IN_SMEM] + [IN_VMEM] * 10,
        out_specs=(IN_VMEM,) * 3,
        compiler_params=pltpu.CompilerParams(vmem_limit_bytes=48 * 1024 * 1024),
        cost_estimate=pl.CostEstimate(
            flops=16 * token_count * width * width,
            bytes_accessed=16 * width * width + 32 * token_count * width,
            transcendentals=0,
        ),
        name="hidden_back",
    )(core.reshape(1, 1), d_out, normed, *active, *slope, *parts)


def kept_grads_kernel(plan, core_ref, d_out_ref, normed_ref, even_ref, odd_ref, d_hidden_ref, *refs):
    kept_ref = refs[-1]
    active_refs = (even_ref, odd_ref)
    width = d_out_ref.shape[1]
    half = width // 2
    first = core_ref[0, 0] == 0
    right = jnp.where(first, normed_ref[...], d_out_ref[...])
    for index, side, slot in plan:
        columns = slice(None) if side is None else slice(side * half, (side + 1) * half)
        left = jnp.where(
            first,
            d_hidden_ref[index, :, columns],
            active_refs[index % 2][index // 2, :, columns],
        )
        grad = contract_rows(left, right)
        if side is None:
            kept_ref[pl.ds(slot[0] * half, half)] = grad[:half]
            kept_ref[pl.ds(slot[1] * half, half)] = grad[half:]
        else:
            kept_ref[pl.ds(slot * half, half)] = grad
    if len(refs) > 1:
        part_refs, total_ref = refs[:4], refs[4]
        total = low_dot(d_hidden_ref[0], part_refs[0][:, :width])
        for index in range(1, 4):
            total = total + low_dot(d_hidden_ref[index], part_refs[index][:, :width])
        total_ref[...] = total


def kept_grads(plan, core, d_out, normed, active, d_hidden, parts=()):
    token_count, width = d_out.shape
    grads = jax.ShapeDtypeStruct((2 * width, width), jnp.float32)
    back = jax.ShapeDtypeStruct((token_count, width), jnp.float32)
    return pl.pallas_call(
        functools.partial(kept_grads_kernel, plan),
        out_shape=(back, grads) if parts else grads,
        in_specs=[IN_SMEM] + [IN_VMEM] * (5 + len(parts)),
        out_specs=(IN_VMEM,) * 2 if parts else IN_VMEM,
        compiler_params=pltpu.CompilerParams(vmem_limit_bytes=48 * 1024 * 1024),
        cost_estimate=pl.CostEstimate(
            flops=4 * token_count * width * width,
            bytes_accessed=8 * width * width + 20 * token_count * width,
            transcendentals=0,
        ),
        name="kept_grads",
    )(core.reshape(1, 1), d_out, normed, *active, d_hidden, *parts)


def orthogonal_kernel(part_count, chunk, full_steps, row_count, factor_ref, *refs):
    moment_refs, grad_refs = refs[:part_count], refs[part_count : 2 * part_count]
    out_ref, rows_ref, gram_ref, low_ref, change_ref = refs[2 * part_count :]
    part_rows, width = moment_refs[0].shape
    factor = factor_ref[0, 0]
    chunks = part_rows // chunk
    bf = jnp.bfloat16

    gram_ref[...] = jnp.zeros_like(gram_ref)
    for index in range(part_count):

        def start(step, carry, index=index):
            here = pl.ds(pl.multiple_of(step * chunk, chunk), chunk)
            rows = (
                momentum_keep * moment_refs[index][here].astype(jnp.float32)
                + factor * grad_refs[index][here].astype(jnp.float32)
            ).astype(bf)
            if full_steps:
                rows_ref[
                    pl.ds(pl.multiple_of(index * part_rows + step * chunk, chunk), chunk)
                ] = rows
            elif index == 0:

                @pl.when(step == 0)
                def _():
                    out_ref[...] = rows[:row_count].astype(jnp.float32)

            gram_ref[...] += contract_rows(rows, rows)
            return carry

        lax.fori_loop(0, chunks, start, 0)
    gram = gram_ref[...]
    diagonal = lax.broadcasted_iota(jnp.int32, gram.shape, 0) == lax.broadcasted_iota(
        jnp.int32, gram.shape, 1
    )
    trace = jnp.sum(jnp.where(diagonal, gram, 0.0))
    inverse = 1.0 / (jnp.sqrt(jnp.full((1, 1), trace)) + 1e-07)
    gram_ref[...] = gram * (inverse * inverse)
    if not full_steps:
        out_ref[...] = inverse * out_ref[...]
    for step in range(5):
        low_ref[...] = gram_ref[...].astype(bf)
        change_ref[...] = (
            newton_two * gram_ref[...] + newton_three * low_dot(low_ref[...], low_ref[...])
        ).astype(bf)
        if step < full_steps:
            scale = inverse if step == 0 else jnp.ones((1, 1), jnp.float32)
            last = step == full_steps - 1
            if step < 4:
                gram_ref[...] = jnp.zeros_like(gram_ref)

            def advance(index, carry, step=step, scale=scale, last=last):
                here = pl.ds(pl.multiple_of(index * chunk, chunk), chunk)
                old = rows_ref[here]
                new = scale * (newton_one * old.astype(jnp.float32) + low_dot(old, change_ref[...]))
                if last:
                    @pl.when(index == 0)
                    def _():
                        out_ref[...] = new[:row_count]
                new = new.astype(bf)
                if not last:
                    rows_ref[here] = new
                gram_ref[...] += contract_rows(new, new)
                return carry

            lax.fori_loop(0, part_count * chunks, advance, 0)
        else:
            rows = out_ref[...]
            out_ref[...] = newton_one * rows + low_dot(rows.astype(bf), change_ref[...])
            if step < 4:
                gram_ref[...] = newton_one * gram_ref[...] + low_dot(low_ref[...], change_ref[...])
                low_ref[...] = gram_ref[...].astype(bf)
                gram_ref[...] = newton_one * gram_ref[...] + low_dot(low_ref[...], change_ref[...])

def orthogonal_rows(moments, grads, factor, row_count, chunk, full_steps):
    count, (part_rows, width) = len(moments), moments[0].shape
    body = functools.partial(orthogonal_kernel, count, chunk, full_steps, row_count)
    flops = 2 * width * width * (count * part_rows * (2 * full_steps + 1) + 9 * width)
    return pl.pallas_call(
        body,
        out_shape=jax.ShapeDtypeStruct((row_count, width), jnp.float32),
        in_specs=[pl.BlockSpec(memory_space=pltpu.SMEM)]
        + [pl.BlockSpec(memory_space=pltpu.VMEM)] * (2 * count),
        out_specs=pl.BlockSpec(memory_space=pltpu.VMEM),
        scratch_shapes=[
            pltpu.VMEM((count * part_rows if full_steps else 16, width), jnp.bfloat16),
            pltpu.VMEM((width, width), jnp.float32),
            pltpu.VMEM((width, width), jnp.bfloat16),
            pltpu.VMEM((width, width), jnp.bfloat16),
        ],
        compiler_params=pltpu.CompilerParams(vmem_limit_bytes=48 * 1024 * 1024),
        cost_estimate=pl.CostEstimate(flops=flops, bytes_accessed=4 * count * part_rows * width, transcendentals=0),
        name="orthogonal_rows",
    )(factor.reshape(1, 1), *moments, *grads)


def adam_step(weight, first_moment, second_moment, gradient, step_rate):
    first_moment = adam_first * first_moment + (1.0 - adam_first) * gradient
    second_moment = adam_second * second_moment + (1.0 - adam_second) * gradient * gradient
    first_hat = first_moment / (1.0 - adam_first**STEP)
    second_hat = second_moment / (1.0 - adam_second**STEP)
    weight = weight * (1.0 - step_rate * decay_rate) - step_rate * first_hat / (
        jnp.sqrt(second_hat) + 1e-08
    )
    return (weight, first_moment, second_moment)


def on_device(
    patches,
    image_ids,
    patch_place,
    labels,
    attn_w,
    mlp_w,
    embed_w,
    vec_w,
    head_w,
    attn_mom,
    mlp_mom,
    embed_m,
    embed_v,
    vec_m,
    vec_v,
    head_m,
    head_v,
):
    groups = lax.axis_size("cls")
    owners = lax.axis_size("dp")
    count = groups * owners
    top = count.bit_length() - 1
    low_bits = groups.bit_length() - 1
    member_index = lax.axis_index("cls")
    owner_index = lax.axis_index("dp")
    me = owner_index * groups + member_index
    core = me & 1
    model_width = vec_w.shape[1]
    slot_count = labels.shape[1]
    high_bits = list(range(top - 1, 2, -1))
    third, fourth, pair = (2, 4), (4, 2), (1, 1)
    third_mine = jnp.where(core == 0, third[0], third[1])
    fourth_mine = jnp.where(core == 0, fourth[0], fourth[1])

    def exchange(value, masks, what="small"):
        with jax.named_scope(what):
            return swap(value, count, masks)

    def plain(bit):
        return (1 << bit,) * 2

    def bit_of(bit):
        return (me >> bit) & 1

    def lane(steps, what):
        return Lane(steps, exchange, what)

    def of_core(value):
        left, right = value[:, :model_width], value[:, model_width:]
        return jnp.where(core == 0, left, right), jnp.where(core == 0, right, left)

    attn_rows, embed_rows, mlp_rows = attn_w.shape[0], embed_w.shape[0], mlp_w.shape[0]
    up_stages = [plain(bit) for bit in high_bits]
    down_stages = up_stages[::-1]

    def ordered_weights(block):
        for axis, bit in enumerate(high_bits):
            block = ordered_pair(bit_of(bit), block, (yield block, plain(bit)), axis)
        block = block.reshape(-1, attn_rows + embed_rows, model_width)
        block = jnp.stack([block, (yield block, third)])
        block = jnp.concatenate([block, (yield block, fourth)], axis=0)
        return block, (yield block, pair)

    sibling = me ^ 1
    places = [
        me,
        me ^ third_mine,
        me ^ fourth_mine,
        me ^ 6,
        sibling,
        sibling ^ fourth_mine,
        sibling ^ third_mine,
        sibling ^ 6,
    ]
    attn_lane = lane(
        ordered_weights(jnp.concatenate([attn_w, embed_w], axis=0).astype(jnp.bfloat16)),
        "attn_weights",
    )
    mlp_lane = lane(
        collecting(mlp_w.astype(jnp.bfloat16)[None], up_stages + [third]), "mlp_weights"
    )
    for _ in high_bits:
        sync((), attn_lane)
    sync((), attn_lane, mlp_lane)
    sync((), attn_lane, mlp_lane)

    shard_rows, shard_width = head_w.shape
    chunk = -(-shard_width // (owners * 128)) * 128
    padding = owners * chunk - shard_width
    owner_bits = list(range(low_bits, top))

    def transposed(value, order):
        value = value.reshape((2,) * len(owner_bits) + value.shape[1:])
        for bit in order:
            axis = top - 1 - bit
            mine = bit_of(bit)
            stay, leave = pick(value, mine, axis), pick(value, 1 - mine, axis)
            value = ordered_pair(mine, stay, (yield leave, plain(bit)), axis)
        return value.reshape((owners,) + value.shape[len(owner_bits) :])

    head_low = jnp.pad(head_w.astype(jnp.bfloat16), ((0, 0), (0, padding)))
    head_low = head_low.reshape(shard_rows, owners, chunk).transpose(1, 0, 2)
    head_lane = lane(transposed(head_low, owner_bits[1:] + owner_bits[:1]), "head")

    def of_chip():
        value = mlp_mom.astype(jnp.bfloat16)
        mine, leave = of_core(value)
        rows = jnp.stack([mine, (yield leave, pair)])
        return (yield from collecting(rows, up_stages + [third, fourth]))

    mom_lane = lane(of_chip(), "mlp_moments")
    attn_mom_lane = lane(
        collecting(attn_mom.astype(jnp.bfloat16)[None], up_stages[2:] + [third, fourth, pair]),
        "attn_moments",
    )
    sync((), attn_lane, mlp_lane, head_lane)
    pieces, others = finish(attn_lane)[0]
    attn_b = jnp.zeros((count // 8, 8, attn_rows, model_width), jnp.bfloat16)
    embed_b = jnp.zeros((count // 8, 8, embed_rows, model_width), jnp.bfloat16)
    for index, place in enumerate(places):
        piece = (pieces if index < 4 else others)[index % 4]
        attn_b = lax.dynamic_update_slice_in_dim(attn_b, piece[:, None, :attn_rows], place & 7, 1)
        embed_b = lax.dynamic_update_slice_in_dim(embed_b, piece[:, None, attn_rows:], place & 7, 1)
    attn_b = attn_b.reshape(count * attn_rows, model_width)
    embed_b = embed_b.reshape(count * embed_rows, model_width)

    attn_b, embed_b = sync((attn_b, embed_b), mlp_lane, head_lane)
    part_a = jnp.concatenate(finish(mlp_lane)[0], axis=0)

    def once(value, stage):
        return (yield value, stage)

    b_lane = lane(once(part_a, fourth), "mlp_weights")
    c_lane = lane(once(part_a, pair), "mlp_weights")
    sync((), b_lane)
    sync((), c_lane)
    image_index = lax.dynamic_index_in_dim(image_ids, member_index, 0, keepdims=False)
    my_labels = lax.dynamic_index_in_dim(labels, member_index, 0, keepdims=False)
    position = patch_place[0]
    patch_dim = patches.shape[1]
    grid_size = (embed_b.shape[0] - patch_dim) // 2
    grid_index = jnp.arange(grid_size)
    places_hot = [(position[axis][:, None] == grid_index[None]).astype(jnp.bfloat16) for axis in (0, 1)]
    patch_wide = jnp.concatenate([patches] + places_hot, axis=1)
    embedded = low_dot(patch_wide, embed_b) + vec_w[10]
    normed, queries, key_rows, values = projections(attn_b, vec_w, embedded)
    mixed_out, summary = mixing(queries, key_rows, values, image_index, H)
    (mixed_out,) = sync((mixed_out,), c_lane, mom_lane)
    part_c = c_lane.result

    masks = [1 << bit for bit in high_bits]
    own_codes = [jnp.array(codes(masks + [third[c], fourth[c]]), jnp.int32) for c in (0, 1)]
    arrival = me ^ jnp.where(
        core == 0,
        jnp.concatenate([own_codes[0], own_codes[1] ^ 1]),
        jnp.concatenate([own_codes[1], own_codes[0] ^ 1]),
    )
    first_bias = jnp.take(vec_w[11:].reshape(count, mlp_rows), arrival, axis=0)
    first_bias = first_bias.reshape(4, -1)

    middle = embedded + low_dot(mixed_out, attn_b[3 * model_width :]) + vec_w[2]
    normed_two = layer_norm(middle, vec_w[6], vec_w[7]).astype(jnp.bfloat16)
    final_rows, active_even, slope_even = hidden_forward(
        normed_two, middle + vec_w[3], first_bias[::2], [part_a.reshape(-1, 2 * model_width), part_c.reshape(-1, 2 * model_width)]
    )
    final_rows, slope_even = sync((final_rows, slope_even), b_lane, head_lane)
    part_b = b_lane.result
    d_lane = lane(once(part_b, pair), "mlp_weights")
    sync((), d_lane)
    (final_rows,) = sync((final_rows,), d_lane, mom_lane, attn_mom_lane)
    mlp_parts = [
        part.reshape(-1, 2 * model_width) for part in (part_a, part_b, part_c, d_lane.result)
    ]
    final_rows, active_odd, slope_odd = hidden_forward(
        normed_two, final_rows, first_bias[1::2], mlp_parts[1::2]
    )
    active, slope = (active_even, active_odd), (slope_even, slope_odd)
    (final_rows,) = sync(
        (final_rows,), head_lane, mom_lane, attn_mom_lane, hold=(mom_lane, attn_mom_lane)
    )
    closing, close_pull = jax.vjp(layer_norm, final_rows, vec_w[8], vec_w[9])
    member = (image_index[None, :] == jnp.arange(slot_count)[:, None]).astype(jnp.float32)
    slot_sizes = jnp.sum(member, axis=1)
    divisor = jnp.maximum(slot_sizes, 1.0)[:, None]
    pooled = product(member, closing) / divisor
    facts = jnp.stack(
        [(slot_sizes > 0.5).astype(jnp.int32), my_labels // 256, my_labels % 256], axis=1
    )
    facts = jnp.pad(facts, ((0, 0), (0, 125))).astype(jnp.bfloat16)
    block = jnp.concatenate([pooled.astype(jnp.bfloat16), facts], axis=1)
    head_b = finish(head_lane)[0].reshape(owners * shard_rows, chunk)
    for axis, bit in enumerate(range(top - 1, -1, -1)):
        block = ordered_pair(bit_of(bit), block, exchange(block, plain(bit), "pooled"), axis)
    block = block.reshape(count * slot_count, -1)
    all_pooled = block[:, :model_width]
    facts = block[:, model_width : model_width + 3].astype(jnp.int32)
    valid = facts[:, 0] > 0
    all_labels = facts[:, 1] * 256 + facts[:, 2]
    image_total = jnp.sum(valid.astype(jnp.float32))

    logits = low_dot(all_pooled, head_b)
    within = owner_index * chunk + jnp.arange(chunk)
    columns = member_index * shard_width + within
    usable = (within < shard_width) & (columns < CLASSES)
    logits = jnp.where(usable[None], logits, -1e30)
    onehot = (usable[None] & (columns[None, :] == all_labels[:, None])).astype(jnp.float32)
    row_max = jnp.max(logits, axis=1)
    exp_sums = jnp.sum(jnp.exp(logits - row_max[:, None]), axis=1)
    stats = jnp.stack([row_max, exp_sums, jnp.sum(onehot * logits, axis=1)])
    for bit in range(top):
        other = exchange(stats, plain(bit), "stats")
        lower = jnp.where(bit_of(bit) == 0, stats, other)
        upper = jnp.where(bit_of(bit) == 0, other, stats)
        row_max = jnp.maximum(lower[0], upper[0])
        exp_sums = lower[1] * jnp.exp(lower[0] - row_max) + upper[1] * jnp.exp(upper[0] - row_max)
        stats = jnp.stack([row_max, exp_sums, lower[2] + upper[2]])
    normaliser = stats[0] + jnp.log(stats[1])
    loss_sum = jnp.sum(jnp.where(valid, normaliser - stats[2], 0.0))
    probs_class = jnp.exp(logits - normaliser[:, None])
    d_logits = (jnp.where(valid[:, None], probs_class - onehot, 0.0) / image_total).astype(
        jnp.bfloat16
    )
    d_pooled = contract_cols(d_logits, head_b)
    d_pooled = d_pooled.reshape((2,) * top + (slot_count, model_width))
    for bit in range(top):
        axis = top - 1 - bit
        mine = bit_of(bit)
        leave = pick(d_pooled, 1 - mine, axis).astype(jnp.bfloat16)
        d_pooled = pick(d_pooled, mine, axis) + exchange(leave, plain(bit), "d_pooled").astype(
            jnp.float32
        )
    d_closing = product(member.T, d_pooled / divisor)
    d_final, g_gain_final, g_shift_final = close_pull(d_closing)
    d_out = d_final.astype(jnp.bfloat16)
    g_second_bias = jnp.sum(d_out.astype(jnp.float32), axis=0)
    d_out, all_pooled = tie(d_out, all_pooled)
    head_grad = contract_rows(all_pooled, d_logits)
    head_squares = jnp.sum(head_grad * head_grad) / model_width
    head_lane = lane(
        transposed(
            head_grad.astype(jnp.bfloat16).reshape(owners, shard_rows, chunk),
            owner_bits[1:] + owner_bits[:1],
        ),
        "head_grads",
    )
    (d_out,) = sync((d_out,), mom_lane, attn_mom_lane)

    d_hidden, bias_grads, away = hidden_back(core, d_out, normed_two, active, slope, mlp_parts)
    (away, d_hidden) = sync((away, d_hidden), mom_lane, attn_mom_lane)
    arrived = exchange(away, pair, "mlp_grads")
    operands = (core, d_out, normed_two, active, d_hidden)
    leave = kept_grads(((1, None, (2, 0)), (3, 1, 1), (2, 1, 3)), *operands)
    leave, arrived, d_hidden = sync(
        (leave, arrived, d_hidden), mom_lane, attn_mom_lane, hold=(mom_lane,)
    )
    operands = (core, d_out, normed_two, active, d_hidden)
    half = 2 * model_width
    leave = (leave + arrived[:half].astype(jnp.float32)).astype(jnp.bfloat16)

    def summing(leave, kept, arrived):
        far = yield leave, fourth
        summed = kept() + arrived.astype(jnp.float32) + far.astype(jnp.float32)
        arrived = yield summed[:model_width].astype(jnp.bfloat16), third
        kept = summed[model_width:] + arrived.astype(jnp.float32)
        kept = kept.reshape(2, -1, mlp_rows, model_width)
        for stage in down_stages:
            half = kept.shape[1] // 2
            arrived = yield kept[:, half:].astype(jnp.bfloat16), stage
            kept = kept[:, :half] + arrived.astype(jnp.float32)
        return kept[:, 0]

    own = []
    mlp_lane = lane(summing(leave, lambda: own[0], arrived[half:]), "mlp_grads")
    sync((), mlp_lane)
    d_normed_two, grads = kept_grads(
        ((0, None, (2, 0)), (3, 0, 1), (2, 0, 3)), *operands, mlp_parts
    )
    own.append(grads)
    (d_normed_two,) = sync((d_normed_two,), head_lane)

    d_mid_norm, g_gain_two, g_shift_two = jax.vjp(layer_norm, middle, vec_w[6], vec_w[7])[1](
        d_normed_two
    )
    d_middle = d_final + d_mid_norm
    d_proj = d_middle.astype(jnp.bfloat16)
    g_out_bias = jnp.sum(d_proj.astype(jnp.float32), axis=0)
    d_mixed = contract_cols(d_proj, attn_b[3 * model_width :]).astype(jnp.bfloat16)
    d_queries, d_keys, d_values = mixing_grads(
        queries, key_rows, values, d_mixed, summary, image_index, H
    )
    d_queries, d_keys, d_values, own[0] = sync(
        (d_queries, d_keys, d_values, own[0]),
        mlp_lane,
        head_lane,
        hold=(head_lane,),
    )
    attn_grad = jnp.concatenate(
        [
            contract_rows(normed, d_queries),
            contract_rows(normed, d_keys),
            contract_rows(normed, d_values),
            contract_rows(mixed_out, d_proj),
        ],
        axis=0,
    )

    quarter = (me >> 1) & 3
    to_third, to_fourth = third_mine >> 1, fourth_mine >> 1

    def quartered(grad, rows):
        grad = grad.reshape(count // 8, 4, 2, rows, model_width)
        leave = pick(grad, 1 - core, 2).astype(jnp.bfloat16)
        grad = pick(grad, core, 2) + (yield leave, pair).astype(jnp.float32)
        leave = [pick(grad, quarter ^ to_fourth, 1), pick(grad, quarter ^ 3, 1)]
        leave = (yield jnp.stack(leave).astype(jnp.bfloat16), fourth).astype(jnp.float32)
        leaving = pick(grad, quarter ^ to_third, 1) + leave[1]
        return pick(grad, quarter, 1) + leave[0], leaving

    def last_sums(grads):
        grad = jnp.concatenate([one[0] for one in grads], axis=1)
        leave = jnp.concatenate([one[1].astype(jnp.bfloat16) for one in grads], axis=1)
        grad = grad + (yield leave, third).astype(jnp.float32)
        grad = grad.reshape((2,) * len(high_bits) + grad.shape[1:])
        for bit in reversed(high_bits):
            axis = top - 1 - bit
            mine = bit_of(bit)
            leave = pick(grad, 1 - mine, axis).astype(jnp.bfloat16)
            grad = pick(grad, mine, axis) + (yield leave, plain(bit)).astype(jnp.float32)
        return grad

    attn_lane = lane(quartered(attn_grad, attn_rows), "attn_grads")
    d_normed = (
        contract_cols(d_queries, attn_b[:model_width])
        + contract_cols(d_keys, attn_b[model_width : 2 * model_width])
        + contract_cols(d_values, attn_b[2 * model_width : 3 * model_width])
    )
    sync((), attn_lane)
    (d_normed,) = sync((d_normed,), mlp_lane, attn_lane)
    d_emb_norm, g_gain_one, g_shift_one = jax.vjp(layer_norm, embedded, vec_w[4], vec_w[5])[1](
        d_normed
    )
    d_embed_low = (d_middle + d_emb_norm).astype(jnp.bfloat16)
    embed_grad = contract_rows(patch_wide, d_embed_low)
    embed_lane = lane(quartered(embed_grad, embed_rows), "embed_grads")
    sync((), embed_lane)
    sync((), embed_lane, mlp_lane)
    finish(attn_lane, embed_lane)
    sum_lane = lane(last_sums([attn_lane.result, embed_lane.result]), "last_grads")
    sync((), sum_lane)
    mlp_grad = finish(mlp_lane)[0]
    all_lane = lane(
        collecting(mlp_grad.astype(jnp.bfloat16), up_stages + [third, fourth]), "mlp_grads_all"
    )
    sync((), all_lane, mom_lane)
    sync((), sum_lane, all_lane)
    sync((), sum_lane, all_lane, mom_lane)
    while sum_lane.result is None:
        sync((), sum_lane, all_lane)
    attn_sum, embed_sum = sum_lane.result[:attn_rows], sum_lane.result[attn_rows:]
    g_query_bias = jnp.sum(d_queries.astype(jnp.float32), axis=0)
    g_value_bias = jnp.sum(d_values.astype(jnp.float32), axis=0)
    g_patch_bias = jnp.sum(d_embed_low.astype(jnp.float32), axis=0)
    g_first_bias = jnp.take(bias_grads.reshape(count, mlp_rows), jnp.argsort(arrival), axis=0)
    vec_grad = jnp.concatenate(
        [
            jnp.stack(
                [
                    g_query_bias,
                    g_value_bias,
                    g_out_bias,
                    g_second_bias,
                    g_gain_one,
                    g_shift_one,
                    g_gain_two,
                    g_shift_two,
                    g_gain_final,
                    g_shift_final,
                    g_patch_bias,
                ]
            ),
            g_first_bias.reshape(-1, model_width),
        ],
        axis=0,
    )
    local_squares = sum(
        jnp.sum(grad * grad, axis=0) for grad in (attn_sum, embed_sum, mlp_grad[0], mlp_grad[1])
    )
    small_sums = jnp.concatenate([vec_grad, (local_squares + head_squares)[None]], axis=0)

    def total(value):
        for bit in range(top):
            value = value + (yield value, plain(bit))
        return value

    small_lane = lane(total(small_sums), "small_sums")
    block_lane = lane(
        collecting(attn_sum.astype(jnp.bfloat16)[None], up_stages[2:] + [third, fourth, pair]),
        "attn_grads_all",
    )
    sync((), small_lane, block_lane)
    small_sums, attn_grads = finish(small_lane, block_lane)
    attn_moms = jnp.concatenate(finish(attn_mom_lane)[0], axis=0).reshape(-1, model_width)
    attn_grads = jnp.concatenate(attn_grads, axis=0).reshape(-1, model_width)
    vec_sum = small_sums[:-1]
    grad_norm = jnp.sqrt(jnp.sum(small_sums[-1]) + jnp.sum(vec_sum * vec_sum))
    factor = jnp.minimum(1.0, clip_limit / (grad_norm + 1e-06))
    attn_mom_out = momentum_keep * attn_mom + factor * attn_sum
    mine, away = mlp_grad[0], exchange(mlp_grad[1], pair)
    mlp_sum = jnp.concatenate(
        [jnp.where(core == 0, mine, away), jnp.where(core == 0, away, mine)], axis=1
    )
    mlp_mom_out = momentum_keep * mlp_mom + factor * mlp_sum

    (factor,) = sync((factor,), head_lane)
    attn_dir = orthogonal_rows([attn_moms], [attn_grads], factor, attn_rows, 768, 4)
    (attn_dir,) = sync((attn_dir,), all_lane, mom_lane, head_lane)
    mlp_grads, mlp_moms = finish(all_lane, mom_lane)
    mlp_result = orthogonal_rows(
        [part.reshape(-1, model_width) for part in mlp_moms],
        [part.reshape(-1, model_width) for part in mlp_grads],
        factor,
        2 * mlp_rows,
        768,
        0,
    )
    (mlp_result,) = sync((mlp_result,), head_lane)
    mlp_other = exchange(mlp_result[mlp_rows:], pair)
    mlp_result = mlp_result[:mlp_rows]
    mlp_dir = jnp.concatenate(
        [
            jnp.where(core == 0, mlp_result, mlp_other),
            jnp.where(core == 0, mlp_other, mlp_result),
        ],
        axis=1,
    )
    head_grad = finish(head_lane)[0].transpose(1, 0, 2)
    head_grad = head_grad.reshape(shard_rows, owners * chunk)[:, :shard_width].astype(jnp.float32)
    mlp_scale = math.sqrt(mlp_rows * count / model_width)
    attn_out = attn_w * (1.0 - muon_rate * decay_rate) - muon_rate * attn_dir
    mlp_out = mlp_w * (1.0 - muon_rate * decay_rate) - muon_rate * mlp_scale * mlp_dir
    embed_out, embed_m_out, embed_v_out = adam_step(
        embed_w, embed_m, embed_v, factor * embed_sum, adam_rate
    )
    vec_out, vec_m_out, vec_v_out = adam_step(vec_w, vec_m, vec_v, factor * vec_sum, vector_rate)
    head_out, head_m_out, head_v_out = adam_step(
        head_w, head_m, head_v, factor * head_grad, adam_rate
    )
    return (
        loss_sum,
        image_total,
        grad_norm,
        attn_out,
        attn_mom_out,
        attn_out.astype(jnp.bfloat16),
        mlp_out,
        mlp_mom_out,
        mlp_out.astype(jnp.bfloat16),
        embed_out,
        embed_m_out,
        embed_v_out,
        embed_out.astype(jnp.bfloat16),
        vec_out,
        vec_m_out,
        vec_v_out,
        vec_out.astype(jnp.bfloat16),
        head_out,
        head_m_out,
        head_v_out,
        head_out.astype(jnp.bfloat16),
    )


def solution(mesh):
    return jax.shard_map(
        on_device,
        mesh=mesh,
        in_specs=(
            P(("dp", "cls"), None),
            P("dp", None),
            P(("dp", "cls"), None, None),
            P("dp", None),
            P(("dp", "cls"), None),
            P(("dp", "cls"), None),
            P(("dp", "cls"), None),
            P(),
            P("dp", "cls"),
            P(("dp", "cls"), None),
            P(("dp", "cls"), None),
            P(("dp", "cls"), None),
            P(("dp", "cls"), None),
            P(),
            P(),
            P("dp", "cls"),
            P("dp", "cls"),
        ),
        out_specs=(
            P(),
            P(),
            P(),
            P(("dp", "cls"), None),
            P(("dp", "cls"), None),
            P(("dp", "cls"), None),
            P(("dp", "cls"), None),
            P(("dp", "cls"), None),
            P(("dp", "cls"), None),
            P(("dp", "cls"), None),
            P(("dp", "cls"), None),
            P(("dp", "cls"), None),
            P(("dp", "cls"), None),
            P(),
            P(),
            P(),
            P(),
            P("dp", "cls"),
            P("dp", "cls"),
            P("dp", "cls"),
            P("dp", "cls"),
        ),
        check_vma=False,
    )
```

```python
import functools
import math

import jax
import jax.numpy as jnp
from jax import lax
from jax.experimental import pallas as pl
from jax.experimental.pallas import tpu as pltpu
from jax.sharding import PartitionSpec as P

H = 12
CLASSES = 21843
STEP = 10


highest = lax.Precision.HIGHEST
newton_one = 3.4445
newton_two = -4.775
newton_three = 2.0315
clip_limit = 0.05
muon_rate = 0.3
decay_rate = 0.05
adam_rate = 0.01
vector_rate = 0.05
momentum_keep = 0.5
adam_first = 0.5
adam_second = 0.999


AXES = ("dp", "cls")


def swap(value, count, masks):
    return lax.ppermute(value, AXES, [(i, i ^ masks[i & 1]) for i in range(count)])


def pick(value, index, axis):
    return lax.dynamic_index_in_dim(value, index, axis, keepdims=False)


def codes(masks):
    found = [0]
    for mask in masks:
        found = found + [code ^ mask for code in found]
    return found


def ordered_pair(bit, mine, other, axis):
    return jnp.where(
        bit == 0, jnp.stack([mine, other], axis=axis), jnp.stack([other, mine], axis=axis)
    )


def product(left_side, right_side):
    return jnp.dot(left_side, right_side, precision=highest)


def low_dot(left_side, right_side):
    return jnp.dot(left_side, right_side, preferred_element_type=jnp.float32)


def contract_rows(left_side, right_side):
    return lax.dot_general(
        left_side, right_side, (((0,), (0,)), ((), ())), preferred_element_type=jnp.float32
    )


def contract_cols(left_side, right_side):
    return lax.dot_general(
        left_side, right_side, (((1,), (1,)), ((), ())), preferred_element_type=jnp.float32
    )


def layer_norm(inputs, gain_row, shift_row):
    mean_row = jnp.mean(inputs, axis=-1, keepdims=True)
    centred = inputs - mean_row
    variance = jnp.mean(centred * centred, axis=-1, keepdims=True)
    return centred * lax.rsqrt(variance + 1e-06) * gain_row + shift_row


def tie(*values):
    return lax.optimization_barrier(values)


class Lane:
    def __init__(self, steps, exchange, what):
        self.steps, self.exchange, self.what = steps, exchange, what
        self.moving, self.result = False, None
        self.value, self.masks = next(steps)

    def advance(self, value, start):
        masks = self.masks
        if self.moving:
            try:
                value, masks = self.steps.send(value)
            except StopIteration as end:
                self.value, self.result, self.moving = None, end.value, False
                return
            if not start:
                self.value, self.masks, self.moving = value, masks, False
                return
        self.moving = True
        self.value, self.masks = self.exchange(value, masks, self.what), masks


def sync(values, *lanes, hold=()):
    lanes = [lane for lane in lanes if lane.result is None]
    tied = tie(*values, *[lane.value for lane in lanes])
    for lane, value in zip(lanes, tied[len(values) :]):
        lane.advance(value, lane not in hold)
    return tied[: len(values)]


def finish(*lanes):
    while any(lane.result is None for lane in lanes):
        sync((), *lanes)
    return [lane.result for lane in lanes]


def collecting(value, stages):
    for stage in stages[:-1]:
        value = jnp.concatenate([value, (yield value, stage)], axis=0)
    return [value, (yield value, stages[-1])]


def gelu_with_slope(value):
    size = jnp.abs(value)
    bell = jnp.exp(-0.5 * value * value)
    t = 1.0 / (1.0 + (0.3275911 * 0.7071067811865476) * size)
    poly = 1.061405429
    for term in (-1.453152027, 1.421413741, -0.284496736, 0.254829592):
        poly = poly * t + term
    tail = 0.5 * poly * t * bell
    share = jnp.where(value < 0, tail, 1.0 - tail)
    return value * share, share + value * (0.3989422804014327 * bell)


def projections(attn_b, vec_w, embedded):
    model_width = attn_b.shape[1]
    normed = layer_norm(embedded, vec_w[4], vec_w[5]).astype(jnp.bfloat16)
    queries = (low_dot(normed, attn_b[:model_width]) + vec_w[0]).astype(jnp.bfloat16)
    key_rows = low_dot(normed, attn_b[model_width : 2 * model_width]).astype(jnp.bfloat16)
    values = (low_dot(normed, attn_b[2 * model_width : 3 * model_width]) + vec_w[1]).astype(
        jnp.bfloat16
    )
    return (normed, queries, key_rows, values)


def half_of(value, half, width):
    lane = lax.broadcasted_iota(jnp.int32, value.shape, 1)
    keep = (lane >= half * width) & (lane < (half + 1) * width)
    return jnp.where(keep, value, jnp.zeros_like(value))


def mixing_kernel(width, rows, ids_down_ref, ids_ref, q_ref, k_ref, v_ref, out_ref, summary_ref, seen_ref):
    step = pl.program_id(0)
    pack = q_ref.shape[1] // width
    keys = [half_of(k_ref[...], half, width) for half in range(pack)]
    values = [half_of(v_ref[...], half, width) for half in range(pack)]
    scale = width ** (-0.5)
    lane = lax.broadcasted_iota(jnp.int32, (rows, seen_ref.shape[1]), 1)
    for start in range(0, q_ref.shape[0], rows):
        here = pl.ds(start, rows)
        same = ids_down_ref[here] == ids_ref[...]
        queries = q_ref[here]
        seen = seen_ref[here]
        total = None
        for half in range(pack):
            scores = jnp.where(same, contract_cols(queries, keys[half]) * scale, -1e30)
            top = jnp.max(scores, axis=1, keepdims=True)
            exponents = jnp.exp(scores - top)
            sums = jnp.sum(exponents, axis=1, keepdims=True)
            probs = (exponents * (1.0 / sums)).astype(jnp.bfloat16)
            mixed = low_dot(probs, values[half])
            total = mixed if total is None else total + mixed
            seen = jnp.where(lane == step * pack + half, top + jnp.log(sums), seen)
        out_ref[here] = total.astype(out_ref.dtype)
        seen_ref[here] = seen

    @pl.when(step == pl.num_programs(0) - 1)
    def _():
        summary_ref[...] = seen_ref[...].T[: summary_ref.shape[0]]


def mixing(queries, key_rows, values, image_index, heads, rows=256):
    token_count, model_width = queries.shape
    width = model_width // heads
    pack = 128 // width
    tile = pl.BlockSpec((token_count, 128), lambda step: (0, step))

    def whole(shape):
        return pl.BlockSpec(shape, lambda step: (0, 0))

    kept = -(-heads // 8) * 8
    return pl.pallas_call(
        functools.partial(mixing_kernel, width, rows),
        grid=(heads // pack,),
        out_shape=(
            jax.ShapeDtypeStruct((token_count, model_width), jnp.bfloat16),
            jax.ShapeDtypeStruct((kept, token_count), jnp.float32),
        ),
        in_specs=[whole((token_count, 1)), whole((1, token_count)), tile, tile, tile],
        out_specs=(tile, whole((kept, token_count))),
        scratch_shapes=[pltpu.VMEM((token_count, 128), jnp.float32)],
        compiler_params=pltpu.CompilerParams(vmem_limit_bytes=32 * 1024 * 1024),
        cost_estimate=pl.CostEstimate(
            flops=4 * token_count * token_count * model_width,
            bytes_accessed=8 * token_count * model_width,
            transcendentals=heads * token_count * token_count,
        ),
        name="mixing",
    )(image_index[:, None], image_index[None, :], queries, key_rows, values)


def mixing_grads_kernel(width, rows, ids_down_ref, ids_ref, summary_ref, q_ref, k_ref, v_ref, d_ref, dq_ref, dk_ref, dv_ref):
    step = pl.program_id(0)
    pack = q_ref.shape[1] // width
    scale = width ** (-0.5)
    keys = [half_of(k_ref[...], half, width) for half in range(pack)]
    values = [half_of(v_ref[...], half, width) for half in range(pack)]
    key_sums, value_sums = 0.0, 0.0
    for start in range(0, q_ref.shape[0], rows):
        here = pl.ds(start, rows)
        same = ids_down_ref[...] == ids_ref[:, here]
        query_sum = 0.0
        for half in range(pack):
            queries, d_mixed = half_of(q_ref[here], half, width), half_of(d_ref[here], half, width)
            scores = contract_cols(keys[half], queries) * scale
            summary = summary_ref[pl.ds(step * pack + half, 1), here]
            probs = jnp.where(same, jnp.exp(jnp.where(same, scores - summary, -1e30)), 0.0)
            d_probs = contract_cols(values[half], d_mixed)
            product = probs * d_probs
            d_scores = product - probs * jnp.sum(product, axis=0, keepdims=True)
            d_scores = d_scores.astype(jnp.bfloat16)
            value_sums = value_sums + low_dot(probs.astype(jnp.bfloat16), d_mixed)
            key_sums = key_sums + low_dot(d_scores, queries)
            query_sum = query_sum + contract_rows(d_scores, keys[half])
        dq_ref[here] = (query_sum * scale).astype(dq_ref.dtype)
    dk_ref[...] = (key_sums * scale).astype(dk_ref.dtype)
    dv_ref[...] = value_sums.astype(dv_ref.dtype)


def mixing_grads(queries, key_rows, values, d_mixed, summary, image_index, heads, rows=256):
    token_count, model_width = queries.shape
    width = model_width // heads
    pack = 128 // width
    tile = pl.BlockSpec((token_count, 128), lambda step: (0, step))

    def whole(shape):
        return pl.BlockSpec(shape, lambda step: (0, 0))

    return pl.pallas_call(
        functools.partial(mixing_grads_kernel, width, rows),
        grid=(heads // pack,),
        out_shape=(jax.ShapeDtypeStruct((token_count, model_width), jnp.bfloat16),) * 3,
        in_specs=[whole((token_count, 1)), whole((1, token_count)), whole(summary.shape)] + [tile] * 4,
        out_specs=(tile,) * 3,
        compiler_params=pltpu.CompilerParams(vmem_limit_bytes=32 * 1024 * 1024),
        cost_estimate=pl.CostEstimate(
            flops=10 * token_count * token_count * model_width,
            bytes_accessed=14 * token_count * model_width,
            transcendentals=heads * token_count * token_count,
        ),
        name="mixing_grads",
    )(image_index[:, None], image_index[None, :], summary, queries, key_rows, values, d_mixed)


IN_VMEM = pl.BlockSpec(memory_space=pltpu.VMEM)
IN_SMEM = pl.BlockSpec(memory_space=pltpu.SMEM)
ANYWHERE = pl.BlockSpec(memory_space=pl.ANY)


def hidden_forward_kernel(rows, normed_ref, middle_ref, bias_ref, *refs):
    part_refs = refs[:-3]
    final_ref, active_ref, slope_ref = refs[-3:]
    width = normed_ref.shape[1]

    def block(step, carry):
        here = pl.ds(pl.multiple_of(step * rows, rows), rows)
        normed = normed_ref[here]
        total = middle_ref[here]
        for index, part_ref in enumerate(part_refs):
            hidden = contract_cols(normed, part_ref[:, :width]) + bias_ref[pl.ds(index, 1)]
            active, slope = gelu_with_slope(hidden)
            active = active.astype(jnp.bfloat16)
            active_ref[index, here] = active
            slope_ref[index, here] = slope
            total = total + low_dot(active, part_ref[:, width:])
        final_ref[here] = total
        return carry

    lax.fori_loop(0, normed_ref.shape[0] // rows, block, 0)


def hidden_forward(normed, middle, bias, parts, rows=256):
    token_count, width = normed.shape
    count = len(parts)
    return pl.pallas_call(
        functools.partial(hidden_forward_kernel, rows),
        out_shape=(
            jax.ShapeDtypeStruct((token_count, width), jnp.float32),
            jax.ShapeDtypeStruct((count, token_count, width), jnp.bfloat16),
            jax.ShapeDtypeStruct((count, token_count, width), jnp.float32),
        ),
        in_specs=[IN_VMEM] * (3 + count),
        out_specs=(IN_VMEM,) * 3,
        compiler_params=pltpu.CompilerParams(vmem_limit_bytes=48 * 1024 * 1024),
        cost_estimate=pl.CostEstimate(
            flops=4 * count * token_count * width * width,
            bytes_accessed=4 * count * width * width + 8 * count * token_count * width,
            transcendentals=2 * count * token_count * width,
        ),
        name="hidden_forward",
    )(normed, middle, bias, *parts)


def hidden_back_kernel(core_ref, d_out_ref, normed_ref, *refs):
    active_refs, slope_refs, part_refs = refs[:2], refs[2:4], refs[4:8]
    d_hidden_ref, bias_ref, away_ref = refs[8:11]
    weights, actives, slopes, d_hiddens, aways, in_sems, out_sems = refs[11:]
    width = d_out_ref.shape[1]
    half = width // 2
    arriving = []
    for index, part_ref in enumerate(part_refs):
        sources = (
            part_ref.at[:, pl.ds(width, width)],
            slope_refs[index % 2].at[index // 2],
            active_refs[index % 2].at[index // 2],
        )
        copies = [
            pltpu.make_async_copy(source, target.at[index], in_sems.at[which, index])
            for which, (source, target) in enumerate(zip(sources, (weights, slopes, actives)))
        ]
        for copy in copies:
            copy.start()
        arriving.append(copies)
    first = core_ref[0, 0] == 0
    right = jnp.where(first, d_out_ref[...], normed_ref[...])
    slots = ((7, 3), (5, 1), (6, 4), (2, 0))
    leaving = []
    for index in range(4):
        for copy in arriving[index]:
            copy.wait()
        d_active = contract_cols(d_out_ref[...], weights[index])
        d_hidden = (slopes[index] * d_active).astype(jnp.bfloat16)
        d_hiddens[index] = d_hidden
        bias_ref[pl.ds(index, 1)] = jnp.sum(d_hidden.astype(jnp.float32), axis=0, keepdims=True)
        left = jnp.where(first, actives[index], d_hidden)
        grad = contract_rows(left, right).astype(jnp.bfloat16)
        aways[index] = grad
        copies = [
            pltpu.make_async_copy(d_hiddens.at[index], d_hidden_ref.at[index], out_sems.at[2, index])
        ]
        for side, slot in enumerate(slots[index]):
            copies.append(
                pltpu.make_async_copy(
                    aways.at[index, pl.ds(side * half, half)],
                    away_ref.at[pl.ds(slot * half, half)],
                    out_sems.at[side, index],
                )
            )
        for copy in copies:
            copy.start()
        leaving += copies
    for copy in leaving:
        copy.wait()


def hidden_back(core, d_out, normed, active, slope, parts):
    token_count, width = d_out.shape
    kept = (4, token_count, width)
    return pl.pallas_call(
        hidden_back_kernel,
        out_shape=(
            jax.ShapeDtypeStruct(kept, jnp.bfloat16),
            jax.ShapeDtypeStruct((4, width), jnp.float32),
            jax.ShapeDtypeStruct((4 * width, width), jnp.bfloat16),
        ),
        in_specs=[IN_SMEM, IN_VMEM, IN_VMEM] + [ANYWHERE] * 8,
        out_specs=(ANYWHERE, IN_VMEM, ANYWHERE),
        scratch_shapes=[
            pltpu.VMEM((4, width, width), jnp.bfloat16),
            pltpu.VMEM(kept, jnp.bfloat16),
            pltpu.VMEM(kept, jnp.float32),
            pltpu.VMEM(kept, jnp.bfloat16),
            pltpu.VMEM((4, width, width), jnp.bfloat16),
            pltpu.SemaphoreType.DMA((3, 4)),
            pltpu.SemaphoreType.DMA((3, 4)),
        ],
        compiler_params=pltpu.CompilerParams(vmem_limit_bytes=48 * 1024 * 1024),
        cost_estimate=pl.CostEstimate(
            flops=16 * token_count * width * width,
            bytes_accessed=16 * width * width + 32 * token_count * width,
            transcendentals=0,
        ),
        name="hidden_back",
    )(core.reshape(1, 1), d_out, normed, *active, *slope, *parts)


def kept_grads_kernel(plan, core_ref, d_out_ref, normed_ref, even_ref, odd_ref, d_hidden_ref, *refs):
    kept_ref = refs[-1]
    active_refs = (even_ref, odd_ref)
    width = d_out_ref.shape[1]
    half = width // 2
    first = core_ref[0, 0] == 0
    right = jnp.where(first, normed_ref[...], d_out_ref[...])
    for index, side, slot in plan:
        columns = slice(None) if side is None else slice(side * half, (side + 1) * half)
        left = jnp.where(
            first,
            d_hidden_ref[index, :, columns],
            active_refs[index % 2][index // 2, :, columns],
        )
        grad = contract_rows(left, right)
        if side is None:
            kept_ref[pl.ds(slot[0] * half, half)] = grad[:half]
            kept_ref[pl.ds(slot[1] * half, half)] = grad[half:]
        else:
            kept_ref[pl.ds(slot * half, half)] = grad
    if len(refs) > 1:
        part_refs, total_ref = refs[:4], refs[4]
        total = low_dot(d_hidden_ref[0], part_refs[0][:, :width])
        for index in range(1, 4):
            total = total + low_dot(d_hidden_ref[index], part_refs[index][:, :width])
        total_ref[...] = total


def kept_grads(plan, core, d_out, normed, active, d_hidden, parts=()):
    token_count, width = d_out.shape
    grads = jax.ShapeDtypeStruct((2 * width, width), jnp.float32)
    back = jax.ShapeDtypeStruct((token_count, width), jnp.float32)
    return pl.pallas_call(
        functools.partial(kept_grads_kernel, plan),
        out_shape=(back, grads) if parts else grads,
        in_specs=[IN_SMEM] + [IN_VMEM] * (5 + len(parts)),
        out_specs=(IN_VMEM,) * 2 if parts else IN_VMEM,
        compiler_params=pltpu.CompilerParams(vmem_limit_bytes=48 * 1024 * 1024),
        cost_estimate=pl.CostEstimate(
            flops=4 * token_count * width * width,
            bytes_accessed=8 * width * width + 20 * token_count * width,
            transcendentals=0,
        ),
        name="kept_grads",
    )(core.reshape(1, 1), d_out, normed, *active, d_hidden, *parts)


def orthogonal_kernel(part_count, chunk, full_steps, row_count, factor_ref, *refs):
    moment_refs, grad_refs = refs[:part_count], refs[part_count : 2 * part_count]
    out_ref, rows_ref, gram_ref, low_ref, change_ref, moments, grads, in_sems = refs[
        2 * part_count :
    ]
    part_rows, width = moment_refs[0].shape
    factor = factor_ref[0, 0]
    chunks = part_rows // chunk
    bf = jnp.bfloat16

    arriving = []
    for index in range(part_count):
        for step in range(chunks):
            here = pl.ds(step * chunk, chunk)
            spot = index * chunks + step
            copies = [
                pltpu.make_async_copy(source.at[here], target.at[spot], in_sems.at[which, spot])
                for which, (source, target) in enumerate(
                    ((moment_refs[index], moments), (grad_refs[index], grads))
                )
            ]
            for copy in copies:
                copy.start()
            arriving.append(copies)
    for spot, copies in enumerate(arriving):
        for copy in copies:
            copy.wait()
        rows = (
            momentum_keep * moments[spot].astype(jnp.float32)
            + factor * grads[spot].astype(jnp.float32)
        ).astype(bf)
        if full_steps:
            rows_ref[pl.ds(spot * chunk, chunk)] = rows
        elif spot == 0:
            out_ref[...] = rows[:row_count].astype(jnp.float32)
        if spot == 0:
            gram_ref[...] = contract_rows(rows, rows)
        else:
            gram_ref[...] += contract_rows(rows, rows)
    gram = gram_ref[...]
    diagonal = lax.broadcasted_iota(jnp.int32, gram.shape, 0) == lax.broadcasted_iota(
        jnp.int32, gram.shape, 1
    )
    trace = jnp.sum(jnp.where(diagonal, gram, 0.0))
    inverse = 1.0 / (jnp.sqrt(jnp.full((1, 1), trace)) + 1e-07)
    gram_ref[...] = gram * (inverse * inverse)
    if not full_steps:
        out_ref[...] = inverse * out_ref[...]
    for step in range(5):
        low_ref[...] = gram_ref[...].astype(bf)
        change_ref[...] = (
            newton_two * gram_ref[...] + newton_three * low_dot(low_ref[...], low_ref[...])
        ).astype(bf)
        if step < full_steps:
            scale = inverse if step == 0 else jnp.ones((1, 1), jnp.float32)
            last = step == full_steps - 1
            if step < 4:
                gram_ref[...] = jnp.zeros_like(gram_ref)

            def advance(index, carry, step=step, scale=scale, last=last):
                here = pl.ds(pl.multiple_of(index * chunk, chunk), chunk)
                old = rows_ref[here]
                new = scale * (newton_one * old.astype(jnp.float32) + low_dot(old, change_ref[...]))
                if last:
                    @pl.when(index == 0)
                    def _():
                        out_ref[...] = new[:row_count]
                new = new.astype(bf)
                if not last:
                    rows_ref[here] = new
                gram_ref[...] += contract_rows(new, new)
                return carry

            lax.fori_loop(0, part_count * chunks, advance, 0)
        else:
            rows = out_ref[...]
            out_ref[...] = newton_one * rows + low_dot(rows.astype(bf), change_ref[...])
            if step < 4:
                gram_ref[...] = newton_one * gram_ref[...] + low_dot(low_ref[...], change_ref[...])
                low_ref[...] = gram_ref[...].astype(bf)
                gram_ref[...] = newton_one * gram_ref[...] + low_dot(low_ref[...], change_ref[...])

def orthogonal_rows(moments, grads, factor, row_count, chunk, full_steps):
    count, (part_rows, width) = len(moments), moments[0].shape
    body = functools.partial(orthogonal_kernel, count, chunk, full_steps, row_count)
    flops = 2 * width * width * (count * part_rows * (2 * full_steps + 1) + 9 * width)
    return pl.pallas_call(
        body,
        out_shape=jax.ShapeDtypeStruct((row_count, width), jnp.float32),
        in_specs=[pl.BlockSpec(memory_space=pltpu.SMEM)]
        + [pl.BlockSpec(memory_space=pl.ANY)] * (2 * count),
        out_specs=pl.BlockSpec(memory_space=pltpu.VMEM),
        scratch_shapes=[
            pltpu.VMEM((count * part_rows if full_steps else 16, width), jnp.bfloat16),
            pltpu.VMEM((width, width), jnp.float32),
            pltpu.VMEM((width, width), jnp.bfloat16),
            pltpu.VMEM((width, width), jnp.bfloat16),
            pltpu.VMEM((count * part_rows // chunk, chunk, width), jnp.bfloat16),
            pltpu.VMEM((count * part_rows // chunk, chunk, width), jnp.bfloat16),
            pltpu.SemaphoreType.DMA((2, count * part_rows // chunk)),
        ],
        compiler_params=pltpu.CompilerParams(vmem_limit_bytes=48 * 1024 * 1024),
        cost_estimate=pl.CostEstimate(flops=flops, bytes_accessed=4 * count * part_rows * width, transcendentals=0),
        name="orthogonal_rows",
    )(factor.reshape(1, 1), *moments, *grads)


def adam_step(weight, first_moment, second_moment, gradient, step_rate):
    first_moment = adam_first * first_moment + (1.0 - adam_first) * gradient
    second_moment = adam_second * second_moment + (1.0 - adam_second) * gradient * gradient
    first_hat = first_moment / (1.0 - adam_first**STEP)
    second_hat = second_moment / (1.0 - adam_second**STEP)
    weight = weight * (1.0 - step_rate * decay_rate) - step_rate * first_hat / (
        jnp.sqrt(second_hat) + 1e-08
    )
    return (weight, first_moment, second_moment)


def on_device(
    patches,
    image_ids,
    patch_place,
    labels,
    attn_w,
    mlp_w,
    embed_w,
    vec_w,
    head_w,
    attn_mom,
    mlp_mom,
    embed_m,
    embed_v,
    vec_m,
    vec_v,
    head_m,
    head_v,
):
    groups = lax.axis_size("cls")
    owners = lax.axis_size("dp")
    count = groups * owners
    top = count.bit_length() - 1
    low_bits = groups.bit_length() - 1
    member_index = lax.axis_index("cls")
    owner_index = lax.axis_index("dp")
    me = owner_index * groups + member_index
    core = me & 1
    model_width = vec_w.shape[1]
    slot_count = labels.shape[1]
    high_bits = list(range(top - 1, 2, -1))
    third, fourth, pair = (2, 4), (4, 2), (1, 1)
    third_mine = jnp.where(core == 0, third[0], third[1])
    fourth_mine = jnp.where(core == 0, fourth[0], fourth[1])

    def exchange(value, masks, what="small"):
        with jax.named_scope(what):
            return swap(value, count, masks)

    def plain(bit):
        return (1 << bit,) * 2

    def bit_of(bit):
        return (me >> bit) & 1

    def lane(steps, what):
        return Lane(steps, exchange, what)

    def of_core(value):
        left, right = value[:, :model_width], value[:, model_width:]
        return jnp.where(core == 0, left, right), jnp.where(core == 0, right, left)

    attn_rows, embed_rows, mlp_rows = attn_w.shape[0], embed_w.shape[0], mlp_w.shape[0]
    up_stages = [plain(bit) for bit in high_bits]
    down_stages = up_stages[::-1]

    def ordered_weights(block):
        for axis, bit in enumerate(high_bits):
            block = ordered_pair(bit_of(bit), block, (yield block, plain(bit)), axis)
        block = block.reshape(-1, attn_rows + embed_rows, model_width)
        block = jnp.stack([block, (yield block, third)])
        block = jnp.concatenate([block, (yield block, fourth)], axis=0)
        return block, (yield block, pair)

    sibling = me ^ 1
    places = [
        me,
        me ^ third_mine,
        me ^ fourth_mine,
        me ^ 6,
        sibling,
        sibling ^ fourth_mine,
        sibling ^ third_mine,
        sibling ^ 6,
    ]
    attn_lane = lane(
        ordered_weights(jnp.concatenate([attn_w, embed_w], axis=0).astype(jnp.bfloat16)),
        "attn_weights",
    )
    mlp_lane = lane(
        collecting(mlp_w.astype(jnp.bfloat16)[None], up_stages + [third]), "mlp_weights"
    )
    for _ in high_bits:
        sync((), attn_lane)
    sync((), attn_lane, mlp_lane)
    sync((), attn_lane, mlp_lane)

    shard_rows, shard_width = head_w.shape
    chunk = -(-shard_width // (owners * 128)) * 128
    padding = owners * chunk - shard_width
    owner_bits = list(range(low_bits, top))

    def transposed(value, order):
        value = value.reshape((2,) * len(owner_bits) + value.shape[1:])
        for bit in order:
            axis = top - 1 - bit
            mine = bit_of(bit)
            stay, leave = pick(value, mine, axis), pick(value, 1 - mine, axis)
            value = ordered_pair(mine, stay, (yield leave, plain(bit)), axis)
        return value.reshape((owners,) + value.shape[len(owner_bits) :])

    head_low = jnp.pad(head_w.astype(jnp.bfloat16), ((0, 0), (0, padding)))
    head_low = head_low.reshape(shard_rows, owners, chunk).transpose(1, 0, 2)
    head_lane = lane(transposed(head_low, owner_bits[1:] + owner_bits[:1]), "head")

    def of_chip():
        value = mlp_mom.astype(jnp.bfloat16)
        mine, leave = of_core(value)
        rows = jnp.stack([mine, (yield leave, pair)])
        return (yield from collecting(rows, up_stages + [third, fourth]))

    mom_lane = lane(of_chip(), "mlp_moments")
    attn_mom_lane = lane(
        collecting(attn_mom.astype(jnp.bfloat16)[None], up_stages[2:] + [third, fourth, pair]),
        "attn_moments",
    )
    sync((), attn_lane, mlp_lane, head_lane)
    pieces, others = finish(attn_lane)[0]
    attn_b = jnp.zeros((count // 8, 8, attn_rows, model_width), jnp.bfloat16)
    embed_b = jnp.zeros((count // 8, 8, embed_rows, model_width), jnp.bfloat16)
    for index, place in enumerate(places):
        piece = (pieces if index < 4 else others)[index % 4]
        attn_b = lax.dynamic_update_slice_in_dim(attn_b, piece[:, None, :attn_rows], place & 7, 1)
        embed_b = lax.dynamic_update_slice_in_dim(embed_b, piece[:, None, attn_rows:], place & 7, 1)
    attn_b = attn_b.reshape(count * attn_rows, model_width)
    embed_b = embed_b.reshape(count * embed_rows, model_width)

    attn_b, embed_b = sync((attn_b, embed_b), mlp_lane, head_lane)
    part_a = jnp.concatenate(finish(mlp_lane)[0], axis=0)

    def once(value, stage):
        return (yield value, stage)

    b_lane = lane(once(part_a, fourth), "mlp_weights")
    c_lane = lane(once(part_a, pair), "mlp_weights")
    sync((), b_lane)
    sync((), c_lane)
    image_index = lax.dynamic_index_in_dim(image_ids, member_index, 0, keepdims=False)
    my_labels = lax.dynamic_index_in_dim(labels, member_index, 0, keepdims=False)
    position = patch_place[0]
    patch_dim = patches.shape[1]
    grid_size = (embed_b.shape[0] - patch_dim) // 2
    grid_index = jnp.arange(grid_size)
    places_hot = [(position[axis][:, None] == grid_index[None]).astype(jnp.bfloat16) for axis in (0, 1)]
    patch_wide = jnp.concatenate([patches] + places_hot, axis=1)
    embedded = low_dot(patch_wide, embed_b) + vec_w[10]
    normed, queries, key_rows, values = projections(attn_b, vec_w, embedded)
    mixed_out, summary = mixing(queries, key_rows, values, image_index, H)
    (mixed_out,) = sync((mixed_out,), c_lane, mom_lane)
    part_c = c_lane.result

    masks = [1 << bit for bit in high_bits]
    own_codes = [jnp.array(codes(masks + [third[c], fourth[c]]), jnp.int32) for c in (0, 1)]
    arrival = me ^ jnp.where(
        core == 0,
        jnp.concatenate([own_codes[0], own_codes[1] ^ 1]),
        jnp.concatenate([own_codes[1], own_codes[0] ^ 1]),
    )
    first_bias = jnp.take(vec_w[11:].reshape(count, mlp_rows), arrival, axis=0)
    first_bias = first_bias.reshape(4, -1)

    middle = embedded + low_dot(mixed_out, attn_b[3 * model_width :]) + vec_w[2]
    normed_two = layer_norm(middle, vec_w[6], vec_w[7]).astype(jnp.bfloat16)
    final_rows, active_even, slope_even = hidden_forward(
        normed_two, middle + vec_w[3], first_bias[::2], [part_a.reshape(-1, 2 * model_width), part_c.reshape(-1, 2 * model_width)]
    )
    final_rows, slope_even = sync((final_rows, slope_even), b_lane, head_lane)
    part_b = b_lane.result
    d_lane = lane(once(part_b, pair), "mlp_weights")
    sync((), d_lane)
    (final_rows,) = sync((final_rows,), d_lane, mom_lane, attn_mom_lane)
    mlp_parts = [
        part.reshape(-1, 2 * model_width) for part in (part_a, part_b, part_c, d_lane.result)
    ]
    final_rows, active_odd, slope_odd = hidden_forward(
        normed_two, final_rows, first_bias[1::2], mlp_parts[1::2]
    )
    active, slope = (active_even, active_odd), (slope_even, slope_odd)
    (final_rows,) = sync(
        (final_rows,), head_lane, mom_lane, attn_mom_lane, hold=(mom_lane, attn_mom_lane)
    )
    closing, close_pull = jax.vjp(layer_norm, final_rows, vec_w[8], vec_w[9])
    member = (image_index[None, :] == jnp.arange(slot_count)[:, None]).astype(jnp.float32)
    slot_sizes = jnp.sum(member, axis=1)
    divisor = jnp.maximum(slot_sizes, 1.0)[:, None]
    pooled = product(member, closing) / divisor
    facts = jnp.stack(
        [(slot_sizes > 0.5).astype(jnp.int32), my_labels // 256, my_labels % 256], axis=1
    )
    facts = jnp.pad(facts, ((0, 0), (0, 125))).astype(jnp.bfloat16)
    block = jnp.concatenate([pooled.astype(jnp.bfloat16), facts], axis=1)
    head_b = finish(head_lane)[0].reshape(owners * shard_rows, chunk)
    for axis, bit in enumerate(range(top - 1, -1, -1)):
        block = ordered_pair(bit_of(bit), block, exchange(block, plain(bit), "pooled"), axis)
    block = block.reshape(count * slot_count, -1)
    all_pooled = block[:, :model_width]
    facts = block[:, model_width : model_width + 3].astype(jnp.int32)
    valid = facts[:, 0] > 0
    all_labels = facts[:, 1] * 256 + facts[:, 2]
    image_total = jnp.sum(valid.astype(jnp.float32))

    logits = low_dot(all_pooled, head_b)
    within = owner_index * chunk + jnp.arange(chunk)
    columns = member_index * shard_width + within
    usable = (within < shard_width) & (columns < CLASSES)
    logits = jnp.where(usable[None], logits, -1e30)
    onehot = (usable[None] & (columns[None, :] == all_labels[:, None])).astype(jnp.float32)
    row_max = jnp.max(logits, axis=1)
    exp_sums = jnp.sum(jnp.exp(logits - row_max[:, None]), axis=1)
    stats = jnp.stack([row_max, exp_sums, jnp.sum(onehot * logits, axis=1)])
    for bit in range(top):
        other = exchange(stats, plain(bit), "stats")
        lower = jnp.where(bit_of(bit) == 0, stats, other)
        upper = jnp.where(bit_of(bit) == 0, other, stats)
        row_max = jnp.maximum(lower[0], upper[0])
        exp_sums = lower[1] * jnp.exp(lower[0] - row_max) + upper[1] * jnp.exp(upper[0] - row_max)
        stats = jnp.stack([row_max, exp_sums, lower[2] + upper[2]])
    normaliser = stats[0] + jnp.log(stats[1])
    loss_sum = jnp.sum(jnp.where(valid, normaliser - stats[2], 0.0))
    probs_class = jnp.exp(logits - normaliser[:, None])
    d_logits = (jnp.where(valid[:, None], probs_class - onehot, 0.0) / image_total).astype(
        jnp.bfloat16
    )
    d_pooled = contract_cols(d_logits, head_b)
    d_pooled = d_pooled.reshape((2,) * top + (slot_count, model_width))
    for bit in range(top):
        axis = top - 1 - bit
        mine = bit_of(bit)
        leave = pick(d_pooled, 1 - mine, axis).astype(jnp.bfloat16)
        d_pooled = pick(d_pooled, mine, axis) + exchange(leave, plain(bit), "d_pooled").astype(
            jnp.float32
        )
    d_closing = product(member.T, d_pooled / divisor)
    d_final, g_gain_final, g_shift_final = close_pull(d_closing)
    d_out = d_final.astype(jnp.bfloat16)
    g_second_bias = jnp.sum(d_out.astype(jnp.float32), axis=0)
    d_out, all_pooled = tie(d_out, all_pooled)
    head_grad = contract_rows(all_pooled, d_logits)
    head_squares = jnp.sum(head_grad * head_grad) / model_width
    head_lane = lane(
        transposed(
            head_grad.astype(jnp.bfloat16).reshape(owners, shard_rows, chunk),
            owner_bits[1:-1] + owner_bits[:1] + owner_bits[-1:],
        ),
        "head_grads",
    )
    (d_out,) = sync((d_out,), mom_lane, attn_mom_lane)

    d_hidden, bias_grads, away = hidden_back(core, d_out, normed_two, active, slope, mlp_parts)
    (away, d_hidden) = sync((away, d_hidden), mom_lane, attn_mom_lane)
    arrived = exchange(away, pair, "mlp_grads")
    operands = (core, d_out, normed_two, active, d_hidden)
    first_plan = ((1, None, (2, 0)), (3, 1, 1), (2, 1, 3))
    second_plan = ((0, None, (2, 0)), (3, 0, 1), (2, 0, 3))
    leave = kept_grads(first_plan, *operands)
    leave, arrived, d_hidden = sync(
        (leave, arrived, d_hidden), attn_mom_lane
    )
    operands = (core, d_out, normed_two, active, d_hidden)
    half = 2 * model_width
    leave = (leave + arrived[:half].astype(jnp.float32)).astype(jnp.bfloat16)

    def summing(leave, kept, arrived):
        far = yield leave, fourth
        summed = kept() + arrived.astype(jnp.float32) + far.astype(jnp.float32)
        arrived = yield summed[:model_width].astype(jnp.bfloat16), third
        kept = summed[model_width:] + arrived.astype(jnp.float32)
        kept = kept.reshape(2, -1, mlp_rows, model_width)
        for stage in down_stages:
            half = kept.shape[1] // 2
            arrived = yield kept[:, half:].astype(jnp.bfloat16), stage
            kept = kept[:, :half] + arrived.astype(jnp.float32)
        return kept[:, 0]

    own = []
    mlp_lane = lane(summing(leave, lambda: own[0], arrived[half:]), "mlp_grads")
    sync((), mlp_lane)
    d_normed_two, grads = kept_grads(second_plan, *operands, mlp_parts)
    own.append(grads)
    (d_normed_two,) = sync((d_normed_two,), head_lane)

    d_mid_norm, g_gain_two, g_shift_two = jax.vjp(layer_norm, middle, vec_w[6], vec_w[7])[1](
        d_normed_two
    )
    d_middle = d_final + d_mid_norm
    d_proj = d_middle.astype(jnp.bfloat16)
    g_out_bias = jnp.sum(d_proj.astype(jnp.float32), axis=0)
    d_mixed = contract_cols(d_proj, attn_b[3 * model_width :]).astype(jnp.bfloat16)
    d_queries, d_keys, d_values = mixing_grads(
        queries, key_rows, values, d_mixed, summary, image_index, H
    )
    d_queries, d_keys, d_values, own[0] = sync(
        (d_queries, d_keys, d_values, own[0]),
        mlp_lane,
        mom_lane,
        head_lane,
        hold=(mom_lane, head_lane),
    )
    attn_grad = jnp.concatenate(
        [
            contract_rows(normed, d_queries),
            contract_rows(normed, d_keys),
            contract_rows(normed, d_values),
            contract_rows(mixed_out, d_proj),
        ],
        axis=0,
    )

    quarter = (me >> 1) & 3
    to_third, to_fourth = third_mine >> 1, fourth_mine >> 1

    def quartered(grad, rows):
        grad = grad.reshape(count // 8, 4, 2, rows, model_width)
        leave = pick(grad, 1 - core, 2).astype(jnp.bfloat16)
        grad = pick(grad, core, 2) + (yield leave, pair).astype(jnp.float32)
        leave = [pick(grad, quarter ^ to_fourth, 1), pick(grad, quarter ^ 3, 1)]
        leave = (yield jnp.stack(leave).astype(jnp.bfloat16), fourth).astype(jnp.float32)
        leaving = pick(grad, quarter ^ to_third, 1) + leave[1]
        return pick(grad, quarter, 1) + leave[0], leaving

    def last_sums(grads):
        grad = jnp.concatenate([one[0] for one in grads], axis=1)
        leave = jnp.concatenate([one[1].astype(jnp.bfloat16) for one in grads], axis=1)
        grad = grad + (yield leave, third).astype(jnp.float32)
        grad = grad.reshape((2,) * len(high_bits) + grad.shape[1:])
        for bit in reversed(high_bits):
            axis = top - 1 - bit
            mine = bit_of(bit)
            leave = pick(grad, 1 - mine, axis).astype(jnp.bfloat16)
            grad = pick(grad, mine, axis) + (yield leave, plain(bit)).astype(jnp.float32)
        return grad

    attn_lane = lane(quartered(attn_grad, attn_rows), "attn_grads")
    d_normed = (
        contract_cols(d_queries, attn_b[:model_width])
        + contract_cols(d_keys, attn_b[model_width : 2 * model_width])
        + contract_cols(d_values, attn_b[2 * model_width : 3 * model_width])
    )
    sync((), attn_lane)
    (d_normed,) = sync((d_normed,), mlp_lane, attn_lane, head_lane)
    d_emb_norm, g_gain_one, g_shift_one = jax.vjp(layer_norm, embedded, vec_w[4], vec_w[5])[1](
        d_normed
    )
    d_embed_low = (d_middle + d_emb_norm).astype(jnp.bfloat16)
    embed_grad = contract_rows(patch_wide, d_embed_low)
    embed_lane = lane(quartered(embed_grad, embed_rows), "embed_grads")
    sync((), embed_lane)
    sync((), embed_lane, mlp_lane, head_lane, hold=(head_lane,))
    finish(attn_lane, embed_lane)
    sum_lane = lane(last_sums([attn_lane.result, embed_lane.result]), "last_grads")
    sync((), sum_lane)
    mlp_grad = finish(mlp_lane)[0]
    all_lane = lane(
        collecting(mlp_grad.astype(jnp.bfloat16), up_stages + [third, fourth]), "mlp_grads_all"
    )
    sync((), all_lane, mom_lane)
    sync((), sum_lane, all_lane)
    sync((), sum_lane, all_lane, mom_lane)
    while sum_lane.result is None:
        sync((), sum_lane, all_lane, hold=(all_lane,))
    attn_sum, embed_sum = sum_lane.result[:attn_rows], sum_lane.result[attn_rows:]
    g_query_bias = jnp.sum(d_queries.astype(jnp.float32), axis=0)
    g_value_bias = jnp.sum(d_values.astype(jnp.float32), axis=0)
    g_patch_bias = jnp.sum(d_embed_low.astype(jnp.float32), axis=0)
    g_first_bias = jnp.take(bias_grads.reshape(count, mlp_rows), jnp.argsort(arrival), axis=0)
    vec_grad = jnp.concatenate(
        [
            jnp.stack(
                [
                    g_query_bias,
                    g_value_bias,
                    g_out_bias,
                    g_second_bias,
                    g_gain_one,
                    g_shift_one,
                    g_gain_two,
                    g_shift_two,
                    g_gain_final,
                    g_shift_final,
                    g_patch_bias,
                ]
            ),
            g_first_bias.reshape(-1, model_width),
        ],
        axis=0,
    )
    local_squares = sum(
        jnp.sum(grad * grad, axis=0) for grad in (attn_sum, embed_sum, mlp_grad[0], mlp_grad[1])
    )
    small_sums = jnp.concatenate([vec_grad, (local_squares + head_squares)[None]], axis=0)

    def total(value):
        for bit in [1, 2, 0] + list(range(3, top)):
            value = value + (yield value, plain(bit))
        return value

    small_lane = lane(total(small_sums), "small_sums")
    block_lane = lane(
        collecting(attn_sum.astype(jnp.bfloat16)[None], up_stages[2:] + [third, fourth, pair]),
        "attn_grads_all",
    )
    sync((), small_lane, block_lane)
    sync((), small_lane, block_lane)
    sync((), small_lane, block_lane, all_lane)
    small_sums, attn_grads = finish(small_lane, block_lane)
    attn_moms = jnp.concatenate(finish(attn_mom_lane)[0], axis=0).reshape(-1, model_width)
    attn_grads = jnp.concatenate(attn_grads, axis=0).reshape(-1, model_width)
    vec_sum = small_sums[:-1]
    grad_norm = jnp.sqrt(jnp.sum(small_sums[-1]) + jnp.sum(vec_sum * vec_sum))
    factor = jnp.minimum(1.0, clip_limit / (grad_norm + 1e-06))
    attn_mom_out = momentum_keep * attn_mom + factor * attn_sum
    mine, away = mlp_grad[0], exchange(mlp_grad[1], pair)
    mlp_sum = jnp.concatenate(
        [jnp.where(core == 0, mine, away), jnp.where(core == 0, away, mine)], axis=1
    )
    mlp_mom_out = momentum_keep * mlp_mom + factor * mlp_sum

    (factor,) = sync((factor,), head_lane)
    attn_dir = orthogonal_rows([attn_moms], [attn_grads], factor, attn_rows, 768, 4)
    (attn_dir,) = sync((attn_dir,), all_lane, mom_lane)
    mlp_grads, mlp_moms = finish(all_lane, mom_lane)
    mlp_result = orthogonal_rows(
        [part.reshape(-1, model_width) for part in mlp_moms],
        [part.reshape(-1, model_width) for part in mlp_grads],
        factor,
        2 * mlp_rows,
        768,
        0,
    )
    (mlp_result,) = sync((mlp_result,), head_lane)
    mlp_other = exchange(mlp_result[mlp_rows:], pair)
    mlp_result = mlp_result[:mlp_rows]
    mlp_dir = jnp.concatenate(
        [
            jnp.where(core == 0, mlp_result, mlp_other),
            jnp.where(core == 0, mlp_other, mlp_result),
        ],
        axis=1,
    )
    head_grad = finish(head_lane)[0].transpose(1, 0, 2)
    head_grad = head_grad.reshape(shard_rows, owners * chunk)[:, :shard_width].astype(jnp.float32)
    mlp_scale = math.sqrt(mlp_rows * count / model_width)
    attn_out = attn_w * (1.0 - muon_rate * decay_rate) - muon_rate * attn_dir
    mlp_out = mlp_w * (1.0 - muon_rate * decay_rate) - muon_rate * mlp_scale * mlp_dir
    embed_out, embed_m_out, embed_v_out = adam_step(
        embed_w, embed_m, embed_v, factor * embed_sum, adam_rate
    )
    vec_out, vec_m_out, vec_v_out = adam_step(vec_w, vec_m, vec_v, factor * vec_sum, vector_rate)
    head_out, head_m_out, head_v_out = adam_step(
        head_w, head_m, head_v, factor * head_grad, adam_rate
    )
    return (
        loss_sum,
        image_total,
        grad_norm,
        attn_out,
        attn_mom_out,
        attn_out.astype(jnp.bfloat16),
        mlp_out,
        mlp_mom_out,
        mlp_out.astype(jnp.bfloat16),
        embed_out,
        embed_m_out,
        embed_v_out,
        embed_out.astype(jnp.bfloat16),
        vec_out,
        vec_m_out,
        vec_v_out,
        vec_out.astype(jnp.bfloat16),
        head_out,
        head_m_out,
        head_v_out,
        head_out.astype(jnp.bfloat16),
    )


def solution(mesh):
    return jax.shard_map(
        on_device,
        mesh=mesh,
        in_specs=(
            P(("dp", "cls"), None),
            P("dp", None),
            P(("dp", "cls"), None, None),
            P("dp", None),
            P(("dp", "cls"), None),
            P(("dp", "cls"), None),
            P(("dp", "cls"), None),
            P(),
            P("dp", "cls"),
            P(("dp", "cls"), None),
            P(("dp", "cls"), None),
            P(("dp", "cls"), None),
            P(("dp", "cls"), None),
            P(),
            P(),
            P("dp", "cls"),
            P("dp", "cls"),
        ),
        out_specs=(
            P(),
            P(),
            P(),
            P(("dp", "cls"), None),
            P(("dp", "cls"), None),
            P(("dp", "cls"), None),
            P(("dp", "cls"), None),
            P(("dp", "cls"), None),
            P(("dp", "cls"), None),
            P(("dp", "cls"), None),
            P(("dp", "cls"), None),
            P(("dp", "cls"), None),
            P(("dp", "cls"), None),
            P(),
            P(),
            P(),
            P(),
            P("dp", "cls"),
            P("dp", "cls"),
            P("dp", "cls"),
            P("dp", "cls"),
        ),
        check_vma=False,
    )
```

```python
import functools
import math

import jax
import jax.numpy as jnp
from jax import lax
from jax.experimental import pallas as pl
from jax.experimental.pallas import tpu as pltpu
from jax.sharding import PartitionSpec as P

H = 12
CLASSES = 21843
STEP = 10


highest = lax.Precision.HIGHEST
newton_one = 3.4445
newton_two = -4.775
newton_three = 2.0315
clip_limit = 0.05
muon_rate = 0.3
decay_rate = 0.05
adam_rate = 0.01
vector_rate = 0.05
momentum_keep = 0.5
adam_first = 0.5
adam_second = 0.999


AXES = ("dp", "cls")


def swap(value, count, masks):
    return lax.ppermute(value, AXES, [(i, i ^ masks[i & 1]) for i in range(count)])


def pick(value, index, axis):
    return lax.dynamic_index_in_dim(value, index, axis, keepdims=False)


def codes(masks):
    found = [0]
    for mask in masks:
        found = found + [code ^ mask for code in found]
    return found


def ordered_pair(bit, mine, other, axis):
    return jnp.where(
        bit == 0, jnp.stack([mine, other], axis=axis), jnp.stack([other, mine], axis=axis)
    )


def product(left_side, right_side):
    return jnp.dot(left_side, right_side, precision=highest)


def low_dot(left_side, right_side):
    return jnp.dot(left_side, right_side, preferred_element_type=jnp.float32)


def contract_rows(left_side, right_side):
    return lax.dot_general(
        left_side, right_side, (((0,), (0,)), ((), ())), preferred_element_type=jnp.float32
    )


def contract_cols(left_side, right_side):
    return lax.dot_general(
        left_side, right_side, (((1,), (1,)), ((), ())), preferred_element_type=jnp.float32
    )


def layer_norm(inputs, gain_row, shift_row):
    mean_row = jnp.mean(inputs, axis=-1, keepdims=True)
    centred = inputs - mean_row
    variance = jnp.mean(centred * centred, axis=-1, keepdims=True)
    return centred * lax.rsqrt(variance + 1e-06) * gain_row + shift_row


def tie(*values):
    return lax.optimization_barrier(values)


class Lane:
    def __init__(self, steps, exchange, what):
        self.steps, self.exchange, self.what = steps, exchange, what
        self.moving, self.result = False, None
        self.value, self.masks = next(steps)

    def advance(self, value, start):
        masks = self.masks
        if self.moving:
            try:
                value, masks = self.steps.send(value)
            except StopIteration as end:
                self.value, self.result, self.moving = None, end.value, False
                return
            if not start:
                self.value, self.masks, self.moving = value, masks, False
                return
        self.moving = True
        self.value, self.masks = self.exchange(value, masks, self.what), masks


def sync(values, *lanes, hold=()):
    lanes = [lane for lane in lanes if lane.result is None]
    tied = tie(*values, *[lane.value for lane in lanes])
    for lane, value in zip(lanes, tied[len(values) :]):
        lane.advance(value, lane not in hold)
    return tied[: len(values)]


def finish(*lanes):
    while any(lane.result is None for lane in lanes):
        sync((), *lanes)
    return [lane.result for lane in lanes]


def collecting(value, stages):
    for stage in stages[:-1]:
        value = jnp.concatenate([value, (yield value, stage)], axis=0)
    return [value, (yield value, stages[-1])]


def gelu_with_slope(value):
    size = jnp.abs(value)
    bell = jnp.exp(-0.5 * value * value)
    t = 1.0 / (1.0 + (0.3275911 * 0.7071067811865476) * size)
    poly = 1.061405429
    for term in (-1.453152027, 1.421413741, -0.284496736, 0.254829592):
        poly = poly * t + term
    tail = 0.5 * poly * t * bell
    share = jnp.where(value < 0, tail, 1.0 - tail)
    return value * share, share + value * (0.3989422804014327 * bell)


def projections(attn_b, vec_w, embedded):
    model_width = attn_b.shape[1]
    normed = layer_norm(embedded, vec_w[4], vec_w[5]).astype(jnp.bfloat16)
    queries = (low_dot(normed, attn_b[:model_width]) + vec_w[0]).astype(jnp.bfloat16)
    key_rows = low_dot(normed, attn_b[model_width : 2 * model_width]).astype(jnp.bfloat16)
    values = (low_dot(normed, attn_b[2 * model_width : 3 * model_width]) + vec_w[1]).astype(
        jnp.bfloat16
    )
    return (normed, queries, key_rows, values)


def half_of(value, half, width):
    lane = lax.broadcasted_iota(jnp.int32, value.shape, 1)
    keep = (lane >= half * width) & (lane < (half + 1) * width)
    return jnp.where(keep, value, jnp.zeros_like(value))


def mixing_kernel(width, rows, ids_down_ref, ids_ref, q_ref, k_ref, v_ref, out_ref, summary_ref, seen_ref):
    step = pl.program_id(0)
    pack = q_ref.shape[1] // width
    keys = [half_of(k_ref[...], half, width) for half in range(pack)]
    values = [half_of(v_ref[...], half, width) for half in range(pack)]
    scale = width ** (-0.5)
    lane = lax.broadcasted_iota(jnp.int32, (rows, seen_ref.shape[1]), 1)
    for start in range(0, q_ref.shape[0], rows):
        here = pl.ds(start, rows)
        same = ids_down_ref[here] == ids_ref[...]
        queries = q_ref[here]
        seen = seen_ref[here]
        total = None
        for half in range(pack):
            scores = jnp.where(same, contract_cols(queries, keys[half]) * scale, -1e30)
            top = jnp.max(scores, axis=1, keepdims=True)
            exponents = jnp.exp(scores - top)
            sums = jnp.sum(exponents, axis=1, keepdims=True)
            probs = (exponents * (1.0 / sums)).astype(jnp.bfloat16)
            mixed = low_dot(probs, values[half])
            total = mixed if total is None else total + mixed
            seen = jnp.where(lane == step * pack + half, top + jnp.log(sums), seen)
        out_ref[here] = total.astype(out_ref.dtype)
        seen_ref[here] = seen

    @pl.when(step == pl.num_programs(0) - 1)
    def _():
        summary_ref[...] = seen_ref[...].T[: summary_ref.shape[0]]


def mixing(queries, key_rows, values, image_index, heads, rows=256):
    token_count, model_width = queries.shape
    width = model_width // heads
    pack = 128 // width
    tile = pl.BlockSpec((token_count, 128), lambda step: (0, step))

    def whole(shape):
        return pl.BlockSpec(shape, lambda step: (0, 0))

    kept = -(-heads // 8) * 8
    return pl.pallas_call(
        functools.partial(mixing_kernel, width, rows),
        grid=(heads // pack,),
        out_shape=(
            jax.ShapeDtypeStruct((token_count, model_width), jnp.bfloat16),
            jax.ShapeDtypeStruct((kept, token_count), jnp.float32),
        ),
        in_specs=[whole((token_count, 1)), whole((1, token_count)), tile, tile, tile],
        out_specs=(tile, whole((kept, token_count))),
        scratch_shapes=[pltpu.VMEM((token_count, 128), jnp.float32)],
        compiler_params=pltpu.CompilerParams(vmem_limit_bytes=32 * 1024 * 1024),
        cost_estimate=pl.CostEstimate(
            flops=4 * token_count * token_count * model_width,
            bytes_accessed=8 * token_count * model_width,
            transcendentals=heads * token_count * token_count,
        ),
        name="mixing",
    )(image_index[:, None], image_index[None, :], queries, key_rows, values)


def mixing_grads_kernel(width, rows, ids_down_ref, ids_ref, summary_ref, q_ref, k_ref, v_ref, d_ref, dq_ref, dk_ref, dv_ref):
    step = pl.program_id(0)
    pack = q_ref.shape[1] // width
    scale = width ** (-0.5)
    keys = [half_of(k_ref[...], half, width) for half in range(pack)]
    values = [half_of(v_ref[...], half, width) for half in range(pack)]
    key_sums, value_sums = 0.0, 0.0
    for start in range(0, q_ref.shape[0], rows):
        here = pl.ds(start, rows)
        same = ids_down_ref[...] == ids_ref[:, here]
        query_sum = 0.0
        for half in range(pack):
            queries, d_mixed = half_of(q_ref[here], half, width), half_of(d_ref[here], half, width)
            scores = contract_cols(keys[half], queries) * scale
            summary = summary_ref[pl.ds(step * pack + half, 1), here]
            probs = jnp.where(same, jnp.exp(jnp.where(same, scores - summary, -1e30)), 0.0)
            d_probs = contract_cols(values[half], d_mixed)
            product = probs * d_probs
            d_scores = product - probs * jnp.sum(product, axis=0, keepdims=True)
            d_scores = d_scores.astype(jnp.bfloat16)
            value_sums = value_sums + low_dot(probs.astype(jnp.bfloat16), d_mixed)
            key_sums = key_sums + low_dot(d_scores, queries)
            query_sum = query_sum + contract_rows(d_scores, keys[half])
        dq_ref[here] = (query_sum * scale).astype(dq_ref.dtype)
    dk_ref[...] = (key_sums * scale).astype(dk_ref.dtype)
    dv_ref[...] = value_sums.astype(dv_ref.dtype)


def mixing_grads(queries, key_rows, values, d_mixed, summary, image_index, heads, rows=256):
    token_count, model_width = queries.shape
    width = model_width // heads
    pack = 128 // width
    tile = pl.BlockSpec((token_count, 128), lambda step: (0, step))

    def whole(shape):
        return pl.BlockSpec(shape, lambda step: (0, 0))

    return pl.pallas_call(
        functools.partial(mixing_grads_kernel, width, rows),
        grid=(heads // pack,),
        out_shape=(jax.ShapeDtypeStruct((token_count, model_width), jnp.bfloat16),) * 3,
        in_specs=[whole((token_count, 1)), whole((1, token_count)), whole(summary.shape)] + [tile] * 4,
        out_specs=(tile,) * 3,
        compiler_params=pltpu.CompilerParams(vmem_limit_bytes=32 * 1024 * 1024),
        cost_estimate=pl.CostEstimate(
            flops=10 * token_count * token_count * model_width,
            bytes_accessed=14 * token_count * model_width,
            transcendentals=heads * token_count * token_count,
        ),
        name="mixing_grads",
    )(image_index[:, None], image_index[None, :], summary, queries, key_rows, values, d_mixed)


IN_VMEM = pl.BlockSpec(memory_space=pltpu.VMEM)
IN_SMEM = pl.BlockSpec(memory_space=pltpu.SMEM)
ANYWHERE = pl.BlockSpec(memory_space=pl.ANY)


def hidden_forward_kernel(rows, normed_ref, middle_ref, bias_ref, *refs):
    part_refs = refs[:-3]
    final_ref, active_ref, slope_ref = refs[-3:]
    width = normed_ref.shape[1]

    def block(step, carry):
        here = pl.ds(pl.multiple_of(step * rows, rows), rows)
        normed = normed_ref[here]
        total = middle_ref[here]
        for index, part_ref in enumerate(part_refs):
            hidden = contract_cols(normed, part_ref[:, :width]) + bias_ref[pl.ds(index, 1)]
            active, slope = gelu_with_slope(hidden)
            active = active.astype(jnp.bfloat16)
            active_ref[index, here] = active
            slope_ref[index, here] = slope
            total = total + low_dot(active, part_ref[:, width:])
        final_ref[here] = total
        return carry

    lax.fori_loop(0, normed_ref.shape[0] // rows, block, 0)


def hidden_forward(normed, middle, bias, parts, rows=256):
    token_count, width = normed.shape
    count = len(parts)
    return pl.pallas_call(
        functools.partial(hidden_forward_kernel, rows),
        out_shape=(
            jax.ShapeDtypeStruct((token_count, width), jnp.float32),
            jax.ShapeDtypeStruct((count, token_count, width), jnp.bfloat16),
            jax.ShapeDtypeStruct((count, token_count, width), jnp.float32),
        ),
        in_specs=[IN_VMEM] * (3 + count),
        out_specs=(IN_VMEM,) * 3,
        compiler_params=pltpu.CompilerParams(vmem_limit_bytes=48 * 1024 * 1024),
        cost_estimate=pl.CostEstimate(
            flops=4 * count * token_count * width * width,
            bytes_accessed=4 * count * width * width + 8 * count * token_count * width,
            transcendentals=2 * count * token_count * width,
        ),
        name="hidden_forward",
    )(normed, middle, bias, *parts)


def hidden_back_kernel(core_ref, d_out_ref, normed_ref, *refs):
    active_refs, slope_refs, part_refs = refs[:2], refs[2:4], refs[4:8]
    d_hidden_ref, bias_ref, away_ref = refs[8:11]
    weights, actives, slopes, d_hiddens, aways, in_sems, out_sems = refs[11:]
    width = d_out_ref.shape[1]
    half = width // 2
    arriving = []
    for index, part_ref in enumerate(part_refs):
        sources = (
            part_ref.at[:, pl.ds(width, width)],
            slope_refs[index % 2].at[index // 2],
            active_refs[index % 2].at[index // 2],
        )
        copies = [
            pltpu.make_async_copy(source, target.at[index], in_sems.at[which, index])
            for which, (source, target) in enumerate(zip(sources, (weights, slopes, actives)))
        ]
        for copy in copies:
            copy.start()
        arriving.append(copies)
    first = core_ref[0, 0] == 0
    right = jnp.where(first, d_out_ref[...], normed_ref[...])
    slots = ((7, 3), (5, 1), (6, 4), (2, 0))
    leaving = []
    for index in range(4):
        for copy in arriving[index]:
            copy.wait()
        d_active = contract_cols(d_out_ref[...], weights[index])
        d_hidden = (slopes[index] * d_active).astype(jnp.bfloat16)
        d_hiddens[index] = d_hidden
        bias_ref[pl.ds(index, 1)] = jnp.sum(d_hidden.astype(jnp.float32), axis=0, keepdims=True)
        left = jnp.where(first, actives[index], d_hidden)
        grad = contract_rows(left, right).astype(jnp.bfloat16)
        aways[index] = grad
        copies = [
            pltpu.make_async_copy(d_hiddens.at[index], d_hidden_ref.at[index], out_sems.at[2, index])
        ]
        for side, slot in enumerate(slots[index]):
            copies.append(
                pltpu.make_async_copy(
                    aways.at[index, pl.ds(side * half, half)],
                    away_ref.at[pl.ds(slot * half, half)],
                    out_sems.at[side, index],
                )
            )
        for copy in copies:
            copy.start()
        leaving += copies
    for copy in leaving:
        copy.wait()


def hidden_back(core, d_out, normed, active, slope, parts):
    token_count, width = d_out.shape
    kept = (4, token_count, width)
    return pl.pallas_call(
        hidden_back_kernel,
        out_shape=(
            jax.ShapeDtypeStruct(kept, jnp.bfloat16),
            jax.ShapeDtypeStruct((4, width), jnp.float32),
            jax.ShapeDtypeStruct((4 * width, width), jnp.bfloat16),
        ),
        in_specs=[IN_SMEM, IN_VMEM, IN_VMEM] + [ANYWHERE] * 8,
        out_specs=(ANYWHERE, IN_VMEM, ANYWHERE),
        scratch_shapes=[
            pltpu.VMEM((4, width, width), jnp.bfloat16),
            pltpu.VMEM(kept, jnp.bfloat16),
            pltpu.VMEM(kept, jnp.float32),
            pltpu.VMEM(kept, jnp.bfloat16),
            pltpu.VMEM((4, width, width), jnp.bfloat16),
            pltpu.SemaphoreType.DMA((3, 4)),
            pltpu.SemaphoreType.DMA((3, 4)),
        ],
        compiler_params=pltpu.CompilerParams(vmem_limit_bytes=48 * 1024 * 1024),
        cost_estimate=pl.CostEstimate(
            flops=16 * token_count * width * width,
            bytes_accessed=16 * width * width + 32 * token_count * width,
            transcendentals=0,
        ),
        name="hidden_back",
    )(core.reshape(1, 1), d_out, normed, *active, *slope, *parts)


def kept_grads_kernel(
    plan, core_ref, d_out_ref, normed_ref, even_ref, odd_ref, d_hidden_ref, *refs
):
    active_refs = (even_ref, odd_ref)
    width = d_out_ref.shape[1]
    half = width // 2
    first = core_ref[0, 0] == 0
    right = jnp.where(first, normed_ref[...], d_out_ref[...])
    kept_ref = refs[-1]
    arrived_ref = refs[0]
    for index, side, slots in plan:
        columns = slice(None) if side is None else slice(side * half, (side + 1) * half)
        left = jnp.where(
            first,
            d_hidden_ref[index, :, columns],
            active_refs[index % 2][index // 2, :, columns],
        )
        grad = contract_rows(left, right)
        for position, slot in enumerate(slots):
            here = pl.ds(slot * half, half)
            rows = grad[position * half : (position + 1) * half]
            rows = rows + arrived_ref[here].astype(jnp.float32)
            kept_ref[here] = rows.astype(kept_ref.dtype)
    if len(refs) > 2:
        part_refs, total_ref = refs[1:5], refs[5]
        total = low_dot(d_hidden_ref[0], part_refs[0][:, :width])
        for index in range(1, 4):
            total = total + low_dot(d_hidden_ref[index], part_refs[index][:, :width])
        total_ref[...] = total


def kept_grads(plan, core, d_out, normed, active, d_hidden, arrived, parts=()):
    token_count, width = d_out.shape
    grads = jax.ShapeDtypeStruct((2 * width, width), jnp.float32 if parts else jnp.bfloat16)
    back = jax.ShapeDtypeStruct((token_count, width), jnp.float32)
    side = 1 if parts else 0
    arrived_spec = pl.BlockSpec((2 * width, width), lambda step: (side, 0))
    return pl.pallas_call(
        functools.partial(kept_grads_kernel, plan),
        grid=(1,),
        out_shape=(back, grads) if parts else grads,
        in_specs=[IN_SMEM] + [IN_VMEM] * 5 + [arrived_spec] + [IN_VMEM] * len(parts),
        out_specs=(IN_VMEM,) * 2 if parts else IN_VMEM,
        compiler_params=pltpu.CompilerParams(vmem_limit_bytes=48 * 1024 * 1024),
        cost_estimate=pl.CostEstimate(
            flops=4 * token_count * width * width,
            bytes_accessed=8 * width * width + 20 * token_count * width,
            transcendentals=0,
        ),
        name="kept_grads",
    )(core.reshape(1, 1), d_out, normed, *active, d_hidden, arrived, *parts)


def orthogonal_kernel(part_count, chunk, full_steps, row_count, factor_ref, *refs):
    moment_refs, grad_refs = refs[:part_count], refs[part_count : 2 * part_count]
    out_ref, rows_ref, gram_ref, low_ref, change_ref, moments, grads, in_sems = refs[
        2 * part_count :
    ]
    part_rows, width = moment_refs[0].shape
    factor = factor_ref[0, 0]
    chunks = part_rows // chunk
    bf = jnp.bfloat16

    arriving = []
    for index in range(part_count):
        for step in range(chunks):
            here = pl.ds(step * chunk, chunk)
            spot = index * chunks + step
            copies = [
                pltpu.make_async_copy(source.at[here], target.at[spot], in_sems.at[which, spot])
                for which, (source, target) in enumerate(
                    ((moment_refs[index], moments), (grad_refs[index], grads))
                )
            ]
            for copy in copies:
                copy.start()
            arriving.append(copies)
    for spot, copies in enumerate(arriving):
        for copy in copies:
            copy.wait()
        rows = (
            momentum_keep * moments[spot].astype(jnp.float32)
            + factor * grads[spot].astype(jnp.float32)
        ).astype(bf)
        if full_steps:
            rows_ref[pl.ds(spot * chunk, chunk)] = rows
        elif spot == 0:
            out_ref[...] = rows[:row_count].astype(jnp.float32)
        if spot == 0:
            gram_ref[...] = contract_rows(rows, rows)
        else:
            gram_ref[...] += contract_rows(rows, rows)
    gram = gram_ref[...]
    diagonal = lax.broadcasted_iota(jnp.int32, gram.shape, 0) == lax.broadcasted_iota(
        jnp.int32, gram.shape, 1
    )
    trace = jnp.sum(jnp.where(diagonal, gram, 0.0))
    inverse = 1.0 / (jnp.sqrt(jnp.full((1, 1), trace)) + 1e-07)
    gram_ref[...] = gram * (inverse * inverse)
    if not full_steps:
        out_ref[...] = inverse * out_ref[...]
    for step in range(5):
        low_ref[...] = gram_ref[...].astype(bf)
        change_ref[...] = (
            newton_two * gram_ref[...] + newton_three * low_dot(low_ref[...], low_ref[...])
        ).astype(bf)
        if step < full_steps:
            scale = inverse if step == 0 else jnp.ones((1, 1), jnp.float32)
            last = step == full_steps - 1
            if step < 4:
                gram_ref[...] = jnp.zeros_like(gram_ref)

            def advance(index, carry, step=step, scale=scale, last=last):
                here = pl.ds(pl.multiple_of(index * chunk, chunk), chunk)
                old = rows_ref[here]
                new = scale * (newton_one * old.astype(jnp.float32) + low_dot(old, change_ref[...]))
                if last:
                    @pl.when(index == 0)
                    def _():
                        out_ref[...] = new[:row_count]
                new = new.astype(bf)
                if not last:
                    rows_ref[here] = new
                gram_ref[...] += contract_rows(new, new)
                return carry

            lax.fori_loop(0, part_count * chunks, advance, 0)
        else:
            rows = out_ref[...]
            out_ref[...] = newton_one * rows + low_dot(rows.astype(bf), change_ref[...])
            if step < 4:
                gram_ref[...] = newton_one * gram_ref[...] + low_dot(low_ref[...], change_ref[...])
                low_ref[...] = gram_ref[...].astype(bf)
                gram_ref[...] = newton_one * gram_ref[...] + low_dot(low_ref[...], change_ref[...])

def orthogonal_rows(moments, grads, factor, row_count, chunk, full_steps):
    count, (part_rows, width) = len(moments), moments[0].shape
    body = functools.partial(orthogonal_kernel, count, chunk, full_steps, row_count)
    flops = 2 * width * width * (count * part_rows * (2 * full_steps + 1) + 9 * width)
    return pl.pallas_call(
        body,
        out_shape=jax.ShapeDtypeStruct((row_count, width), jnp.float32),
        in_specs=[pl.BlockSpec(memory_space=pltpu.SMEM)]
        + [pl.BlockSpec(memory_space=pl.ANY)] * (2 * count),
        out_specs=pl.BlockSpec(memory_space=pltpu.VMEM),
        scratch_shapes=[
            pltpu.VMEM((count * part_rows if full_steps else 16, width), jnp.bfloat16),
            pltpu.VMEM((width, width), jnp.float32),
            pltpu.VMEM((width, width), jnp.bfloat16),
            pltpu.VMEM((width, width), jnp.bfloat16),
            pltpu.VMEM((count * part_rows // chunk, chunk, width), jnp.bfloat16),
            pltpu.VMEM((count * part_rows // chunk, chunk, width), jnp.bfloat16),
            pltpu.SemaphoreType.DMA((2, count * part_rows // chunk)),
        ],
        compiler_params=pltpu.CompilerParams(vmem_limit_bytes=48 * 1024 * 1024),
        cost_estimate=pl.CostEstimate(flops=flops, bytes_accessed=4 * count * part_rows * width, transcendentals=0),
        name="orthogonal_rows",
    )(factor.reshape(1, 1), *moments, *grads)


def adam_step(weight, first_moment, second_moment, gradient, step_rate):
    first_moment = adam_first * first_moment + (1.0 - adam_first) * gradient
    second_moment = adam_second * second_moment + (1.0 - adam_second) * gradient * gradient
    first_hat = first_moment / (1.0 - adam_first**STEP)
    second_hat = second_moment / (1.0 - adam_second**STEP)
    weight = weight * (1.0 - step_rate * decay_rate) - step_rate * first_hat / (
        jnp.sqrt(second_hat) + 1e-08
    )
    return (weight, first_moment, second_moment)


def on_device(
    patches,
    image_ids,
    patch_place,
    labels,
    attn_w,
    mlp_w,
    embed_w,
    vec_w,
    head_w,
    attn_mom,
    mlp_mom,
    embed_m,
    embed_v,
    vec_m,
    vec_v,
    head_m,
    head_v,
):
    groups = lax.axis_size("cls")
    owners = lax.axis_size("dp")
    count = groups * owners
    top = count.bit_length() - 1
    low_bits = groups.bit_length() - 1
    member_index = lax.axis_index("cls")
    owner_index = lax.axis_index("dp")
    me = owner_index * groups + member_index
    core = me & 1
    model_width = vec_w.shape[1]
    slot_count = labels.shape[1]
    high_bits = list(range(top - 1, 2, -1))
    third, fourth, pair = (2, 4), (4, 2), (1, 1)
    third_mine = jnp.where(core == 0, third[0], third[1])
    fourth_mine = jnp.where(core == 0, fourth[0], fourth[1])

    def exchange(value, masks, what="small"):
        with jax.named_scope(what):
            return swap(value, count, masks)

    def plain(bit):
        return (1 << bit,) * 2

    def bit_of(bit):
        return (me >> bit) & 1

    def lane(steps, what):
        return Lane(steps, exchange, what)

    def of_core(value):
        left, right = value[:, :model_width], value[:, model_width:]
        return jnp.where(core == 0, left, right), jnp.where(core == 0, right, left)

    attn_rows, embed_rows, mlp_rows = attn_w.shape[0], embed_w.shape[0], mlp_w.shape[0]
    up_stages = [plain(bit) for bit in high_bits]
    down_stages = up_stages[::-1]

    def ordered_weights(block):
        for axis, bit in enumerate(high_bits):
            block = ordered_pair(bit_of(bit), block, (yield block, plain(bit)), axis)
        block = block.reshape(-1, attn_rows + embed_rows, model_width)
        block = jnp.stack([block, (yield block, third)])
        block = jnp.concatenate([block, (yield block, fourth)], axis=0)
        return block, (yield block, pair)

    sibling = me ^ 1
    places = [
        me,
        me ^ third_mine,
        me ^ fourth_mine,
        me ^ 6,
        sibling,
        sibling ^ fourth_mine,
        sibling ^ third_mine,
        sibling ^ 6,
    ]
    attn_lane = lane(
        ordered_weights(jnp.concatenate([attn_w, embed_w], axis=0).astype(jnp.bfloat16)),
        "attn_weights",
    )
    mlp_lane = lane(
        collecting(mlp_w.astype(jnp.bfloat16)[None], up_stages + [third]), "mlp_weights"
    )
    for _ in high_bits:
        sync((), attn_lane)
    sync((), attn_lane, mlp_lane)
    sync((), attn_lane, mlp_lane)

    shard_rows, shard_width = head_w.shape
    chunk = -(-shard_width // (owners * 128)) * 128
    padding = owners * chunk - shard_width
    owner_bits = list(range(low_bits, top))

    def transposed(value, order):
        value = value.reshape((2,) * len(owner_bits) + value.shape[1:])
        for bit in order:
            axis = top - 1 - bit
            mine = bit_of(bit)
            stay, leave = pick(value, mine, axis), pick(value, 1 - mine, axis)
            value = ordered_pair(mine, stay, (yield leave, plain(bit)), axis)
        return value.reshape((owners,) + value.shape[len(owner_bits) :])

    head_low = jnp.pad(head_w.astype(jnp.bfloat16), ((0, 0), (0, padding)))
    head_low = head_low.reshape(shard_rows, owners, chunk).transpose(1, 0, 2)
    head_lane = lane(transposed(head_low, owner_bits[1:] + owner_bits[:1]), "head")

    def of_chip():
        value = mlp_mom.astype(jnp.bfloat16)
        mine, leave = of_core(value)
        rows = jnp.stack([mine, (yield leave, pair)])
        return (yield from collecting(rows, up_stages + [third, fourth]))

    mom_lane = lane(of_chip(), "mlp_moments")
    attn_mom_lane = lane(
        collecting(attn_mom.astype(jnp.bfloat16)[None], up_stages[2:] + [third, fourth, pair]),
        "attn_moments",
    )
    sync((), attn_lane, mlp_lane, head_lane)
    pieces, others = finish(attn_lane)[0]
    attn_b = jnp.zeros((count // 8, 8, attn_rows, model_width), jnp.bfloat16)
    embed_b = jnp.zeros((count // 8, 8, embed_rows, model_width), jnp.bfloat16)
    for index, place in enumerate(places):
        piece = (pieces if index < 4 else others)[index % 4]
        attn_b = lax.dynamic_update_slice_in_dim(attn_b, piece[:, None, :attn_rows], place & 7, 1)
        embed_b = lax.dynamic_update_slice_in_dim(embed_b, piece[:, None, attn_rows:], place & 7, 1)
    attn_b = attn_b.reshape(count * attn_rows, model_width)
    embed_b = embed_b.reshape(count * embed_rows, model_width)

    attn_b, embed_b = sync((attn_b, embed_b), mlp_lane, head_lane)
    part_a = jnp.concatenate(finish(mlp_lane)[0], axis=0)

    def once(value, stage):
        return (yield value, stage)

    b_lane = lane(once(part_a, fourth), "mlp_weights")
    c_lane = lane(once(part_a, pair), "mlp_weights")
    sync((), b_lane)
    sync((), c_lane)
    image_index = lax.dynamic_index_in_dim(image_ids, member_index, 0, keepdims=False)
    my_labels = lax.dynamic_index_in_dim(labels, member_index, 0, keepdims=False)
    position = patch_place[0]
    patch_dim = patches.shape[1]
    grid_size = (embed_b.shape[0] - patch_dim) // 2
    grid_index = jnp.arange(grid_size)
    places_hot = [(position[axis][:, None] == grid_index[None]).astype(jnp.bfloat16) for axis in (0, 1)]
    patch_wide = jnp.concatenate([patches] + places_hot, axis=1)
    embedded = low_dot(patch_wide, embed_b) + vec_w[10]
    normed, queries, key_rows, values = projections(attn_b, vec_w, embedded)
    mixed_out, summary = mixing(queries, key_rows, values, image_index, H)
    (mixed_out,) = sync((mixed_out,), c_lane, mom_lane)
    part_c = c_lane.result

    masks = [1 << bit for bit in high_bits]
    own_codes = [jnp.array(codes(masks + [third[c], fourth[c]]), jnp.int32) for c in (0, 1)]
    arrival = me ^ jnp.where(
        core == 0,
        jnp.concatenate([own_codes[0], own_codes[1] ^ 1]),
        jnp.concatenate([own_codes[1], own_codes[0] ^ 1]),
    )
    first_bias = jnp.take(vec_w[11:].reshape(count, mlp_rows), arrival, axis=0)
    first_bias = first_bias.reshape(4, -1)

    middle = embedded + low_dot(mixed_out, attn_b[3 * model_width :]) + vec_w[2]
    normed_two = layer_norm(middle, vec_w[6], vec_w[7]).astype(jnp.bfloat16)
    final_rows, active_even, slope_even = hidden_forward(
        normed_two, middle + vec_w[3], first_bias[::2], [part_a.reshape(-1, 2 * model_width), part_c.reshape(-1, 2 * model_width)]
    )
    final_rows, slope_even = sync((final_rows, slope_even), b_lane, head_lane)
    part_b = b_lane.result
    d_lane = lane(once(part_b, pair), "mlp_weights")
    sync((), d_lane)
    (final_rows,) = sync((final_rows,), d_lane, mom_lane, attn_mom_lane)
    mlp_parts = [
        part.reshape(-1, 2 * model_width) for part in (part_a, part_b, part_c, d_lane.result)
    ]
    final_rows, active_odd, slope_odd = hidden_forward(
        normed_two, final_rows, first_bias[1::2], mlp_parts[1::2]
    )
    active, slope = (active_even, active_odd), (slope_even, slope_odd)
    (final_rows,) = sync(
        (final_rows,), head_lane, mom_lane, attn_mom_lane, hold=(mom_lane, attn_mom_lane)
    )
    closing, close_pull = jax.vjp(layer_norm, final_rows, vec_w[8], vec_w[9])
    member = (image_index[None, :] == jnp.arange(slot_count)[:, None]).astype(jnp.float32)
    slot_sizes = jnp.sum(member, axis=1)
    divisor = jnp.maximum(slot_sizes, 1.0)[:, None]
    pooled = product(member, closing) / divisor
    facts = jnp.stack(
        [(slot_sizes > 0.5).astype(jnp.int32), my_labels // 256, my_labels % 256], axis=1
    )
    facts = jnp.pad(facts, ((0, 0), (0, 125))).astype(jnp.bfloat16)
    block = jnp.concatenate([pooled.astype(jnp.bfloat16), facts], axis=1)
    head_b = finish(head_lane)[0].reshape(owners * shard_rows, chunk)
    for axis, bit in enumerate(range(top - 1, -1, -1)):
        block = ordered_pair(bit_of(bit), block, exchange(block, plain(bit), "pooled"), axis)
    block = block.reshape(count * slot_count, -1)
    all_pooled = block[:, :model_width]
    facts = block[:, model_width : model_width + 3].astype(jnp.int32)
    valid = facts[:, 0] > 0
    all_labels = facts[:, 1] * 256 + facts[:, 2]
    image_total = jnp.sum(valid.astype(jnp.float32))

    logits = low_dot(all_pooled, head_b)
    within = owner_index * chunk + jnp.arange(chunk)
    columns = member_index * shard_width + within
    usable = (within < shard_width) & (columns < CLASSES)
    logits = jnp.where(usable[None], logits, -1e30)
    onehot = (usable[None] & (columns[None, :] == all_labels[:, None])).astype(jnp.float32)
    row_max = jnp.max(logits, axis=1)
    exp_sums = jnp.sum(jnp.exp(logits - row_max[:, None]), axis=1)
    stats = jnp.stack([row_max, exp_sums, jnp.sum(onehot * logits, axis=1)])
    for bit in range(top):
        other = exchange(stats, plain(bit), "stats")
        lower = jnp.where(bit_of(bit) == 0, stats, other)
        upper = jnp.where(bit_of(bit) == 0, other, stats)
        row_max = jnp.maximum(lower[0], upper[0])
        exp_sums = lower[1] * jnp.exp(lower[0] - row_max) + upper[1] * jnp.exp(upper[0] - row_max)
        stats = jnp.stack([row_max, exp_sums, lower[2] + upper[2]])
    normaliser = stats[0] + jnp.log(stats[1])
    loss_sum = jnp.sum(jnp.where(valid, normaliser - stats[2], 0.0))
    probs_class = jnp.exp(logits - normaliser[:, None])
    d_logits = (jnp.where(valid[:, None], probs_class - onehot, 0.0) / image_total).astype(
        jnp.bfloat16
    )
    d_pooled = contract_cols(d_logits, head_b)
    d_pooled = d_pooled.reshape((2,) * top + (slot_count, model_width))
    for bit in range(top):
        axis = top - 1 - bit
        mine = bit_of(bit)
        leave = pick(d_pooled, 1 - mine, axis).astype(jnp.bfloat16)
        d_pooled = pick(d_pooled, mine, axis) + exchange(leave, plain(bit), "d_pooled").astype(
            jnp.float32
        )
    d_closing = product(member.T, d_pooled / divisor)
    d_final, g_gain_final, g_shift_final = close_pull(d_closing)
    d_out = d_final.astype(jnp.bfloat16)
    g_second_bias = jnp.sum(d_out.astype(jnp.float32), axis=0)
    d_out, all_pooled = tie(d_out, all_pooled)
    head_grad = contract_rows(all_pooled, d_logits)
    head_squares = jnp.sum(head_grad * head_grad) / model_width
    head_lane = lane(
        transposed(
            head_grad.astype(jnp.bfloat16).reshape(owners, shard_rows, chunk),
            owner_bits[1:-1] + owner_bits[:1] + owner_bits[-1:],
        ),
        "head_grads",
    )
    (d_out,) = sync((d_out,), mom_lane, attn_mom_lane)

    d_hidden, bias_grads, away = hidden_back(core, d_out, normed_two, active, slope, mlp_parts)
    (away, d_hidden) = sync((away, d_hidden), mom_lane, attn_mom_lane)
    arrived = exchange(away, pair, "mlp_grads")
    operands = (core, d_out, normed_two, active, d_hidden)
    first_plan = ((1, None, (2, 0)), (3, 1, (1,)), (2, 1, (3,)))
    second_plan = ((0, None, (2, 0)), (3, 0, (1,)), (2, 0, (3,)))
    leave = kept_grads(first_plan, *operands, arrived)
    leave, arrived, d_hidden = sync(
        (leave, arrived, d_hidden), attn_mom_lane
    )
    operands = (core, d_out, normed_two, active, d_hidden)

    def summing(leave, kept):
        far = yield leave, fourth
        summed = kept() + far.astype(jnp.float32)
        arrived = yield summed[:model_width].astype(jnp.bfloat16), third
        kept = summed[model_width:] + arrived.astype(jnp.float32)
        kept = kept.reshape(2, -1, mlp_rows, model_width)
        for stage in down_stages:
            half = kept.shape[1] // 2
            arrived = yield kept[:, half:].astype(jnp.bfloat16), stage
            kept = kept[:, :half] + arrived.astype(jnp.float32)
        return kept[:, 0]

    own = []
    mlp_lane = lane(summing(leave, lambda: own[0]), "mlp_grads")
    sync((), mlp_lane)
    d_normed_two, grads = kept_grads(second_plan, *operands, arrived, mlp_parts)
    own.append(grads)
    (d_normed_two,) = sync((d_normed_two,), head_lane)

    d_mid_norm, g_gain_two, g_shift_two = jax.vjp(layer_norm, middle, vec_w[6], vec_w[7])[1](
        d_normed_two
    )
    d_middle = d_final + d_mid_norm
    d_proj = d_middle.astype(jnp.bfloat16)
    g_out_bias = jnp.sum(d_proj.astype(jnp.float32), axis=0)
    d_mixed = contract_cols(d_proj, attn_b[3 * model_width :]).astype(jnp.bfloat16)
    d_queries, d_keys, d_values = mixing_grads(
        queries, key_rows, values, d_mixed, summary, image_index, H
    )
    d_queries, d_keys, d_values, own[0] = sync(
        (d_queries, d_keys, d_values, own[0]),
        mlp_lane,
        mom_lane,
        head_lane,
        hold=(mom_lane, head_lane),
    )
    attn_grad = jnp.concatenate(
        [
            contract_rows(normed, d_queries),
            contract_rows(normed, d_keys),
            contract_rows(normed, d_values),
            contract_rows(mixed_out, d_proj),
        ],
        axis=0,
    )

    quarter = (me >> 1) & 3
    to_third, to_fourth = third_mine >> 1, fourth_mine >> 1

    def quartered(grad, rows):
        grad = grad.reshape(count // 8, 4, 2, rows, model_width)
        leave = pick(grad, 1 - core, 2).astype(jnp.bfloat16)
        grad = pick(grad, core, 2) + (yield leave, pair).astype(jnp.float32)
        leave = [pick(grad, quarter ^ to_fourth, 1), pick(grad, quarter ^ 3, 1)]
        leave = (yield jnp.stack(leave).astype(jnp.bfloat16), fourth).astype(jnp.float32)
        leaving = pick(grad, quarter ^ to_third, 1) + leave[1]
        return pick(grad, quarter, 1) + leave[0], leaving

    def last_sums(grads):
        grad = jnp.concatenate([one[0] for one in grads], axis=1)
        leave = jnp.concatenate([one[1].astype(jnp.bfloat16) for one in grads], axis=1)
        grad = grad + (yield leave, third).astype(jnp.float32)
        grad = grad.reshape((2,) * len(high_bits) + grad.shape[1:])
        for bit in reversed(high_bits):
            axis = top - 1 - bit
            mine = bit_of(bit)
            leave = pick(grad, 1 - mine, axis).astype(jnp.bfloat16)
            grad = pick(grad, mine, axis) + (yield leave, plain(bit)).astype(jnp.float32)
        return grad

    attn_lane = lane(quartered(attn_grad, attn_rows), "attn_grads")
    d_normed = (
        contract_cols(d_queries, attn_b[:model_width])
        + contract_cols(d_keys, attn_b[model_width : 2 * model_width])
        + contract_cols(d_values, attn_b[2 * model_width : 3 * model_width])
    )
    sync((), attn_lane)
    (d_normed,) = sync((d_normed,), mlp_lane, attn_lane, head_lane)
    d_emb_norm, g_gain_one, g_shift_one = jax.vjp(layer_norm, embedded, vec_w[4], vec_w[5])[1](
        d_normed
    )
    d_embed_low = (d_middle + d_emb_norm).astype(jnp.bfloat16)
    embed_grad = contract_rows(patch_wide, d_embed_low)
    embed_lane = lane(quartered(embed_grad, embed_rows), "embed_grads")
    sync((), embed_lane)
    sync((), embed_lane, mlp_lane, head_lane, hold=(head_lane,))
    finish(attn_lane, embed_lane)
    sum_lane = lane(last_sums([attn_lane.result, embed_lane.result]), "last_grads")
    sync((), sum_lane)
    mlp_grad = finish(mlp_lane)[0]
    all_lane = lane(
        collecting(mlp_grad.astype(jnp.bfloat16), up_stages + [third, fourth]), "mlp_grads_all"
    )
    sync((), all_lane)
    sync((), sum_lane, all_lane, mom_lane)
    sync((), sum_lane, all_lane)
    while sum_lane.result is None:
        sync((), sum_lane, all_lane, mom_lane, hold=(all_lane,))
    attn_sum, embed_sum = sum_lane.result[:attn_rows], sum_lane.result[attn_rows:]
    g_query_bias = jnp.sum(d_queries.astype(jnp.float32), axis=0)
    g_value_bias = jnp.sum(d_values.astype(jnp.float32), axis=0)
    g_patch_bias = jnp.sum(d_embed_low.astype(jnp.float32), axis=0)
    g_first_bias = jnp.take(bias_grads.reshape(count, mlp_rows), jnp.argsort(arrival), axis=0)
    vec_grad = jnp.concatenate(
        [
            jnp.stack(
                [
                    g_query_bias,
                    g_value_bias,
                    g_out_bias,
                    g_second_bias,
                    g_gain_one,
                    g_shift_one,
                    g_gain_two,
                    g_shift_two,
                    g_gain_final,
                    g_shift_final,
                    g_patch_bias,
                ]
            ),
            g_first_bias.reshape(-1, model_width),
        ],
        axis=0,
    )
    local_squares = sum(
        jnp.sum(grad * grad, axis=0) for grad in (attn_sum, embed_sum, mlp_grad[0], mlp_grad[1])
    )
    small_sums = jnp.concatenate([vec_grad, (local_squares + head_squares)[None]], axis=0)

    def total(value):
        for bit in [1, 2, 0] + list(range(3, top)):
            value = value + (yield value, plain(bit))
        return value

    small_lane = lane(total(small_sums), "small_sums")
    block_lane = lane(
        collecting(attn_sum.astype(jnp.bfloat16)[None], up_stages[2:] + [third, fourth, pair]),
        "attn_grads_all",
    )
    sync((), small_lane, block_lane)
    sync((), small_lane, block_lane)
    sync((), small_lane, block_lane, all_lane)
    small_sums, attn_grads = finish(small_lane, block_lane)
    attn_moms = jnp.concatenate(finish(attn_mom_lane)[0], axis=0).reshape(-1, model_width)
    attn_grads = jnp.concatenate(attn_grads, axis=0).reshape(-1, model_width)
    vec_sum = small_sums[:-1]
    grad_norm = jnp.sqrt(jnp.sum(small_sums[-1]) + jnp.sum(vec_sum * vec_sum))
    factor = jnp.minimum(1.0, clip_limit / (grad_norm + 1e-06))
    attn_mom_out = momentum_keep * attn_mom + factor * attn_sum
    mine, away = mlp_grad[0], exchange(mlp_grad[1], pair)
    mlp_sum = jnp.concatenate(
        [jnp.where(core == 0, mine, away), jnp.where(core == 0, away, mine)], axis=1
    )
    mlp_mom_out = momentum_keep * mlp_mom + factor * mlp_sum

    (factor,) = sync((factor,), head_lane)
    attn_dir = orthogonal_rows([attn_moms], [attn_grads], factor, attn_rows, 768, 4)
    (attn_dir,) = sync((attn_dir,), all_lane, mom_lane)
    mlp_grads, mlp_moms = finish(all_lane, mom_lane)
    mlp_result = orthogonal_rows(
        [part.reshape(-1, model_width) for part in mlp_moms],
        [part.reshape(-1, model_width) for part in mlp_grads],
        factor,
        2 * mlp_rows,
        768,
        0,
    )
    (mlp_result,) = sync((mlp_result,), head_lane)
    mlp_other = exchange(mlp_result[mlp_rows:], pair)
    mlp_result = mlp_result[:mlp_rows]
    mlp_dir = jnp.concatenate(
        [
            jnp.where(core == 0, mlp_result, mlp_other),
            jnp.where(core == 0, mlp_other, mlp_result),
        ],
        axis=1,
    )
    head_grad = finish(head_lane)[0].transpose(1, 0, 2)
    head_grad = head_grad.reshape(shard_rows, owners * chunk)[:, :shard_width].astype(jnp.float32)
    mlp_scale = math.sqrt(mlp_rows * count / model_width)
    attn_out = attn_w * (1.0 - muon_rate * decay_rate) - muon_rate * attn_dir
    mlp_out = mlp_w * (1.0 - muon_rate * decay_rate) - muon_rate * mlp_scale * mlp_dir
    embed_out, embed_m_out, embed_v_out = adam_step(
        embed_w, embed_m, embed_v, factor * embed_sum, adam_rate
    )
    vec_out, vec_m_out, vec_v_out = adam_step(vec_w, vec_m, vec_v, factor * vec_sum, vector_rate)
    head_out, head_m_out, head_v_out = adam_step(
        head_w, head_m, head_v, factor * head_grad, adam_rate
    )
    return (
        loss_sum,
        image_total,
        grad_norm,
        attn_out,
        attn_mom_out,
        attn_out.astype(jnp.bfloat16),
        mlp_out,
        mlp_mom_out,
        mlp_out.astype(jnp.bfloat16),
        embed_out,
        embed_m_out,
        embed_v_out,
        embed_out.astype(jnp.bfloat16),
        vec_out,
        vec_m_out,
        vec_v_out,
        vec_out.astype(jnp.bfloat16),
        head_out,
        head_m_out,
        head_v_out,
        head_out.astype(jnp.bfloat16),
    )


def solution(mesh):
    return jax.shard_map(
        on_device,
        mesh=mesh,
        in_specs=(
            P(("dp", "cls"), None),
            P("dp", None),
            P(("dp", "cls"), None, None),
            P("dp", None),
            P(("dp", "cls"), None),
            P(("dp", "cls"), None),
            P(("dp", "cls"), None),
            P(),
            P("dp", "cls"),
            P(("dp", "cls"), None),
            P(("dp", "cls"), None),
            P(("dp", "cls"), None),
            P(("dp", "cls"), None),
            P(),
            P(),
            P("dp", "cls"),
            P("dp", "cls"),
        ),
        out_specs=(
            P(),
            P(),
            P(),
            P(("dp", "cls"), None),
            P(("dp", "cls"), None),
            P(("dp", "cls"), None),
            P(("dp", "cls"), None),
            P(("dp", "cls"), None),
            P(("dp", "cls"), None),
            P(("dp", "cls"), None),
            P(("dp", "cls"), None),
            P(("dp", "cls"), None),
            P(("dp", "cls"), None),
            P(),
            P(),
            P(),
            P(),
            P("dp", "cls"),
            P("dp", "cls"),
            P("dp", "cls"),
            P("dp", "cls"),
        ),
        check_vma=False,
    )
```

```python
import functools
import math

import jax
import jax.numpy as jnp
from jax import lax
from jax.experimental import pallas as pl
from jax.experimental.pallas import tpu as pltpu
from jax.sharding import PartitionSpec as P

H = 12
CLASSES = 21843
STEP = 10


highest = lax.Precision.HIGHEST
newton_one = 3.4445
newton_two = -4.775
newton_three = 2.0315
clip_limit = 0.05
muon_rate = 0.3
decay_rate = 0.05
adam_rate = 0.01
vector_rate = 0.05
momentum_keep = 0.5
adam_first = 0.5
adam_second = 0.999


AXES = ("dp", "cls")


def swap(value, count, masks):
    return lax.ppermute(value, AXES, [(i, i ^ masks[i & 1]) for i in range(count)])


def pick(value, index, axis):
    return lax.dynamic_index_in_dim(value, index, axis, keepdims=False)


def codes(masks):
    found = [0]
    for mask in masks:
        found = found + [code ^ mask for code in found]
    return found


def ordered_pair(bit, mine, other, axis):
    return jnp.where(
        bit == 0, jnp.stack([mine, other], axis=axis), jnp.stack([other, mine], axis=axis)
    )


def product(left_side, right_side):
    return jnp.dot(left_side, right_side, precision=highest)


def low_dot(left_side, right_side):
    return jnp.dot(left_side, right_side, preferred_element_type=jnp.float32)


def contract_rows(left_side, right_side):
    return lax.dot_general(
        left_side, right_side, (((0,), (0,)), ((), ())), preferred_element_type=jnp.float32
    )


def contract_cols(left_side, right_side):
    return lax.dot_general(
        left_side, right_side, (((1,), (1,)), ((), ())), preferred_element_type=jnp.float32
    )


def layer_norm(inputs, gain_row, shift_row):
    mean_row = jnp.mean(inputs, axis=-1, keepdims=True)
    centred = inputs - mean_row
    variance = jnp.mean(centred * centred, axis=-1, keepdims=True)
    return centred * lax.rsqrt(variance + 1e-06) * gain_row + shift_row


def tie(*values):
    return lax.optimization_barrier(values)


class Lane:
    def __init__(self, steps, exchange, what):
        self.steps, self.exchange, self.what = steps, exchange, what
        self.moving, self.result = False, None
        self.value, self.masks = next(steps)

    def advance(self, value, start):
        masks = self.masks
        if self.moving:
            try:
                value, masks = self.steps.send(value)
            except StopIteration as end:
                self.value, self.result, self.moving = None, end.value, False
                return
            if not start:
                self.value, self.masks, self.moving = value, masks, False
                return
        self.moving = True
        self.value, self.masks = self.exchange(value, masks, self.what), masks


def sync(values, *lanes, hold=()):
    lanes = [lane for lane in lanes if lane.result is None]
    tied = tie(*values, *[lane.value for lane in lanes])
    for lane, value in zip(lanes, tied[len(values) :]):
        lane.advance(value, lane not in hold)
    return tied[: len(values)]


def finish(*lanes):
    while any(lane.result is None for lane in lanes):
        sync((), *lanes)
    return [lane.result for lane in lanes]


def collecting(value, stages):
    for stage in stages[:-1]:
        value = jnp.concatenate([value, (yield value, stage)], axis=0)
    return [value, (yield value, stages[-1])]


def gelu_with_slope(value):
    size = jnp.abs(value)
    bell = jnp.exp(-0.5 * value * value)
    t = 1.0 / (1.0 + (0.3275911 * 0.7071067811865476) * size)
    poly = 1.061405429
    for term in (-1.453152027, 1.421413741, -0.284496736, 0.254829592):
        poly = poly * t + term
    tail = 0.5 * poly * t * bell
    share = jnp.where(value < 0, tail, 1.0 - tail)
    return value * share, share + value * (0.3989422804014327 * bell)


def projections(attn_b, vec_w, embedded):
    model_width = attn_b.shape[1]
    normed = layer_norm(embedded, vec_w[4], vec_w[5]).astype(jnp.bfloat16)
    queries = (low_dot(normed, attn_b[:model_width]) + vec_w[0]).astype(jnp.bfloat16)
    key_rows = low_dot(normed, attn_b[model_width : 2 * model_width]).astype(jnp.bfloat16)
    values = (low_dot(normed, attn_b[2 * model_width : 3 * model_width]) + vec_w[1]).astype(
        jnp.bfloat16
    )
    return (normed, queries, key_rows, values)


def half_of(value, half, width):
    lane = lax.broadcasted_iota(jnp.int32, value.shape, 1)
    keep = (lane >= half * width) & (lane < (half + 1) * width)
    return jnp.where(keep, value, jnp.zeros_like(value))


def mixing_kernel(width, rows, ids_down_ref, ids_ref, q_ref, k_ref, v_ref, out_ref, summary_ref, seen_ref):
    step = pl.program_id(0)
    pack = q_ref.shape[1] // width
    keys = [half_of(k_ref[...], half, width) for half in range(pack)]
    values = [half_of(v_ref[...], half, width) for half in range(pack)]
    scale = width ** (-0.5)
    lane = lax.broadcasted_iota(jnp.int32, (rows, seen_ref.shape[1]), 1)
    for start in range(0, q_ref.shape[0], rows):
        here = pl.ds(start, rows)
        same = ids_down_ref[here] == ids_ref[...]
        queries = q_ref[here]
        seen = seen_ref[here]
        total = None
        for half in range(pack):
            scores = jnp.where(same, contract_cols(queries, keys[half]) * scale, -1e30)
            top = jnp.max(scores, axis=1, keepdims=True)
            exponents = jnp.exp(scores - top)
            sums = jnp.sum(exponents, axis=1, keepdims=True)
            probs = (exponents * (1.0 / sums)).astype(jnp.bfloat16)
            mixed = low_dot(probs, values[half])
            total = mixed if total is None else total + mixed
            seen = jnp.where(lane == step * pack + half, top + jnp.log(sums), seen)
        out_ref[here] = total.astype(out_ref.dtype)
        seen_ref[here] = seen

    @pl.when(step == pl.num_programs(0) - 1)
    def _():
        summary_ref[...] = seen_ref[...].T[: summary_ref.shape[0]]


def mixing(queries, key_rows, values, image_index, heads, rows=256):
    token_count, model_width = queries.shape
    width = model_width // heads
    pack = 128 // width
    tile = pl.BlockSpec((token_count, 128), lambda step: (0, step))

    def whole(shape):
        return pl.BlockSpec(shape, lambda step: (0, 0))

    kept = -(-heads // 8) * 8
    return pl.pallas_call(
        functools.partial(mixing_kernel, width, rows),
        grid=(heads // pack,),
        out_shape=(
            jax.ShapeDtypeStruct((token_count, model_width), jnp.bfloat16),
            jax.ShapeDtypeStruct((kept, token_count), jnp.float32),
        ),
        in_specs=[whole((token_count, 1)), whole((1, token_count)), tile, tile, tile],
        out_specs=(tile, whole((kept, token_count))),
        scratch_shapes=[pltpu.VMEM((token_count, 128), jnp.float32)],
        compiler_params=pltpu.CompilerParams(vmem_limit_bytes=32 * 1024 * 1024),
        cost_estimate=pl.CostEstimate(
            flops=4 * token_count * token_count * model_width,
            bytes_accessed=8 * token_count * model_width,
            transcendentals=heads * token_count * token_count,
        ),
        name="mixing",
    )(image_index[:, None], image_index[None, :], queries, key_rows, values)


def mixing_grads_kernel(width, rows, ids_down_ref, ids_ref, summary_ref, q_ref, k_ref, v_ref, d_ref, dq_ref, dk_ref, dv_ref):
    step = pl.program_id(0)
    pack = q_ref.shape[1] // width
    scale = width ** (-0.5)
    keys = [half_of(k_ref[...], half, width) for half in range(pack)]
    values = [half_of(v_ref[...], half, width) for half in range(pack)]
    key_sums, value_sums = 0.0, 0.0
    for start in range(0, q_ref.shape[0], rows):
        here = pl.ds(start, rows)
        same = ids_down_ref[...] == ids_ref[:, here]
        query_sum = 0.0
        for half in range(pack):
            queries, d_mixed = half_of(q_ref[here], half, width), half_of(d_ref[here], half, width)
            scores = contract_cols(keys[half], queries) * scale
            summary = summary_ref[pl.ds(step * pack + half, 1), here]
            probs = jnp.where(same, jnp.exp(jnp.where(same, scores - summary, -1e30)), 0.0)
            d_probs = contract_cols(values[half], d_mixed)
            product = probs * d_probs
            d_scores = product - probs * jnp.sum(product, axis=0, keepdims=True)
            d_scores = d_scores.astype(jnp.bfloat16)
            value_sums = value_sums + low_dot(probs.astype(jnp.bfloat16), d_mixed)
            key_sums = key_sums + low_dot(d_scores, queries)
            query_sum = query_sum + contract_rows(d_scores, keys[half])
        dq_ref[here] = (query_sum * scale).astype(dq_ref.dtype)
    dk_ref[...] = (key_sums * scale).astype(dk_ref.dtype)
    dv_ref[...] = value_sums.astype(dv_ref.dtype)


def mixing_grads(queries, key_rows, values, d_mixed, summary, image_index, heads, rows=256):
    token_count, model_width = queries.shape
    width = model_width // heads
    pack = 128 // width
    tile = pl.BlockSpec((token_count, 128), lambda step: (0, step))

    def whole(shape):
        return pl.BlockSpec(shape, lambda step: (0, 0))

    return pl.pallas_call(
        functools.partial(mixing_grads_kernel, width, rows),
        grid=(heads // pack,),
        out_shape=(jax.ShapeDtypeStruct((token_count, model_width), jnp.bfloat16),) * 3,
        in_specs=[whole((token_count, 1)), whole((1, token_count)), whole(summary.shape)] + [tile] * 4,
        out_specs=(tile,) * 3,
        compiler_params=pltpu.CompilerParams(vmem_limit_bytes=32 * 1024 * 1024),
        cost_estimate=pl.CostEstimate(
            flops=10 * token_count * token_count * model_width,
            bytes_accessed=14 * token_count * model_width,
            transcendentals=heads * token_count * token_count,
        ),
        name="mixing_grads",
    )(image_index[:, None], image_index[None, :], summary, queries, key_rows, values, d_mixed)


IN_VMEM = pl.BlockSpec(memory_space=pltpu.VMEM)
IN_SMEM = pl.BlockSpec(memory_space=pltpu.SMEM)
ANYWHERE = pl.BlockSpec(memory_space=pl.ANY)


def hidden_forward_kernel(rows, normed_ref, middle_ref, bias_ref, *refs):
    part_refs = refs[:-3]
    final_ref, active_ref, slope_ref = refs[-3:]
    width = normed_ref.shape[1]

    def block(step, carry):
        here = pl.ds(pl.multiple_of(step * rows, rows), rows)
        normed = normed_ref[here]
        total = middle_ref[here]
        for index, part_ref in enumerate(part_refs):
            hidden = contract_cols(normed, part_ref[:, :width]) + bias_ref[pl.ds(index, 1)]
            active, slope = gelu_with_slope(hidden)
            active = active.astype(jnp.bfloat16)
            active_ref[index, here] = active
            slope_ref[index, here] = slope
            total = total + low_dot(active, part_ref[:, width:])
        final_ref[here] = total
        return carry

    lax.fori_loop(0, normed_ref.shape[0] // rows, block, 0)


def hidden_forward(normed, middle, bias, parts, rows=256):
    token_count, width = normed.shape
    count = len(parts)
    return pl.pallas_call(
        functools.partial(hidden_forward_kernel, rows),
        out_shape=(
            jax.ShapeDtypeStruct((token_count, width), jnp.float32),
            jax.ShapeDtypeStruct((count, token_count, width), jnp.bfloat16),
            jax.ShapeDtypeStruct((count, token_count, width), jnp.float32),
        ),
        in_specs=[IN_VMEM] * (3 + count),
        out_specs=(IN_VMEM,) * 3,
        compiler_params=pltpu.CompilerParams(vmem_limit_bytes=48 * 1024 * 1024),
        cost_estimate=pl.CostEstimate(
            flops=4 * count * token_count * width * width,
            bytes_accessed=4 * count * width * width + 8 * count * token_count * width,
            transcendentals=2 * count * token_count * width,
        ),
        name="hidden_forward",
    )(normed, middle, bias, *parts)


def hidden_back_kernel(core_ref, d_out_ref, normed_ref, *refs):
    active_refs, slope_refs, part_refs = refs[:2], refs[2:4], refs[4:8]
    d_hidden_ref, bias_ref, away_ref = refs[8:11]
    weights, actives, slopes, d_hiddens, aways, in_sems, out_sems = refs[11:]
    width = d_out_ref.shape[1]
    half = width // 2
    arriving = []
    for index, part_ref in enumerate(part_refs):
        sources = (
            part_ref.at[:, pl.ds(width, width)],
            slope_refs[index % 2].at[index // 2],
            active_refs[index % 2].at[index // 2],
        )
        copies = [
            pltpu.make_async_copy(source, target.at[index], in_sems.at[which, index])
            for which, (source, target) in enumerate(zip(sources, (weights, slopes, actives)))
        ]
        for copy in copies:
            copy.start()
        arriving.append(copies)
    first = core_ref[0, 0] == 0
    right = jnp.where(first, d_out_ref[...], normed_ref[...])
    slots = ((7, 3), (5, 1), (6, 4), (2, 0))
    leaving = []
    for index in range(4):
        for copy in arriving[index]:
            copy.wait()
        d_active = contract_cols(d_out_ref[...], weights[index])
        d_hidden = (slopes[index] * d_active).astype(jnp.bfloat16)
        d_hiddens[index] = d_hidden
        bias_ref[pl.ds(index, 1)] = jnp.sum(d_hidden.astype(jnp.float32), axis=0, keepdims=True)
        left = jnp.where(first, actives[index], d_hidden)
        grad = contract_rows(left, right).astype(jnp.bfloat16)
        aways[index] = grad
        copies = [
            pltpu.make_async_copy(d_hiddens.at[index], d_hidden_ref.at[index], out_sems.at[2, index])
        ]
        for side, slot in enumerate(slots[index]):
            copies.append(
                pltpu.make_async_copy(
                    aways.at[index, pl.ds(side * half, half)],
                    away_ref.at[pl.ds(slot * half, half)],
                    out_sems.at[side, index],
                )
            )
        for copy in copies:
            copy.start()
        leaving += copies
    for copy in leaving:
        copy.wait()


def hidden_back(core, d_out, normed, active, slope, parts):
    token_count, width = d_out.shape
    kept = (4, token_count, width)
    return pl.pallas_call(
        hidden_back_kernel,
        out_shape=(
            jax.ShapeDtypeStruct(kept, jnp.bfloat16),
            jax.ShapeDtypeStruct((4, width), jnp.float32),
            jax.ShapeDtypeStruct((4 * width, width), jnp.bfloat16),
        ),
        in_specs=[IN_SMEM, IN_VMEM, IN_VMEM] + [ANYWHERE] * 8,
        out_specs=(ANYWHERE, IN_VMEM, ANYWHERE),
        scratch_shapes=[
            pltpu.VMEM((4, width, width), jnp.bfloat16),
            pltpu.VMEM(kept, jnp.bfloat16),
            pltpu.VMEM(kept, jnp.float32),
            pltpu.VMEM(kept, jnp.bfloat16),
            pltpu.VMEM((4, width, width), jnp.bfloat16),
            pltpu.SemaphoreType.DMA((3, 4)),
            pltpu.SemaphoreType.DMA((3, 4)),
        ],
        compiler_params=pltpu.CompilerParams(vmem_limit_bytes=48 * 1024 * 1024),
        cost_estimate=pl.CostEstimate(
            flops=16 * token_count * width * width,
            bytes_accessed=16 * width * width + 32 * token_count * width,
            transcendentals=0,
        ),
        name="hidden_back",
    )(core.reshape(1, 1), d_out, normed, *active, *slope, *parts)


def kept_grads_kernel(
    plan, core_ref, d_out_ref, normed_ref, even_ref, odd_ref, d_hidden_ref, *refs
):
    active_refs = (even_ref, odd_ref)
    width = d_out_ref.shape[1]
    half = width // 2
    first = core_ref[0, 0] == 0
    right = jnp.where(first, normed_ref[...], d_out_ref[...])
    kept_ref = refs[-1]
    arrived_ref = refs[0]
    for index, side, slots in plan:
        columns = slice(None) if side is None else slice(side * half, (side + 1) * half)
        left = jnp.where(
            first,
            d_hidden_ref[index, :, columns],
            active_refs[index % 2][index // 2, :, columns],
        )
        grad = contract_rows(left, right)
        for position, slot in enumerate(slots):
            here = pl.ds(slot * half, half)
            rows = grad[position * half : (position + 1) * half]
            rows = rows + arrived_ref[here].astype(jnp.float32)
            kept_ref[here] = rows.astype(kept_ref.dtype)
    if len(refs) > 2:
        part_refs, total_ref = refs[1:5], refs[5]
        total = low_dot(d_hidden_ref[0], part_refs[0][:, :width])
        for index in range(1, 4):
            total = total + low_dot(d_hidden_ref[index], part_refs[index][:, :width])
        total_ref[...] = total


def kept_grads(plan, core, d_out, normed, active, d_hidden, arrived, parts=()):
    token_count, width = d_out.shape
    grads = jax.ShapeDtypeStruct((2 * width, width), jnp.float32 if parts else jnp.bfloat16)
    back = jax.ShapeDtypeStruct((token_count, width), jnp.float32)
    side = 1 if parts else 0
    arrived_spec = pl.BlockSpec((2 * width, width), lambda step: (side, 0))
    return pl.pallas_call(
        functools.partial(kept_grads_kernel, plan),
        grid=(1,),
        out_shape=(back, grads) if parts else grads,
        in_specs=[IN_SMEM] + [IN_VMEM] * 5 + [arrived_spec] + [IN_VMEM] * len(parts),
        out_specs=(IN_VMEM,) * 2 if parts else IN_VMEM,
        compiler_params=pltpu.CompilerParams(vmem_limit_bytes=48 * 1024 * 1024),
        cost_estimate=pl.CostEstimate(
            flops=4 * token_count * width * width,
            bytes_accessed=8 * width * width + 20 * token_count * width,
            transcendentals=0,
        ),
        name="kept_grads",
    )(core.reshape(1, 1), d_out, normed, *active, d_hidden, arrived, *parts)


def orthogonal_kernel(part_count, chunk, full_steps, row_count, factor_ref, *refs):
    moment_refs, grad_refs = refs[:part_count], refs[part_count : 2 * part_count]
    out_ref, rows_ref, gram_ref, low_ref, change_ref, moments, grads, in_sems = refs[
        2 * part_count :
    ]
    part_rows, width = moment_refs[0].shape
    factor = factor_ref[0, 0]
    chunks = part_rows // chunk
    bf = jnp.bfloat16

    arriving = []
    for index in range(part_count):
        for step in range(chunks):
            here = pl.ds(step * chunk, chunk)
            spot = index * chunks + step
            copies = [
                pltpu.make_async_copy(source.at[here], target.at[spot], in_sems.at[which, spot])
                for which, (source, target) in enumerate(
                    ((moment_refs[index], moments), (grad_refs[index], grads))
                )
            ]
            for copy in copies:
                copy.start()
            arriving.append(copies)
    for spot, copies in enumerate(arriving):
        for copy in copies:
            copy.wait()
        rows = (
            momentum_keep * moments[spot].astype(jnp.float32)
            + factor * grads[spot].astype(jnp.float32)
        ).astype(bf)
        if full_steps:
            rows_ref[pl.ds(spot * chunk, chunk)] = rows
        elif spot == 0:
            out_ref[...] = rows[:row_count].astype(jnp.float32)
        if spot == 0:
            gram_ref[...] = contract_rows(rows, rows)
        else:
            gram_ref[...] += contract_rows(rows, rows)
    gram = gram_ref[...]
    diagonal = lax.broadcasted_iota(jnp.int32, gram.shape, 0) == lax.broadcasted_iota(
        jnp.int32, gram.shape, 1
    )
    trace = jnp.sum(jnp.where(diagonal, gram, 0.0))
    inverse = 1.0 / (jnp.sqrt(jnp.full((1, 1), trace)) + 1e-07)
    gram_ref[...] = gram * (inverse * inverse)
    if not full_steps:
        out_ref[...] = inverse * out_ref[...]
    for step in range(5):
        low_ref[...] = gram_ref[...].astype(bf)
        change_ref[...] = (
            newton_two * gram_ref[...] + newton_three * low_dot(low_ref[...], low_ref[...])
        ).astype(bf)
        if step < full_steps:
            scale = inverse if step == 0 else jnp.ones((1, 1), jnp.float32)
            last = step == full_steps - 1
            if step < 4:
                gram_ref[...] = jnp.zeros_like(gram_ref)

            def advance(index, carry, step=step, scale=scale, last=last):
                here = pl.ds(pl.multiple_of(index * chunk, chunk), chunk)
                old = rows_ref[here]
                new = scale * (newton_one * old.astype(jnp.float32) + low_dot(old, change_ref[...]))
                if last:
                    @pl.when(index == 0)
                    def _():
                        out_ref[...] = new[:row_count]
                new = new.astype(bf)
                if not last:
                    rows_ref[here] = new
                gram_ref[...] += contract_rows(new, new)
                return carry

            lax.fori_loop(0, part_count * chunks, advance, 0)
        else:
            rows = out_ref[...]
            out_ref[...] = newton_one * rows + low_dot(rows.astype(bf), change_ref[...])
            if step < 4:
                gram_ref[...] = newton_one * gram_ref[...] + low_dot(low_ref[...], change_ref[...])
                low_ref[...] = gram_ref[...].astype(bf)
                gram_ref[...] = newton_one * gram_ref[...] + low_dot(low_ref[...], change_ref[...])

def orthogonal_rows(moments, grads, factor, row_count, chunk, full_steps):
    count, (part_rows, width) = len(moments), moments[0].shape
    body = functools.partial(orthogonal_kernel, count, chunk, full_steps, row_count)
    flops = 2 * width * width * (count * part_rows * (2 * full_steps + 1) + 9 * width)
    return pl.pallas_call(
        body,
        out_shape=jax.ShapeDtypeStruct((row_count, width), jnp.float32),
        in_specs=[pl.BlockSpec(memory_space=pltpu.SMEM)]
        + [pl.BlockSpec(memory_space=pl.ANY)] * (2 * count),
        out_specs=pl.BlockSpec(memory_space=pltpu.VMEM),
        scratch_shapes=[
            pltpu.VMEM((count * part_rows if full_steps else 16, width), jnp.bfloat16),
            pltpu.VMEM((width, width), jnp.float32),
            pltpu.VMEM((width, width), jnp.bfloat16),
            pltpu.VMEM((width, width), jnp.bfloat16),
            pltpu.VMEM((count * part_rows // chunk, chunk, width), jnp.bfloat16),
            pltpu.VMEM((count * part_rows // chunk, chunk, width), jnp.bfloat16),
            pltpu.SemaphoreType.DMA((2, count * part_rows // chunk)),
        ],
        compiler_params=pltpu.CompilerParams(vmem_limit_bytes=48 * 1024 * 1024),
        cost_estimate=pl.CostEstimate(flops=flops, bytes_accessed=4 * count * part_rows * width, transcendentals=0),
        name="orthogonal_rows",
    )(factor.reshape(1, 1), *moments, *grads)


def adam_step(weight, first_moment, second_moment, gradient, step_rate):
    first_moment = adam_first * first_moment + (1.0 - adam_first) * gradient
    second_moment = adam_second * second_moment + (1.0 - adam_second) * gradient * gradient
    first_hat = first_moment / (1.0 - adam_first**STEP)
    second_hat = second_moment / (1.0 - adam_second**STEP)
    weight = weight * (1.0 - step_rate * decay_rate) - step_rate * first_hat / (
        jnp.sqrt(second_hat) + 1e-08
    )
    return (weight, first_moment, second_moment)


def on_device(
    patches,
    image_ids,
    patch_place,
    labels,
    attn_w,
    mlp_w,
    embed_w,
    vec_w,
    head_w,
    attn_mom,
    mlp_mom,
    embed_m,
    embed_v,
    vec_m,
    vec_v,
    head_m,
    head_v,
):
    groups = lax.axis_size("cls")
    owners = lax.axis_size("dp")
    count = groups * owners
    top = count.bit_length() - 1
    low_bits = groups.bit_length() - 1
    member_index = lax.axis_index("cls")
    owner_index = lax.axis_index("dp")
    me = owner_index * groups + member_index
    core = me & 1
    model_width = vec_w.shape[1]
    slot_count = labels.shape[1]
    high_bits = list(range(top - 1, 2, -1))
    third, fourth, pair = (2, 4), (4, 2), (1, 1)
    third_mine = jnp.where(core == 0, third[0], third[1])
    fourth_mine = jnp.where(core == 0, fourth[0], fourth[1])

    def exchange(value, masks, what="small"):
        with jax.named_scope(what):
            return swap(value, count, masks)

    def plain(bit):
        return (1 << bit,) * 2

    def bit_of(bit):
        return (me >> bit) & 1

    def lane(steps, what):
        return Lane(steps, exchange, what)

    def of_core(value):
        left, right = value[:, :model_width], value[:, model_width:]
        return jnp.where(core == 0, left, right), jnp.where(core == 0, right, left)

    attn_rows, embed_rows, mlp_rows = attn_w.shape[0], embed_w.shape[0], mlp_w.shape[0]
    up_stages = [plain(bit) for bit in high_bits]
    down_stages = up_stages[::-1]

    def ordered_weights(block):
        for axis, bit in enumerate(high_bits):
            block = ordered_pair(bit_of(bit), block, (yield block, plain(bit)), axis)
        block = block.reshape(-1, attn_rows + embed_rows, model_width)
        block = jnp.stack([block, (yield block, third)])
        block = jnp.concatenate([block, (yield block, fourth)], axis=0)
        return block, (yield block, pair)

    sibling = me ^ 1
    places = [
        me,
        me ^ third_mine,
        me ^ fourth_mine,
        me ^ 6,
        sibling,
        sibling ^ fourth_mine,
        sibling ^ third_mine,
        sibling ^ 6,
    ]
    attn_lane = lane(
        ordered_weights(jnp.concatenate([attn_w, embed_w], axis=0).astype(jnp.bfloat16)),
        "attn_weights",
    )
    mlp_lane = lane(
        collecting(mlp_w.astype(jnp.bfloat16)[None], up_stages + [third]), "mlp_weights"
    )
    for _ in high_bits:
        sync((), attn_lane)
    sync((), attn_lane, mlp_lane)
    sync((), attn_lane, mlp_lane)

    shard_rows, shard_width = head_w.shape
    chunk = -(-shard_width // (owners * 128)) * 128
    padding = owners * chunk - shard_width
    owner_bits = list(range(low_bits, top))

    def transposed(value, order):
        value = value.reshape((2,) * len(owner_bits) + value.shape[1:])
        for bit in order:
            axis = top - 1 - bit
            mine = bit_of(bit)
            stay, leave = pick(value, mine, axis), pick(value, 1 - mine, axis)
            value = ordered_pair(mine, stay, (yield leave, plain(bit)), axis)
        return value.reshape((owners,) + value.shape[len(owner_bits) :])

    head_low = jnp.pad(head_w.astype(jnp.bfloat16), ((0, 0), (0, padding)))
    head_low = head_low.reshape(shard_rows, owners, chunk).transpose(1, 0, 2)
    head_lane = lane(transposed(head_low, owner_bits[1:] + owner_bits[:1]), "head")

    def of_chip():
        value = mlp_mom.astype(jnp.bfloat16)
        mine, leave = of_core(value)
        rows = jnp.stack([mine, (yield leave, pair)])
        return (yield from collecting(rows, up_stages + [third, fourth]))

    mom_lane = lane(of_chip(), "mlp_moments")
    attn_mom_lane = lane(
        collecting(attn_mom.astype(jnp.bfloat16)[None], up_stages[2:] + [third, fourth, pair]),
        "attn_moments",
    )
    sync((), attn_lane, mlp_lane, head_lane)
    pieces, others = finish(attn_lane)[0]
    attn_b = jnp.zeros((count // 8, 8, attn_rows, model_width), jnp.bfloat16)
    embed_b = jnp.zeros((count // 8, 8, embed_rows, model_width), jnp.bfloat16)
    for index, place in enumerate(places):
        piece = (pieces if index < 4 else others)[index % 4]
        attn_b = lax.dynamic_update_slice_in_dim(attn_b, piece[:, None, :attn_rows], place & 7, 1)
        embed_b = lax.dynamic_update_slice_in_dim(embed_b, piece[:, None, attn_rows:], place & 7, 1)
    attn_b = attn_b.reshape(count * attn_rows, model_width)
    embed_b = embed_b.reshape(count * embed_rows, model_width)

    attn_b, embed_b = sync((attn_b, embed_b), mlp_lane, head_lane)
    part_a = jnp.concatenate(finish(mlp_lane)[0], axis=0)

    def once(value, stage):
        return (yield value, stage)

    b_lane = lane(once(part_a, fourth), "mlp_weights")
    c_lane = lane(once(part_a, pair), "mlp_weights")
    sync((), b_lane)
    sync((), c_lane)
    image_index = lax.dynamic_index_in_dim(image_ids, member_index, 0, keepdims=False)
    my_labels = lax.dynamic_index_in_dim(labels, member_index, 0, keepdims=False)
    position = patch_place[0]
    patch_dim = patches.shape[1]
    grid_size = (embed_b.shape[0] - patch_dim) // 2
    grid_index = jnp.arange(grid_size)
    places_hot = [(position[axis][:, None] == grid_index[None]).astype(jnp.bfloat16) for axis in (0, 1)]
    patch_wide = jnp.concatenate([patches] + places_hot, axis=1)
    embedded = low_dot(patch_wide, embed_b) + vec_w[10]
    normed, queries, key_rows, values = projections(attn_b, vec_w, embedded)
    mixed_out, summary = mixing(queries, key_rows, values, image_index, H)
    (mixed_out,) = sync((mixed_out,), c_lane, mom_lane)
    part_c = c_lane.result

    masks = [1 << bit for bit in high_bits]
    own_codes = [jnp.array(codes(masks + [third[c], fourth[c]]), jnp.int32) for c in (0, 1)]
    arrival = me ^ jnp.where(
        core == 0,
        jnp.concatenate([own_codes[0], own_codes[1] ^ 1]),
        jnp.concatenate([own_codes[1], own_codes[0] ^ 1]),
    )
    first_bias = jnp.take(vec_w[11:].reshape(count, mlp_rows), arrival, axis=0)
    first_bias = first_bias.reshape(4, -1)

    middle = embedded + low_dot(mixed_out, attn_b[3 * model_width :]) + vec_w[2]
    normed_two = layer_norm(middle, vec_w[6], vec_w[7]).astype(jnp.bfloat16)
    final_rows, active_even, slope_even = hidden_forward(
        normed_two, middle + vec_w[3], first_bias[::2], [part_a.reshape(-1, 2 * model_width), part_c.reshape(-1, 2 * model_width)]
    )
    final_rows, slope_even = sync((final_rows, slope_even), b_lane, head_lane)
    part_b = b_lane.result
    d_lane = lane(once(part_b, pair), "mlp_weights")
    sync((), d_lane)
    (final_rows,) = sync((final_rows,), d_lane, mom_lane, attn_mom_lane)
    mlp_parts = [
        part.reshape(-1, 2 * model_width) for part in (part_a, part_b, part_c, d_lane.result)
    ]
    final_rows, active_odd, slope_odd = hidden_forward(
        normed_two, final_rows, first_bias[1::2], mlp_parts[1::2]
    )
    active, slope = (active_even, active_odd), (slope_even, slope_odd)
    (final_rows,) = sync(
        (final_rows,), head_lane, mom_lane, attn_mom_lane, hold=(mom_lane, attn_mom_lane)
    )
    closing, close_pull = jax.vjp(layer_norm, final_rows, vec_w[8], vec_w[9])
    member = (image_index[None, :] == jnp.arange(slot_count)[:, None]).astype(jnp.float32)
    slot_sizes = jnp.sum(member, axis=1)
    divisor = jnp.maximum(slot_sizes, 1.0)[:, None]
    pooled = product(member, closing) / divisor
    facts = jnp.stack(
        [(slot_sizes > 0.5).astype(jnp.int32), my_labels // 256, my_labels % 256], axis=1
    )
    facts = jnp.pad(facts, ((0, 0), (0, 125))).astype(jnp.bfloat16)
    block = jnp.concatenate([pooled.astype(jnp.bfloat16), facts], axis=1)
    head_b = finish(head_lane)[0].reshape(owners * shard_rows, chunk)
    for axis, bit in enumerate(high_bits):
        block = ordered_pair(bit_of(bit), block, exchange(block, plain(bit), "pooled"), axis)
    axis = len(high_bits)
    for step, stage in enumerate((third, fourth)):
        bit = jnp.where(core == step, bit_of(1), bit_of(2))
        block = ordered_pair(bit, block, exchange(block, stage, "pooled"), axis + step)
    block = jnp.where(core == 0, jnp.swapaxes(block, axis, axis + 1), block)
    block = ordered_pair(core, block, exchange(block, pair, "pooled"), axis + 2)
    block = block.reshape(count * slot_count, -1)
    all_pooled = block[:, :model_width]
    facts = block[:, model_width : model_width + 3].astype(jnp.int32)
    valid = facts[:, 0] > 0
    all_labels = facts[:, 1] * 256 + facts[:, 2]
    image_total = jnp.sum(valid.astype(jnp.float32))

    logits = low_dot(all_pooled, head_b)
    within = owner_index * chunk + jnp.arange(chunk)
    columns = member_index * shard_width + within
    usable = (within < shard_width) & (columns < CLASSES)
    logits = jnp.where(usable[None], logits, -1e30)
    onehot = (usable[None] & (columns[None, :] == all_labels[:, None])).astype(jnp.float32)
    row_max = jnp.max(logits, axis=1)
    exp_sums = jnp.sum(jnp.exp(logits - row_max[:, None]), axis=1)
    stats = jnp.stack([row_max, exp_sums, jnp.sum(onehot * logits, axis=1)])
    for bit in range(top):
        other = exchange(stats, plain(bit), "stats")
        lower = jnp.where(bit_of(bit) == 0, stats, other)
        upper = jnp.where(bit_of(bit) == 0, other, stats)
        row_max = jnp.maximum(lower[0], upper[0])
        exp_sums = lower[1] * jnp.exp(lower[0] - row_max) + upper[1] * jnp.exp(upper[0] - row_max)
        stats = jnp.stack([row_max, exp_sums, lower[2] + upper[2]])
    normaliser = stats[0] + jnp.log(stats[1])
    loss_sum = jnp.sum(jnp.where(valid, normaliser - stats[2], 0.0))
    probs_class = jnp.exp(logits - normaliser[:, None])
    d_logits = (jnp.where(valid[:, None], probs_class - onehot, 0.0) / image_total).astype(
        jnp.bfloat16
    )
    d_pooled = contract_cols(d_logits, head_b)
    quarter = (me >> 1) & 3
    to_third, to_fourth = third_mine >> 1, fourth_mine >> 1

    def quartered(grad, rows):
        grad = grad.reshape(count // 8, 4, 2, rows, model_width)
        leave = pick(grad, 1 - core, 2).astype(jnp.bfloat16)
        grad = pick(grad, core, 2) + (yield leave, pair).astype(jnp.float32)
        leave = [pick(grad, quarter ^ to_fourth, 1), pick(grad, quarter ^ 3, 1)]
        leave = (yield jnp.stack(leave).astype(jnp.bfloat16), fourth).astype(jnp.float32)
        leaving = pick(grad, quarter ^ to_third, 1) + leave[1]
        return pick(grad, quarter, 1) + leave[0], leaving

    def last_sums(grads):
        grad = jnp.concatenate([one[0] for one in grads], axis=1)
        leave = jnp.concatenate([one[1].astype(jnp.bfloat16) for one in grads], axis=1)
        grad = grad + (yield leave, third).astype(jnp.float32)
        grad = grad.reshape((2,) * len(high_bits) + grad.shape[1:])
        for bit in reversed(high_bits):
            axis = top - 1 - bit
            mine = bit_of(bit)
            leave = pick(grad, 1 - mine, axis).astype(jnp.bfloat16)
            grad = pick(grad, mine, axis) + (yield leave, plain(bit)).astype(jnp.float32)
        return grad

    (parts,) = finish(lane(quartered(d_pooled, slot_count), "d_pooled"))
    (d_pooled,) = finish(lane(last_sums([parts]), "d_pooled"))

    d_closing = product(member.T, d_pooled / divisor)
    d_final, g_gain_final, g_shift_final = close_pull(d_closing)
    d_out = d_final.astype(jnp.bfloat16)
    g_second_bias = jnp.sum(d_out.astype(jnp.float32), axis=0)
    d_out, all_pooled = tie(d_out, all_pooled)
    head_grad = contract_rows(all_pooled, d_logits)
    head_squares = jnp.sum(head_grad * head_grad) / model_width
    head_lane = lane(
        transposed(
            head_grad.astype(jnp.bfloat16).reshape(owners, shard_rows, chunk),
            owner_bits[1:-1] + owner_bits[:1] + owner_bits[-1:],
        ),
        "head_grads",
    )
    (d_out,) = sync((d_out,), mom_lane, attn_mom_lane)

    d_hidden, bias_grads, away = hidden_back(core, d_out, normed_two, active, slope, mlp_parts)
    (away, d_hidden) = sync((away, d_hidden), mom_lane, attn_mom_lane)
    arrived = exchange(away, pair, "mlp_grads")
    operands = (core, d_out, normed_two, active, d_hidden)
    first_plan = ((1, None, (2, 0)), (3, 1, (1,)), (2, 1, (3,)))
    second_plan = ((0, None, (2, 0)), (3, 0, (1,)), (2, 0, (3,)))
    leave = kept_grads(first_plan, *operands, arrived)
    leave, arrived, d_hidden = sync(
        (leave, arrived, d_hidden), attn_mom_lane
    )
    operands = (core, d_out, normed_two, active, d_hidden)

    def summing(leave, kept):
        far = yield leave, fourth
        summed = kept() + far.astype(jnp.float32)
        arrived = yield summed[:model_width].astype(jnp.bfloat16), third
        kept = summed[model_width:] + arrived.astype(jnp.float32)
        kept = kept.reshape(2, -1, mlp_rows, model_width)
        for stage in down_stages:
            half = kept.shape[1] // 2
            arrived = yield kept[:, half:].astype(jnp.bfloat16), stage
            kept = kept[:, :half] + arrived.astype(jnp.float32)
        return kept[:, 0]

    own = []
    mlp_lane = lane(summing(leave, lambda: own[0]), "mlp_grads")
    sync((), mlp_lane)
    d_normed_two, grads = kept_grads(second_plan, *operands, arrived, mlp_parts)
    own.append(grads)
    (d_normed_two,) = sync((d_normed_two,), head_lane)

    d_mid_norm, g_gain_two, g_shift_two = jax.vjp(layer_norm, middle, vec_w[6], vec_w[7])[1](
        d_normed_two
    )
    d_middle = d_final + d_mid_norm
    d_proj = d_middle.astype(jnp.bfloat16)
    g_out_bias = jnp.sum(d_proj.astype(jnp.float32), axis=0)
    d_mixed = contract_cols(d_proj, attn_b[3 * model_width :]).astype(jnp.bfloat16)
    d_queries, d_keys, d_values = mixing_grads(
        queries, key_rows, values, d_mixed, summary, image_index, H
    )
    d_queries, d_keys, d_values, own[0] = sync(
        (d_queries, d_keys, d_values, own[0]),
        mlp_lane,
        mom_lane,
        head_lane,
        hold=(mom_lane, head_lane),
    )
    attn_grad = jnp.concatenate(
        [
            contract_rows(normed, d_queries),
            contract_rows(normed, d_keys),
            contract_rows(normed, d_values),
            contract_rows(mixed_out, d_proj),
        ],
        axis=0,
    )

    attn_lane = lane(quartered(attn_grad, attn_rows), "attn_grads")
    d_normed = (
        contract_cols(d_queries, attn_b[:model_width])
        + contract_cols(d_keys, attn_b[model_width : 2 * model_width])
        + contract_cols(d_values, attn_b[2 * model_width : 3 * model_width])
    )
    sync((), attn_lane)
    (d_normed,) = sync((d_normed,), mlp_lane, attn_lane, head_lane)
    d_emb_norm, g_gain_one, g_shift_one = jax.vjp(layer_norm, embedded, vec_w[4], vec_w[5])[1](
        d_normed
    )
    d_embed_low = (d_middle + d_emb_norm).astype(jnp.bfloat16)
    embed_grad = contract_rows(patch_wide, d_embed_low)
    embed_lane = lane(quartered(embed_grad, embed_rows), "embed_grads")
    sync((), embed_lane)
    sync((), embed_lane, mlp_lane, head_lane, hold=(head_lane,))
    finish(attn_lane, embed_lane)
    sum_lane = lane(last_sums([attn_lane.result, embed_lane.result]), "last_grads")
    sync((), sum_lane)
    mlp_grad = finish(mlp_lane)[0]
    all_lane = lane(
        collecting(mlp_grad.astype(jnp.bfloat16), up_stages + [third, fourth]), "mlp_grads_all"
    )
    sync((), all_lane)
    sync((), sum_lane, all_lane, mom_lane)
    sync((), sum_lane, all_lane)
    while sum_lane.result is None:
        sync((), sum_lane, all_lane, mom_lane, hold=(all_lane,))
    attn_sum, embed_sum = sum_lane.result[:attn_rows], sum_lane.result[attn_rows:]
    g_query_bias = jnp.sum(d_queries.astype(jnp.float32), axis=0)
    g_value_bias = jnp.sum(d_values.astype(jnp.float32), axis=0)
    g_patch_bias = jnp.sum(d_embed_low.astype(jnp.float32), axis=0)
    g_first_bias = jnp.take(bias_grads.reshape(count, mlp_rows), jnp.argsort(arrival), axis=0)
    vec_grad = jnp.concatenate(
        [
            jnp.stack(
                [
                    g_query_bias,
                    g_value_bias,
                    g_out_bias,
                    g_second_bias,
                    g_gain_one,
                    g_shift_one,
                    g_gain_two,
                    g_shift_two,
                    g_gain_final,
                    g_shift_final,
                    g_patch_bias,
                ]
            ),
            g_first_bias.reshape(-1, model_width),
        ],
        axis=0,
    )
    local_squares = sum(
        jnp.sum(grad * grad, axis=0) for grad in (attn_sum, embed_sum, mlp_grad[0], mlp_grad[1])
    )
    small_sums = jnp.concatenate([vec_grad, (local_squares + head_squares)[None]], axis=0)

    def total(value):
        for bit in [1, 2, 0] + list(range(3, top)):
            value = value + (yield value, plain(bit))
        return value

    small_lane = lane(total(small_sums), "small_sums")
    block_lane = lane(
        collecting(attn_sum.astype(jnp.bfloat16)[None], up_stages[2:] + [third, fourth, pair]),
        "attn_grads_all",
    )
    sync((), small_lane, block_lane)
    sync((), small_lane, block_lane)
    sync((), small_lane, block_lane, all_lane)
    small_sums, attn_grads = finish(small_lane, block_lane)
    attn_moms = jnp.concatenate(finish(attn_mom_lane)[0], axis=0).reshape(-1, model_width)
    attn_grads = jnp.concatenate(attn_grads, axis=0).reshape(-1, model_width)
    vec_sum = small_sums[:-1]
    grad_norm = jnp.sqrt(jnp.sum(small_sums[-1]) + jnp.sum(vec_sum * vec_sum))
    factor = jnp.minimum(1.0, clip_limit / (grad_norm + 1e-06))
    attn_mom_out = momentum_keep * attn_mom + factor * attn_sum
    mine, away = mlp_grad[0], exchange(mlp_grad[1], pair)
    mlp_sum = jnp.concatenate(
        [jnp.where(core == 0, mine, away), jnp.where(core == 0, away, mine)], axis=1
    )
    mlp_mom_out = momentum_keep * mlp_mom + factor * mlp_sum

    (factor,) = sync((factor,), head_lane)
    attn_dir = orthogonal_rows([attn_moms], [attn_grads], factor, attn_rows, 768, 4)
    (attn_dir,) = sync((attn_dir,), all_lane, mom_lane)
    mlp_grads, mlp_moms = finish(all_lane, mom_lane)
    mlp_result = orthogonal_rows(
        [part.reshape(-1, model_width) for part in mlp_moms],
        [part.reshape(-1, model_width) for part in mlp_grads],
        factor,
        2 * mlp_rows,
        768,
        0,
    )
    (mlp_result,) = sync((mlp_result,), head_lane)
    mlp_other = exchange(mlp_result[mlp_rows:], pair)
    mlp_result = mlp_result[:mlp_rows]
    mlp_dir = jnp.concatenate(
        [
            jnp.where(core == 0, mlp_result, mlp_other),
            jnp.where(core == 0, mlp_other, mlp_result),
        ],
        axis=1,
    )
    head_grad = finish(head_lane)[0].transpose(1, 0, 2)
    head_grad = head_grad.reshape(shard_rows, owners * chunk)[:, :shard_width].astype(jnp.float32)
    mlp_scale = math.sqrt(mlp_rows * count / model_width)
    attn_out = attn_w * (1.0 - muon_rate * decay_rate) - muon_rate * attn_dir
    mlp_out = mlp_w * (1.0 - muon_rate * decay_rate) - muon_rate * mlp_scale * mlp_dir
    embed_out, embed_m_out, embed_v_out = adam_step(
        embed_w, embed_m, embed_v, factor * embed_sum, adam_rate
    )
    vec_out, vec_m_out, vec_v_out = adam_step(vec_w, vec_m, vec_v, factor * vec_sum, vector_rate)
    head_out, head_m_out, head_v_out = adam_step(
        head_w, head_m, head_v, factor * head_grad, adam_rate
    )
    return (
        loss_sum,
        image_total,
        grad_norm,
        attn_out,
        attn_mom_out,
        attn_out.astype(jnp.bfloat16),
        mlp_out,
        mlp_mom_out,
        mlp_out.astype(jnp.bfloat16),
        embed_out,
        embed_m_out,
        embed_v_out,
        embed_out.astype(jnp.bfloat16),
        vec_out,
        vec_m_out,
        vec_v_out,
        vec_out.astype(jnp.bfloat16),
        head_out,
        head_m_out,
        head_v_out,
        head_out.astype(jnp.bfloat16),
    )


def solution(mesh):
    return jax.shard_map(
        on_device,
        mesh=mesh,
        in_specs=(
            P(("dp", "cls"), None),
            P("dp", None),
            P(("dp", "cls"), None, None),
            P("dp", None),
            P(("dp", "cls"), None),
            P(("dp", "cls"), None),
            P(("dp", "cls"), None),
            P(),
            P("dp", "cls"),
            P(("dp", "cls"), None),
            P(("dp", "cls"), None),
            P(("dp", "cls"), None),
            P(("dp", "cls"), None),
            P(),
            P(),
            P("dp", "cls"),
            P("dp", "cls"),
        ),
        out_specs=(
            P(),
            P(),
            P(),
            P(("dp", "cls"), None),
            P(("dp", "cls"), None),
            P(("dp", "cls"), None),
            P(("dp", "cls"), None),
            P(("dp", "cls"), None),
            P(("dp", "cls"), None),
            P(("dp", "cls"), None),
            P(("dp", "cls"), None),
            P(("dp", "cls"), None),
            P(("dp", "cls"), None),
            P(),
            P(),
            P(),
            P(),
            P("dp", "cls"),
            P("dp", "cls"),
            P("dp", "cls"),
            P("dp", "cls"),
        ),
        check_vma=False,
    )
```
